128 devices in a mesh: tm: 8 (over x, y_lo), space: 16 (over z, y_hi, core).
Axes of the slice: x: 4, y: 4 (y_hi: 2, y_lo: 2; y = y_hi * 2 + y_lo), z: 4, core: 2. Of those that a mesh axis runs over, the one named last changes fastest.
Arguments:
- frames: bfloat16 [32, 3, 128, 768], P('tm', None, 'space'), may hold values from -6 to 6
- states: bfloat16 [32, 16, 128, 768], P('tm', None, 'space'), may hold values from -4 to 4
- start_state: bfloat16 [16, 128, 768], P(None, 'space'), may hold values from -4 to 4
- cotangent: bfloat16 [32, 12, 128, 768], P('tm', None, 'space'), may hold values from -6 to 6
- w_rec: bfloat16 [16, 9, 16], replicated, may hold values from -0.1875 to 0.1875
- w_in: bfloat16 [16, 9, 3], replicated, may hold values from -1.25 to 1.25
- bias_vec: float32 [16], replicated, may hold values from -2 to 2
- retain: float32 [16], replicated, may hold values from 0.3 to 0.95
- w_head: bfloat16 [12, 16], replicated, may hold values from -1.5 to 1.5
Outputs:
- grad_rec: float32 [16, 9, 16], replicated
- grad_in: float32 [16, 9, 3], replicated
- grad_bias: float32 [16], replicated
- grad_retain: float32 [16], replicated
- grad_head: float32 [12, 16], replicated
- grad_frames: bfloat16 [32, 3, 128, 768], P('tm', None, 'space')
- boundary_grads: float32 [8, 16, 128, 768], P('tm', None, 'space')
The draws below stay inside these ranges and needn't reach their ends.
All inputs are finite; a program needn't handle non-finite values.
Results may differ from the reference program's by a relative error of at most 0.0075.
Values may be sent and summed in bfloat16 or wider, within the bound.
A program may use at most 64 MiB of HBM per device.

```python
import jax
import jax.numpy as jnp

C = 16
IN = 3
OUT = 12
COLS = 768
F_DEV = 4
NT = 32
NR = 128


def levels(stream_key, dims, split, least, top_value):
    loudness, own = 1.0, jax.random.fold_in(stream_key, 6)
    for axis_at, shards_of in split:
        draws = jnp.exp(jax.random.uniform(jax.random.fold_in(own, axis_at), (shards_of,), jnp.float32, least / len(split), top_value / len(split)))
        loudness = loudness * jnp.repeat(draws, dims[axis_at] // shards_of).reshape([-1 if axis == axis_at else 1 for axis in range(len(dims))])
    return loudness


def scatter_about(key, shape, width, most, cuts=(), dtype=jnp.bfloat16):
    gain = levels(key, shape, cuts, -0.22, 0.18) if cuts else 1.0
    values = jax.random.normal(key, shape, jnp.float32) * width * gain
    return jnp.minimum(jnp.maximum(values, -most), most).astype(dtype)


def setup_inputs(seed: int = 0) -> dict:
    key_of = jax.random.split(jax.random.key(seed), 10)
    frames = scatter_about(key_of[0], (NT, IN, NR, COLS), 1.0, 6.0, ((0, 8), (2, 16)))
    states = scatter_about(key_of[1], (NT, C, NR, COLS), 0.7, 4.0, ((0, 8), (2, 16)))
    start_state = scatter_about(key_of[2], (C, NR, COLS), 0.7, 4.0, ((1, 16),))
    cotangent = scatter_about(key_of[3], (NT, OUT, NR, COLS), 1.0, 6.0, ((0, 8), (2, 16)))
    w_rec = scatter_about(key_of[4], (C, 9, C), (64 * C) ** -0.5, 0.1875)
    w_in = scatter_about(key_of[5], (C, 9, IN), (9 * IN) ** -0.5, 1.25)
    bias_vec = scatter_about(key_of[6], (C,), 0.5, 2.0, (), jnp.float32)
    retain = jnp.clip(jax.random.uniform(key_of[7], (C,), jnp.float32, 0.3, 0.95), 0.3, 0.95)
    w_head = scatter_about(key_of[8], (OUT, C), C ** -0.5, 1.5)
    return {"frames": frames, "states": states, "start_state": start_state, "cotangent": cotangent, "w_rec": w_rec, "w_in": w_in, "bias_vec": bias_vec, "retain": retain, "w_head": w_head}


def taps_of(padded, row_count, col_count, flipped):
    pieces = []
    for row_step in range(3):
        for col_step in range(3):
            row_at = 2 - row_step if flipped else row_step
            col_at = 2 - col_step if flipped else col_step
            pieces.append(padded[..., row_at:row_at + row_count, col_at:col_at + col_count])
    return jnp.stack(pieces, axis=-4)


def pad_both(field):
    widths = [(0, 0)] * (field.ndim - 2) + [(1, 1), (1, 1)]
    return jnp.pad(field, widths)


def reference(frames, states, start_state, cotangent, w_rec, w_in, bias_vec, retain, w_head):
    f32 = jnp.float32
    total = states.shape[0]
    row_count = states.shape[2]
    col_count = states.shape[3]
    previous = jnp.concatenate([start_state[None], states[:-1]], axis=0)
    rec_w = w_rec.astype(f32)
    in_w = w_in.astype(f32)
    head_w = w_head.astype(f32)
    carried = jnp.zeros(start_state.shape, f32)
    rec_grad = jnp.zeros(w_rec.shape, f32)
    in_grad = jnp.zeros(w_in.shape, f32)
    bias_grad = jnp.zeros(bias_vec.shape, f32)
    keep_grad = jnp.zeros(retain.shape, f32)
    inputs_list = []
    bounds = []
    for index in reversed(range(total)):
        prev_taps = taps_of(pad_both(previous[index].astype(f32)), row_count, col_count, False)
        frame_taps = taps_of(pad_both(frames[index].astype(f32)), row_count, col_count, False)
        preact = jnp.einsum('okc,kcrw->orw', rec_w, prev_taps) + jnp.einsum('okc,kcrw->orw', in_w, frame_taps)
        preact = preact + bias_vec[:, None, None]
        slopes = 1.0 - jnp.tanh(preact) ** 2
        gradient = carried + jnp.einsum('oc,orw->crw', head_w, cotangent[index].astype(f32))
        dpre = (gradient * slopes).astype(jnp.bfloat16).astype(f32)
        back_taps = taps_of(pad_both(dpre), row_count, col_count, True)
        carried = retain[:, None, None] * gradient + jnp.einsum('okc,korw->crw', rec_w, back_taps)
        rec_grad = rec_grad + jnp.einsum('orw,kcrw->okc', dpre, prev_taps)
        in_grad = in_grad + jnp.einsum('orw,kcrw->okc', dpre, frame_taps)
        bias_grad = bias_grad + jnp.sum(dpre, axis=(1, 2))
        keep_grad = keep_grad + jnp.sum(gradient * previous[index].astype(f32), axis=(1, 2))
        inputs_list.append(jnp.einsum('okc,korw->crw', in_w, back_taps).astype(jnp.bfloat16))
        if index % F_DEV == 0:
            bounds.append(carried)
    head_grad = jnp.einsum('forw,fcrw->oc', cotangent.astype(f32), states.astype(f32))
    grad_frames = jnp.stack(inputs_list[::-1], axis=0)
    boundary_grads = jnp.stack(bounds[::-1], axis=0)
    return rec_grad, in_grad, bias_grad, keep_grad, head_grad, grad_frames, boundary_grads
```

```python
import functools

import jax
import jax.numpy as jnp
from jax import lax
from jax.experimental import pallas as pl
from jax.experimental.pallas import tpu as pltpu
from jax.sharding import PartitionSpec as P

MESH = pl.DeviceIdType.MESH
F32 = jnp.float32
BF16 = jnp.bfloat16
W = 128
CH = 16
ROWS = 8
STEPS = 4
HALO = [STEPS + 1 - k for k in range(STEPS)]
A_AT = [0, 5, 9]
B_AT = [12, 17, 21, 24]
MSG = 26 * CH
TILE = ROWS * CH


def dot(a, b):
    return lax.dot_general(a, b, (((1,), (0,)), ((), ())), preferred_element_type=F32)


def dot_exact(a, b):
    return lax.dot_general(a, b, (((1,), (0,)), ((), ())), preferred_element_type=F32, precision=lax.Precision.HIGHEST)


def dot_nt(a, b):
    return lax.dot_general(a, b, (((1,), (1,)), ((), ())), preferred_element_type=F32)


def iota2(shape, dim):
    return lax.broadcasted_iota(jnp.int32, shape, dim)


def onehot(cond):
    return jnp.where(cond, 1.0, 0.0).astype(BF16)


def tiles(value, count):
    return [value[CH * i : CH * (i + 1)] for i in range(count)]


def kernel(
    tm_count, space_count, cols, chunks,
    frames_ref, states_ref, start_ref, cot_ref, small_ref, chan_ref,
    gf_ref, bound_ref, sums_ref,
    zpa, zpb, za, zb, qsend, stage_up, stage_dn, h_up, h_dn, p_up, p_dn, p_stage_up, p_stage_dn,
    slopes, pushed, xs, dkeep, gkeep, gfs, bnd, c_own, c_up, c_dn, c_send,
    wa, wb, wp, wt, d1prev, d2prev, gprev, biasb, retb, gram, headacc, rpart, rs, ag, red,
    h_ssem, h_rsem, p_ssem, p_rsem, e_ssem, c_ssem, c_rsem, s1, r1, s2, r2, s3, r3,
):
    tm = lax.axis_index("tm")
    sp = lax.axis_index("space")
    has_up = sp > 0
    has_dn = sp < space_count - 1
    is_last = tm == tm_count - 1
    is_first = tm == 0
    blocks = cols // W
    skew0 = STEPS * (tm_count - 1 - tm)

    zh = jnp.zeros((MSG, W), BF16)
    z2 = jnp.zeros((2 * CH, W), BF16)
    h_up[0] = zh
    h_dn[0] = zh
    p_up[0] = z2
    p_dn[0] = z2
    for k in range(STEPS):
        za[0, k] = jnp.zeros((TILE, W), BF16)
        zb[0, k] = jnp.zeros((TILE, W), BF16)
        gprev[k] = jnp.zeros((16 * CH, W), F32)
        d1prev[k] = jnp.zeros((16 * CH, W), BF16)
        d2prev[k] = jnp.zeros((16 * CH, W), BF16)
    gram[...] = jnp.zeros_like(gram)

    @pl.when(jnp.logical_not(has_up))
    def _():
        for j in range(chunks):
            h_up[j + 1] = zh
            p_up[j + 1] = z2
            c_up[j] = jnp.zeros((STEPS * CH, W), BF16)

    @pl.when(jnp.logical_not(has_dn))
    def _():
        for j in range(chunks):
            h_dn[j + 1] = zh
            p_dn[j + 1] = z2
            c_dn[j] = jnp.zeros((STEPS * CH, W), BF16)

    @pl.when(is_last)
    def _():
        for j in range(chunks):
            c_own[j] = jnp.zeros((TILE, W), BF16)
            c_up[j] = jnp.zeros((STEPS * CH, W), BF16)
            c_dn[j] = jnp.zeros((STEPS * CH, W), BF16)

    barrier = pltpu.get_barrier_semaphore()

    def greet(t, s):
        pl.semaphore_signal(barrier, inc=1, device_id=(t, s), device_id_type=MESH)

    for p in range(1, tm_count):
        greet(lax.rem(tm + p, tm_count), sp)
    for q in range(1, space_count):
        greet(tm, lax.rem(sp + q, space_count))
    for dt in (1, tm_count - 1):
        for ds in (1, space_count - 1):
            greet(lax.rem(tm + dt, tm_count), lax.rem(sp + ds, space_count))

    pr = iota2((TILE, TILE), 0)
    pc = iota2((TILE, TILE), 1)
    perm_a = onehot((pr // CH == lax.rem(pc, ROWS)) & (lax.rem(pr, CH) == pc // ROWS))
    bc = iota2((TILE, 15 * ROWS), 1)
    br = iota2((TILE, 15 * ROWS), 0)
    b_chan = bc // ROWS
    b_chan = b_chan + jnp.where(b_chan >= 3, 1, 0)
    perm_b = onehot((br // CH == lax.rem(bc, ROWS)) & (lax.rem(br, CH) == b_chan))
    ones_b = jnp.where(lax.rem(iota2((TILE, cols), 0), CH) == 3, 1.0, 0.0)

    def flat(value, channels):
        return value.astype(F32).reshape(channels * ROWS, cols)

    def put(ref, index, value):
        value = value.astype(BF16)
        ref[index, 0] = jnp.zeros((TILE, W), BF16)
        for c in range(blocks):
            ref[index, c + 1] = value[:, W * c : W * (c + 1)]
        for c in range(blocks + 1, chunks + 1):
            ref[index, c] = jnp.zeros((TILE, W), BF16)

    for f in range(STEPS):
        put(zpa, f, dot(perm_a, flat(states_ref[f], CH).astype(BF16)))
        both = jnp.concatenate([flat(frames_ref[f], 3), flat(cot_ref[f], 12)], axis=0).astype(BF16)
        put(zpb, f, dot(perm_b, both) + ones_b)

    @pl.when(is_first)
    def _():
        put(zpa, STEPS, dot(perm_a, flat(start_ref[...], CH).astype(BF16)))

    pl.semaphore_wait(barrier, tm_count - 1 + space_count - 1 + 4)

    def h_copy(j, up):
        src, dst, target = (stage_up, h_dn, sp - 1) if up else (stage_dn, h_up, sp + 1)
        way = 0 if up else 1
        return pltpu.make_async_remote_copy(
            src_ref=src.at[j], dst_ref=dst.at[j + 1], send_sem=h_ssem.at[way, j], recv_sem=h_rsem.at[way, j],
            device_id=(tm, target), device_id_type=MESH,
        )

    def p_copy(j, way):
        src = [qsend.at[j], qsend.at[j, pl.ds(0, 2 * CH)], qsend.at[j, pl.ds(6 * CH, 2 * CH)]][way]
        dst = [za.at[j + 1, STEPS - 1], p_dn.at[j + 1], p_up.at[j + 1]][way]
        target = (tm + 1, [sp, sp - 1, sp + 1][way])
        return pltpu.make_async_remote_copy(
            src_ref=src, dst_ref=dst, send_sem=p_ssem.at[way, j], recv_sem=p_rsem.at[way, j],
            device_id=target, device_id_type=MESH,
        )

    def s_copy(j, way):
        src = [None, p_stage_up.at[j], p_stage_dn.at[j]][way]
        dst = [None, p_dn.at[j + 1], p_up.at[j + 1]][way]
        target = (tm, [sp, sp - 1, sp + 1][way])
        return pltpu.make_async_remote_copy(
            src_ref=src, dst_ref=dst, send_sem=e_ssem.at[way, j], recv_sem=p_rsem.at[way, j],
            device_id=target, device_id_type=MESH,
        )

    def c_copy(j, way):
        src = [c_send.at[j], c_send.at[j, pl.ds(0, STEPS * CH)], c_send.at[j, pl.ds(STEPS * CH, STEPS * CH)]][way]
        dst = [c_own.at[j], c_dn.at[j], c_up.at[j]][way]
        target = (tm - 1, [sp, sp - 1, sp + 1][way])
        return pltpu.make_async_remote_copy(
            src_ref=src, dst_ref=dst, send_sem=c_ssem.at[way, j], recv_sem=c_rsem.at[way, j],
            device_id=target, device_id_type=MESH,
        )

    def skewer(shift):
        return onehot(iota2((2 * W, W), 0) == iota2((2 * W, W), 1) + (W - shift))

    def skewed(ref, index, j, shift):
        wide = jnp.concatenate([ref[index, j], ref[index, j + 1]], axis=1)
        return dot(wide, skewer(shift)).astype(BF16)

    def send_chunk(j, carry):
        for k in range(STEPS):
            h = HALO[k]
            b_val = skewed(zpb, STEPS - 1 - k, j, skew0 + k)
            zb[j + 1, k] = b_val
            stage_up[j, B_AT[k] * CH : (B_AT[k] + h) * CH] = b_val[: h * CH]
            stage_dn[j, B_AT[k] * CH : (B_AT[k] + h) * CH] = b_val[TILE - h * CH :]
            if k < STEPS - 1:
                a_val = skewed(zpa, STEPS - 2 - k, j, skew0 + k)
                za[j + 1, k] = a_val
                stage_up[j, A_AT[k] * CH : (A_AT[k] + h) * CH] = a_val[: h * CH]
                stage_dn[j, A_AT[k] * CH : (A_AT[k] + h) * CH] = a_val[TILE - h * CH :]

        @pl.when(has_up)
        def _():
            h_copy(j, True).start()

        @pl.when(has_dn)
        def _():
            h_copy(j, False).start()

        @pl.when(jnp.logical_not(is_last))
        def _():
            qsend[j] = skewed(zpa, STEPS - 1, j, skew0 - 1)
            p_copy(j, 0).start()

            @pl.when(has_up)
            def _():
                p_copy(j, 1).start()

            @pl.when(has_dn)
            def _():
                p_copy(j, 2).start()

        @pl.when(is_first)
        def _():
            a_val = skewed(zpa, STEPS, j, skew0 + STEPS - 1)
            za[j + 1, STEPS - 1] = a_val
            p_stage_up[j] = a_val[: 2 * CH]
            p_stage_dn[j] = a_val[6 * CH :]

            @pl.when(has_up)
            def _():
                s_copy(j, 1).start()

            @pl.when(has_dn)
            def _():
                s_copy(j, 2).start()

        return carry

    lax.fori_loop(0, chunks, send_chunk, 0)

    small = small_ref[...]
    biasb[...] = jnp.concatenate([jnp.broadcast_to(chan_ref[:, 0:1], (CH, W))] * 16, axis=0)
    retb[...] = jnp.concatenate([jnp.broadcast_to(chan_ref[:, 1:2], (CH, W))] * 16, axis=0)

    def spread(rows, cols_n, flat_w, width, pick, at, relation):
        r_i = iota2((rows, cols_n), 0) // CH
        c_i = iota2((rows, cols_n), 1) // CH
        left = onehot(lax.rem(iota2((rows, CH), 0), CH) == iota2((rows, CH), 1))
        base = dot(left, flat_w).astype(BF16)
        total = jnp.zeros((rows, cols_n), F32)
        s_r = iota2((width, cols_n), 0)
        s_c = lax.rem(iota2((width, cols_n), 1), CH)
        for a in range(3):
            part = dot(base, onehot(pick(a, s_r, s_c)))
            total = jnp.where(relation(r_i, c_i) == a, part, total)
        return total.astype(BF16)

    fwd = small[:, 0:144]
    bwd = small[:, 144:288]
    fwd_in = small[:, 288:320]
    head_t = small[:, 320:336]
    bwd_in = small[:, 336:480]
    for m in range(3):
        b = 2 - m
        ahead = lambda r, c: c - r
        wa[m] = spread(256, 288, fwd, 144, lambda a, s, c: s == (3 * a + b) * CH + c, 0, ahead)
        wb[m] = spread(256, 288, fwd_in, 32, lambda a, s, c: (s == (3 * a + b) * 3 + c) & (c < 3), 0, ahead)
    wp[...] = spread(256, 288, head_t, 16, lambda a, s, c: (s == c - 4) & (c >= 4) & (a == 1), 0, ahead)
    for b in range(3):
        behind = lambda r, c: r + 2 - c
        t_b = spread(224, 256, bwd, 144, lambda a, s, c: s == (3 * a + b) * CH + c, 0, behind)
        rr = iota2((32, 256), 0)
        left = onehot(rr[:, :CH] // ROWS == iota2((32, CH), 1))
        base = dot(left, bwd_in).astype(BF16)
        for k in range(STEPS):
            n = 16 - 2 * k
            first = STEPS - 1 - k
            r_i = lax.rem(rr, ROWS)
            c_i = iota2((32, 256), 1) // CH - first
            total = jnp.zeros((32, 256), F32)
            for a in range(3):
                s_r = iota2((144, 256), 0)
                s_c = lax.rem(iota2((144, 256), 1), CH)
                part = dot(base, onehot(s_r == (3 * a + b) * CH + s_c))
                total = jnp.where(r_i + 2 - c_i == a, part, total)
            wt[k, b, 0 : CH * (n - 2)] = t_b[0 : CH * (n - 2)]
            wt[k, b, CH * (n - 2) : CH * n] = total.astype(BF16)

    lane = iota2((1, W), 1)

    def shifted(now, before, steps):
        moved = pltpu.roll(now, steps, 1)
        return moved, jnp.where(lane >= steps, moved, before)

    def get_slopes(j):
        for k in range(STEPS):
            h = HALO[k]
            n = 16 - 2 * k

            def whole(slot):
                if k < STEPS - 1:
                    up_a = h_up[slot, A_AT[k] * CH : (A_AT[k] + h) * CH]
                    dn_a = h_dn[slot, A_AT[k] * CH : (A_AT[k] + h) * CH]
                else:
                    up_a, dn_a = p_up[slot], p_dn[slot]
                up_b = h_up[slot, B_AT[k] * CH : (B_AT[k] + h) * CH]
                dn_b = h_dn[slot, B_AT[k] * CH : (B_AT[k] + h) * CH]
                return (
                    jnp.concatenate([up_a, za[slot, k], dn_a], axis=0),
                    jnp.concatenate([up_b, zb[slot, k], dn_b], axis=0),
                )

            a_now, b_now = whole(j + 1)
            a_old, b_old = whole(j)
            both = jnp.concatenate([a_now, b_now], axis=0)
            both_old = jnp.concatenate([a_old, b_old], axis=0)
            size = CH * (n + 2)
            preact = biasb[0 : CH * n]
            for m in range(3):
                if m == 0:
                    x = both
                else:
                    x = jnp.where(lane >= m, pltpu.roll(both, m, 1), pltpu.roll(both_old, m, 1))
                x_a, x_b = x[:size], x[size:]
                preact = preact + dot(wa[m, 0 : CH * n, 0:size], x_a) + dot(wb[m, 0 : CH * n, 0:size], x_b)
                if m == 1:
                    pushed[j, k, 0 : CH * n] = dot(wp[0 : CH * n, 0:size], x_b)
                low = (h - 1) * CH
                xs[j, k, m, 0 : 10 * CH] = x_a[low : low + 10 * CH]
                xs[j, k, m, 10 * CH : 20 * CH] = x_b[low : low + 10 * CH]
            col = W * j + lane - (skew0 + k + 1)
            row = ROWS * sp + iota2((CH * n, 1), 0) // CH + (k - STEPS)
            inside = (col >= 0) & (col < cols) & (row >= 0) & (row < ROWS * space_count)
            t = jnp.tanh(preact)
            slopes[j, k, 0 : CH * n] = jnp.where(inside, 1.0 - t * t, 0.0)

    def await_inputs(j):
        @pl.when(has_up)
        def _():
            h_copy(j, False).wait_recv()

        @pl.when(has_dn)
        def _():
            h_copy(j, True).wait_recv()

        @pl.when(jnp.logical_not(is_first))
        def _():
            p_copy(j, 0).wait_recv()

        @pl.when(has_dn)
        def _():
            p_copy(j, 1).wait_recv()

        @pl.when(has_up)
        def _():
            p_copy(j, 2).wait_recv()

    def prepare(j, carry):
        await_inputs(j)
        get_slopes(j)
        return carry

    def post(j, carry):
        for k in range(STEPS):
            zero = jnp.zeros((CH, W), BF16)
            d = tiles(dkeep[j, k], ROWS)
            g = tiles(gkeep[j, k], ROWS)
            right = jnp.concatenate(
                [
                    jnp.concatenate(d + [zero, zero], axis=1),
                    jnp.concatenate([zero] + d + [zero], axis=1),
                    jnp.concatenate([zero, zero] + d, axis=1),
                    jnp.concatenate([zero] + g + [zero], axis=1),
                ],
                axis=0,
            )
            rows_of = []
            for half in range(2):
                for m in range(3):
                    x = xs[j, k, m, half * 10 * CH : (half + 1) * 10 * CH]
                    rows_of.append(jnp.concatenate(tiles(x, 10), axis=1))
            left = jnp.concatenate(rows_of, axis=0)
            gram[...] += dot_nt(left, right)
        return carry

    def chain(j):
        carried = jnp.concatenate([c_up[j], c_own[j], c_dn[j]], axis=0).astype(F32)
        for k in range(STEPS):
            n = 16 - 2 * k
            size = CH * n
            g = carried + pushed[j, k, 0:size]
            d = (g * slopes[j, k, 0:size]).astype(BF16)
            r1_, d1 = shifted(d, d1prev[k, 0:size], 1)
            r2_, d2 = shifted(d, d2prev[k, 0:size], 2)
            d1prev[k, 0:size] = r1_
            d2prev[k, 0:size] = r2_
            inner = g[CH : size - CH]
            rg, gs = shifted(inner, gprev[k, 0 : size - 2 * CH], 1)
            gprev[k, 0 : size - 2 * CH] = rg
            conv = (
                dot(wt[k, 0, 0:size, 0:size], d)
                + dot(wt[k, 1, 0:size, 0:size], d1)
                + dot(wt[k, 2, 0:size, 0:size], d2)
            )
            carried = retb[0 : size - 2 * CH] * gs + conv[0 : size - 2 * CH]
            gfs[j, k] = conv[size - 2 * CH : size]
            at = (STEPS - k) * CH
            dkeep[j, k] = d[at : at + TILE]
            gkeep[j, k] = g[at : at + TILE].astype(BF16)
        bnd[j] = carried
        c_send[j] = carried.astype(BF16)

    def step(j, carry):
        @pl.when(is_last)
        def _():
            prepare(j, 0)

        @pl.when(jnp.logical_not(is_last))
        def _():
            c_copy(j, 0).wait_recv()

            @pl.when(has_dn)
            def _():
                c_copy(j, 1).wait_recv()

            @pl.when(has_up)
            def _():
                c_copy(j, 2).wait_recv()

        chain(j)

        @pl.when(jnp.logical_not(is_first))
        def _():
            c_copy(j, 0).start()

            @pl.when(has_up)
            def _():
                c_copy(j, 1).start()

            @pl.when(has_dn)
            def _():
                c_copy(j, 2).start()

        @pl.when(jnp.logical_not(is_last))
        def _():
            post(j, 0)

        return carry

    @pl.when(jnp.logical_not(is_last))
    def _():
        lax.fori_loop(0, chunks, prepare, 0)

    total = jnp.zeros((12 * ROWS, TILE), F32)
    for f in range(STEPS):
        total = total + dot_nt(flat(cot_ref[f], 12).astype(BF16), flat(states_ref[f], CH).astype(BF16))
    same = lax.rem(iota2((12 * ROWS, TILE), 0), ROWS) == lax.rem(iota2((12 * ROWS, TILE), 1), ROWS)
    total = jnp.where(same, total, 0.0)
    pick_l = jnp.where(iota2((CH, 12 * ROWS), 0) == iota2((CH, 12 * ROWS), 1) // ROWS, 1.0, 0.0)
    pick_r = jnp.where(iota2((TILE, W), 0) // ROWS == iota2((TILE, W), 1), 1.0, 0.0)
    headacc[...] = dot_exact(dot_exact(pick_l, total), pick_r)

    lax.fori_loop(0, chunks, step, 0)

    @pl.when(is_last)
    def _():
        lax.fori_loop(0, chunks, post, 0)

    rpart[0:48, 0:64] = gram[0:48]
    rpart[0:48, 64:128] = gram[48:96]
    rpart[48:64] = headacc[...]
    piece = 64 // tm_count

    def cut(t):
        return pl.ds(pl.multiple_of(t * piece, 8), piece)

    def first_copy(p):
        t = lax.rem(tm + p, tm_count)
        return pltpu.make_async_remote_copy(
            src_ref=rpart.at[cut(t)], dst_ref=rs.at[p], send_sem=s1.at[p], recv_sem=r1.at[p],
            device_id=(t, sp), device_id_type=MESH,
        )

    for p in range(1, tm_count):
        first_copy(p).start()

    out_shift = skew0 + STEPS + 1
    for c in range(blocks):
        def unskew(now, after, shift):
            return jnp.where(lane < W - shift, pltpu.roll(now, W - shift, 1), pltpu.roll(after, W - shift, 1))

        value = unskew(bnd[c], bnd[c + 1], out_shift)
        for r in range(ROWS):
            bound_ref[r, :, W * c : W * (c + 1)] = value[CH * r : CH * (r + 1)]
        for k in range(STEPS):
            value = unskew(gfs[c, k, 0:24], gfs[c + 1, k, 0:24], skew0 + k + 2)
            gf_ref[STEPS - 1 - k, :, :, W * c : W * (c + 1)] = value.reshape(3, ROWS, W).astype(BF16)

    part = rpart[cut(tm)]
    for p in range(1, tm_count):
        first_copy(p).wait_recv()
        part = part + rs[p]
    ag[sp] = part

    def second_copy(q):
        s = lax.rem(sp + q, space_count)
        return pltpu.make_async_remote_copy(
            src_ref=ag.at[sp], dst_ref=ag.at[sp], send_sem=s2.at[q], recv_sem=r2.at[q],
            device_id=(tm, s), device_id_type=MESH,
        )

    for q in range(1, space_count):
        second_copy(q).start()
    for q in range(1, space_count):
        second_copy(q).wait_recv()
    part = ag[0]
    for q in range(1, space_count):
        part = part + ag[q]
    red[cut(tm)] = part

    def third_copy(p):
        t = lax.rem(tm + p, tm_count)
        return pltpu.make_async_remote_copy(
            src_ref=red.at[cut(tm)], dst_ref=red.at[cut(tm)], send_sem=s3.at[p], recv_sem=r3.at[p],
            device_id=(t, sp), device_id_type=MESH,
        )

    for p in range(1, tm_count):
        third_copy(p).start()
    for p in range(1, tm_count):
        third_copy(p).wait_recv()
    sums_ref[...] = red[...]

    for p in range(1, tm_count):
        first_copy(p).wait_send()
        third_copy(p).wait_send()
    for q in range(1, space_count):
        second_copy(q).wait_send()

    def drain(j, carry):
        @pl.when(has_up)
        def _():
            h_copy(j, True).wait_send()

        @pl.when(has_dn)
        def _():
            h_copy(j, False).wait_send()

        @pl.when(jnp.logical_not(is_last))
        def _():
            p_copy(j, 0).wait_send()

            @pl.when(has_up)
            def _():
                p_copy(j, 1).wait_send()

            @pl.when(has_dn)
            def _():
                p_copy(j, 2).wait_send()

        @pl.when(is_first)
        def _():
            @pl.when(has_up)
            def _():
                s_copy(j, 1).wait_send()

            @pl.when(has_dn)
            def _():
                s_copy(j, 2).wait_send()

        @pl.when(jnp.logical_not(is_first))
        def _():
            c_copy(j, 0).wait_send()

            @pl.when(has_up)
            def _():
                c_copy(j, 1).wait_send()

            @pl.when(has_dn)
            def _():
                c_copy(j, 2).wait_send()

        return carry

    lax.fori_loop(0, chunks, drain, 0)


def on_device(tm_count, space_count, frames, states, start_state, cotangent, w_rec, w_in, bias_vec, retain, w_head):
    cols = states.shape[3]
    chunks = -(-(cols + STEPS * tm_count + 1) // W)
    pad = lambda value, rows, width: jnp.pad(value, ((0, rows - value.shape[0]), (0, width - value.shape[1])))
    small = jnp.concatenate(
        [
            w_rec.reshape(16, 144),
            w_rec.transpose(2, 1, 0).reshape(16, 144),
            pad(w_in.reshape(16, 27), 16, 32),
            pad(w_head.T, 16, 16),
            pad(w_in.transpose(2, 1, 0).reshape(3, 144), 16, 144),
        ],
        axis=1,
    )
    small = pad(small, 16, 512)
    chan = jnp.stack([bias_vec, retain], axis=1)
    vmem = pl.BlockSpec(memory_space=pltpu.VMEM)
    dma = pltpu.SemaphoreType.DMA
    scratch = [
        pltpu.VMEM((STEPS + 1, chunks + 1, TILE, W), BF16),
        pltpu.VMEM((STEPS, chunks + 1, TILE, W), BF16),
        pltpu.VMEM((chunks + 1, STEPS, TILE, W), BF16),
        pltpu.VMEM((chunks + 1, STEPS, TILE, W), BF16),
        pltpu.VMEM((chunks, TILE, W), BF16),
        pltpu.VMEM((chunks, MSG, W), BF16),
        pltpu.VMEM((chunks, MSG, W), BF16),
        pltpu.VMEM((chunks + 1, MSG, W), BF16),
        pltpu.VMEM((chunks + 1, MSG, W), BF16),
        pltpu.VMEM((chunks + 1, 2 * CH, W), BF16),
        pltpu.VMEM((chunks + 1, 2 * CH, W), BF16),
        pltpu.VMEM((chunks, 2 * CH, W), BF16),
        pltpu.VMEM((chunks, 2 * CH, W), BF16),
        pltpu.VMEM((chunks, STEPS, 256, W), F32),
        pltpu.VMEM((chunks, STEPS, 256, W), F32),
        pltpu.VMEM((chunks, STEPS, 3, 20 * CH, W), BF16),
        pltpu.VMEM((chunks, STEPS, TILE, W), BF16),
        pltpu.VMEM((chunks, STEPS, TILE, W), BF16),
        pltpu.VMEM((chunks, STEPS, 32, W), F32),
        pltpu.VMEM((chunks, TILE, W), F32),
        pltpu.VMEM((chunks, TILE, W), BF16),
        pltpu.VMEM((chunks, STEPS * CH, W), BF16),
        pltpu.VMEM((chunks, STEPS * CH, W), BF16),
        pltpu.VMEM((chunks, TILE, W), BF16),
        pltpu.VMEM((3, 256, 288), BF16),
        pltpu.VMEM((3, 256, 288), BF16),
        pltpu.VMEM((256, 288), BF16),
        pltpu.VMEM((STEPS, 3, 256, 256), BF16),
        pltpu.VMEM((STEPS, 256, W), BF16),
        pltpu.VMEM((STEPS, 256, W), BF16),
        pltpu.VMEM((STEPS, 256, W), F32),
        pltpu.VMEM((256, W), F32),
        pltpu.VMEM((256, W), F32),
        pltpu.VMEM((96, 64), F32),
        pltpu.VMEM((CH, W), F32),
        pltpu.VMEM((64, W), F32),
        pltpu.VMEM((tm_count, 64 // tm_count, W), F32),
        pltpu.VMEM((space_count, 64 // tm_count, W), F32),
        pltpu.VMEM((64, W), F32),
        dma((2, chunks)), dma((2, chunks)),
        dma((3, chunks)), dma((3, chunks)), dma((3, chunks)),
        dma((3, chunks)), dma((3, chunks)),
        dma((tm_count,)), dma((tm_count,)),
        dma((space_count,)), dma((space_count,)),
        dma((tm_count,)), dma((tm_count,)),
    ]
    grad_frames, bound, sums = pl.pallas_call(
        functools.partial(kernel, tm_count, space_count, cols, chunks),
        out_shape=[
            jax.ShapeDtypeStruct((STEPS, 3, ROWS, cols), BF16),
            jax.ShapeDtypeStruct((ROWS, CH, cols), F32),
            jax.ShapeDtypeStruct((64, W), F32),
        ],
        in_specs=[vmem] * 6,
        out_specs=[vmem] * 3,
        scratch_shapes=scratch,
        compiler_params=pltpu.CompilerParams(
            collective_id=0, has_side_effects=True, vmem_limit_bytes=56 * 1024 * 1024
        ),
    )(frames, states, start_state, cotangent, small, chan)
    def taps(block, width):
        parts = block[:, :, 0:48].reshape(3, CH, 3, CH)[::-1, :width]
        return parts.transpose(3, 2, 0, 1).reshape(CH, 9, width)

    rec = sums[0:48, 0:64].reshape(3, CH, 64)
    other = sums[0:48, 64:128].reshape(3, CH, 64)
    grad_rec = taps(rec, CH)
    grad_in = taps(other, 3)
    grad_bias = other[1, 3, 16:32]
    eye = jnp.eye(CH, dtype=bool)
    grad_retain = jnp.sum(jnp.where(eye, rec[1, :, 48:64], 0.0), axis=0)
    grad_head = sums[48:60, 0:16]
    return (grad_rec, grad_in, grad_bias, grad_retain, grad_head, grad_frames, bound.transpose(1, 0, 2)[None])


def solution(mesh):
    banded = P("tm", None, "space", None)
    in_specs = (banded, banded, P(None, "space", None), banded, P(), P(), P(), P(), P())
    out_specs = (P(), P(), P(), P(), P(), banded, banded)
    return jax.shard_map(
        functools.partial(on_device, mesh.shape["tm"], mesh.shape["space"]),
        mesh=mesh, in_specs=in_specs, out_specs=out_specs, check_vma=False,
    )
```

```python
import functools

import jax
import jax.numpy as jnp
from jax import lax
from jax.experimental import pallas as pl
from jax.experimental.pallas import tpu as pltpu
from jax.sharding import PartitionSpec as P

MESH = pl.DeviceIdType.MESH
F32 = jnp.float32
BF16 = jnp.bfloat16
W = 128
CH = 16
ROWS = 8
STEPS = 4
HALO = [STEPS + 1 - k for k in range(STEPS)]
A_AT = [0, 5, 9]
B_AT = [12, 17, 21, 24]
MSG = 26 * CH
TILE = ROWS * CH


def dot(a, b):
    return lax.dot_general(a, b, (((1,), (0,)), ((), ())), preferred_element_type=F32)


def dot_exact(a, b):
    return lax.dot_general(a, b, (((1,), (0,)), ((), ())), preferred_element_type=F32, precision=lax.Precision.HIGHEST)


def dot_tn(a, b):
    return lax.dot_general(a, b, (((0,), (0,)), ((), ())), preferred_element_type=F32)


def dot_nt(a, b):
    return lax.dot_general(a, b, (((1,), (1,)), ((), ())), preferred_element_type=F32)


def iota2(shape, dim):
    return lax.broadcasted_iota(jnp.int32, shape, dim)


def onehot(cond):
    return jnp.where(cond, 1.0, 0.0).astype(BF16)


def tiles(value, count):
    return [value[CH * i : CH * (i + 1)] for i in range(count)]


def kernel(
    tm_count, space_count, cols, chunks,
    frames_in, states_in, start_in, cot_in, wrec_ref, win_ref, bias_ref, retain_ref, whead_ref,
    gf_ref, bound_ref, sums_ref,
    frames_ref, states_ref, start_ref, cot_ref,
    zpa, zpb, za, zb, qsend, stage_up, stage_dn, h_up, h_dn, p_up, p_dn, p_stage_up, p_stage_dn,
    slopes, pushed, xs, dkeep, gkeep, gfs, bnd, c_own, c_up, c_dn, c_send,
    wf0, wf1, wf2, wf3, wp, wt0, wt1, wt2, wt3, d1prev, d2prev, gprev, biasb, retb, gram, headacc, rpart, rs, ag, red,
    h_ssem, h_rsem, p_ssem, p_rsem, e_ssem, c_ssem, c_rsem, s1, r1, s2, r2, s3, r3, in_sem,
):
    tm = lax.axis_index("tm")
    sp = lax.axis_index("space")
    has_up = sp > 0
    has_dn = sp < space_count - 1
    is_last = tm == tm_count - 1
    is_first = tm == 0
    blocks = cols // W
    wf = [wf0, wf1, wf2, wf3]
    wt = [wt0, wt1, wt2, wt3]
    skew0 = STEPS * (tm_count - 1 - tm)

    loads = [
        pltpu.make_async_copy(src, dst, in_sem.at[i])
        for i, (src, dst) in enumerate(
            [(states_in, states_ref), (frames_in, frames_ref), (cot_in, cot_ref), (start_in, start_ref)]
        )
    ]
    for load in loads:
        load.start()

    zh = jnp.zeros((MSG, W), BF16)
    z2 = jnp.zeros((2 * CH, W), BF16)
    h_up[0] = zh
    h_dn[0] = zh
    p_up[0] = z2
    p_dn[0] = z2
    for k in range(STEPS):
        za[0, k] = jnp.zeros((TILE, W), BF16)
        zb[0, k] = jnp.zeros((TILE, W), BF16)
        gprev[k] = jnp.zeros((16 * CH, W), F32)
        d1prev[k] = jnp.zeros((16 * CH, W), BF16)
        d2prev[k] = jnp.zeros((16 * CH, W), BF16)
    gram[...] = jnp.zeros_like(gram)

    @pl.when(jnp.logical_not(has_up))
    def _():
        for j in range(chunks):
            h_up[j + 1] = zh
            p_up[j + 1] = z2
            c_up[j] = jnp.zeros((STEPS * CH, W), BF16)

    @pl.when(jnp.logical_not(has_dn))
    def _():
        for j in range(chunks):
            h_dn[j + 1] = zh
            p_dn[j + 1] = z2
            c_dn[j] = jnp.zeros((STEPS * CH, W), BF16)

    @pl.when(is_last)
    def _():
        for j in range(chunks):
            c_own[j] = jnp.zeros((TILE, W), BF16)
            c_up[j] = jnp.zeros((STEPS * CH, W), BF16)
            c_dn[j] = jnp.zeros((STEPS * CH, W), BF16)

    barrier = pltpu.get_barrier_semaphore()

    def greet(t, s):
        pl.semaphore_signal(barrier, inc=1, device_id=(t, s), device_id_type=MESH)

    for p in range(1, tm_count):
        greet(lax.rem(tm + p, tm_count), sp)
    for q in range(1, space_count):
        greet(tm, lax.rem(sp + q, space_count))
    for dt in (1, tm_count - 1):
        for ds in (1, space_count - 1):
            greet(lax.rem(tm + dt, tm_count), lax.rem(sp + ds, space_count))

    pr = iota2((TILE, TILE), 0)
    pc = iota2((TILE, TILE), 1)
    perm_a = onehot((pr // CH == lax.rem(pc, ROWS)) & (lax.rem(pr, CH) == pc // ROWS))
    bc = iota2((TILE, 15 * ROWS), 1)
    br = iota2((TILE, 15 * ROWS), 0)
    b_chan = bc // ROWS
    b_chan = b_chan + jnp.where(b_chan >= 3, 1, 0)
    perm_b = onehot((br // CH == lax.rem(bc, ROWS)) & (lax.rem(br, CH) == b_chan))
    ones_b = jnp.where(lax.rem(iota2((TILE, cols), 0), CH) == 3, 1.0, 0.0)

    def flat(value, channels):
        return value.astype(F32).reshape(channels * ROWS, cols)

    def put(ref, index, value):
        value = value.astype(BF16)
        ref[index, 0] = jnp.zeros((TILE, W), BF16)
        for c in range(blocks):
            ref[index, c + 1] = value[:, W * c : W * (c + 1)]
        for c in range(blocks + 1, chunks + 1):
            ref[index, c] = jnp.zeros((TILE, W), BF16)

    for load in loads:
        load.wait()
    for f in range(STEPS):
        put(zpa, f, dot(perm_a, flat(states_ref[f], CH).astype(BF16)))
        both = jnp.concatenate([flat(frames_ref[f], 3), flat(cot_ref[f], 12)], axis=0).astype(BF16)
        put(zpb, f, dot(perm_b, both) + ones_b)

    @pl.when(is_first)
    def _():
        put(zpa, STEPS, dot(perm_a, flat(start_ref[...], CH).astype(BF16)))

    pl.semaphore_wait(barrier, tm_count - 1 + space_count - 1 + 4)

    def h_copy(j, up):
        src, dst, target = (stage_up, h_dn, sp - 1) if up else (stage_dn, h_up, sp + 1)
        way = 0 if up else 1
        return pltpu.make_async_remote_copy(
            src_ref=src.at[j], dst_ref=dst.at[j + 1], send_sem=h_ssem.at[way, j], recv_sem=h_rsem.at[way, j],
            device_id=(tm, target), device_id_type=MESH,
        )

    def p_copy(j, way):
        src = [qsend.at[j], qsend.at[j, pl.ds(0, 2 * CH)], qsend.at[j, pl.ds(6 * CH, 2 * CH)]][way]
        dst = [za.at[j + 1, STEPS - 1], p_dn.at[j + 1], p_up.at[j + 1]][way]
        target = (tm + 1, [sp, sp - 1, sp + 1][way])
        return pltpu.make_async_remote_copy(
            src_ref=src, dst_ref=dst, send_sem=p_ssem.at[way, j], recv_sem=p_rsem.at[way, j],
            device_id=target, device_id_type=MESH,
        )

    def s_copy(j, way):
        src = [None, p_stage_up.at[j], p_stage_dn.at[j]][way]
        dst = [None, p_dn.at[j + 1], p_up.at[j + 1]][way]
        target = (tm, [sp, sp - 1, sp + 1][way])
        return pltpu.make_async_remote_copy(
            src_ref=src, dst_ref=dst, send_sem=e_ssem.at[way, j], recv_sem=p_rsem.at[way, j],
            device_id=target, device_id_type=MESH,
        )

    def c_copy(j, way):
        src = [c_send.at[j], c_send.at[j, pl.ds(0, STEPS * CH)], c_send.at[j, pl.ds(STEPS * CH, STEPS * CH)]][way]
        dst = [c_own.at[j], c_dn.at[j], c_up.at[j]][way]
        target = (tm - 1, [sp, sp - 1, sp + 1][way])
        return pltpu.make_async_remote_copy(
            src_ref=src, dst_ref=dst, send_sem=c_ssem.at[way, j], recv_sem=c_rsem.at[way, j],
            device_id=target, device_id_type=MESH,
        )

    def skewer(shift):
        return onehot(iota2((2 * W, W), 0) == iota2((2 * W, W), 1) + (W - shift))

    def skewed(ref, index, j, shift):
        wide = jnp.concatenate([ref[index, j], ref[index, j + 1]], axis=1)
        return dot(wide, skewer(shift)).astype(BF16)

    def send_chunk(j, carry):
        for k in range(STEPS):
            h = HALO[k]
            b_val = skewed(zpb, STEPS - 1 - k, j, skew0 + k)
            zb[j + 1, k] = b_val
            stage_up[j, B_AT[k] * CH : (B_AT[k] + h) * CH] = b_val[: h * CH]
            stage_dn[j, B_AT[k] * CH : (B_AT[k] + h) * CH] = b_val[TILE - h * CH :]
            if k < STEPS - 1:
                a_val = skewed(zpa, STEPS - 2 - k, j, skew0 + k)
                za[j + 1, k] = a_val
                stage_up[j, A_AT[k] * CH : (A_AT[k] + h) * CH] = a_val[: h * CH]
                stage_dn[j, A_AT[k] * CH : (A_AT[k] + h) * CH] = a_val[TILE - h * CH :]

        @pl.when(has_up)
        def _():
            h_copy(j, True).start()

        @pl.when(has_dn)
        def _():
            h_copy(j, False).start()

        @pl.when(is_first)
        def _():
            a_val = skewed(zpa, STEPS, j, skew0 + STEPS - 1)
            za[j + 1, STEPS - 1] = a_val
            p_stage_up[j] = a_val[: 2 * CH]
            p_stage_dn[j] = a_val[6 * CH :]

            @pl.when(has_up)
            def _():
                s_copy(j, 1).start()

            @pl.when(has_dn)
            def _():
                s_copy(j, 2).start()

        return carry

    def send_previous(j, carry):
        qsend[j] = skewed(zpa, STEPS - 1, j, skew0 - 1)
        p_copy(j, 0).start()

        @pl.when(has_up)
        def _():
            p_copy(j, 1).start()

        @pl.when(has_dn)
        def _():
            p_copy(j, 2).start()

        return carry

    def column(ref):
        row = ref[...].reshape(1, CH)
        eye = iota2((CH, CH), 0) == iota2((CH, CH), 1)
        value = jnp.sum(jnp.where(eye, row, 0.0), axis=1, keepdims=True)
        return jnp.concatenate([jnp.broadcast_to(value, (CH, W))] * 16, axis=0)

    def build_weights():
        biasb[...] = column(bias_ref)
        retb[...] = column(retain_ref)
        rec = [wrec_ref[t] for t in range(9)]
        inp = [win_ref[t] for t in range(9)]
        chan_of = iota2((32, CH), 0) // ROWS == iota2((32, CH), 1)
        inp_rows = [dot(onehot(chan_of[:, :3]), inp[t]).astype(BF16) for t in range(9)]
        for k in range(STEPS):
            n = 16 - 2 * k
            size = CH * (n + 2)
            at = iota2((1, 6 * size), 1)
            part = at // size
            row_in = lax.rem(at, size) // CH
            chan = lax.rem(at, CH)
            picks = []
            for m in range(3):
                picks.append(
                    (
                        onehot((iota2((CH, 6 * size), 0) == chan) & (part == 2 * m)),
                        onehot((iota2((3, 6 * size), 0) == chan) & (part == 2 * m + 1)),
                    )
                )
            base = []
            for a in range(3):
                total = jnp.zeros((CH, 6 * size), F32)
                for m in range(3):
                    t = 3 * a + 2 - m
                    total = total + dot(rec[t], picks[m][0]) + dot_tn(inp[t], picks[m][1])
                base.append(total)
            for r in range(n):
                ahead = row_in - r
                value = jnp.where(ahead == 0, base[0], jnp.where(ahead == 1, base[1], jnp.where(ahead == 2, base[2], 0.0)))
                wf[k][CH * r : CH * (r + 1)] = value.astype(BF16)
            size = CH * n
            at = iota2((1, 3 * size), 1)
            part = at // size
            row_in = lax.rem(at, size) // CH
            chan = lax.rem(at, CH)
            picks = [onehot((iota2((CH, 3 * size), 0) == chan) & (part == b)) for b in range(3)]
            base = []
            base_in = []
            for a in range(3):
                total = jnp.zeros((CH, 3 * size), F32)
                total_in = jnp.zeros((32, 3 * size), F32)
                for b in range(3):
                    t = 3 * a + b
                    total = total + dot_tn(rec[t], picks[b])
                    total_in = total_in + dot(inp_rows[t], picks[b])
                base.append(total)
                base_in.append(total_in)
            for r in range(n - 2):
                behind = r + 2 - row_in
                value = jnp.where(
                    behind == 0, base[0], jnp.where(behind == 1, base[1], jnp.where(behind == 2, base[2], 0.0))
                )
                wt[k][CH * r : CH * (r + 1)] = value.astype(BF16)
            behind = lax.rem(iota2((32, 1), 0), ROWS) + 2 - (row_in - (STEPS - 1 - k))
            value = jnp.where(
                behind == 0, base_in[0], jnp.where(behind == 1, base_in[1], jnp.where(behind == 2, base_in[2], 0.0))
            )
            wt[k][CH * (n - 2) : CH * n] = value.astype(BF16)
        pick = onehot(iota2((12, 256), 0) == lax.rem(iota2((12, 256), 1), CH) - 4)
        base_h = dot_tn(whead_ref[...], pick)
        for r in range(16):
            wp[CH * r : CH * (r + 1)] = jnp.where(iota2((1, 256), 1) // CH == r, base_h, 0.0).astype(BF16)

    def head_gradient():
        total = jnp.zeros((12 * ROWS, TILE), F32)
        for f in range(STEPS):
            total = total + dot_nt(flat(cot_ref[f], 12).astype(BF16), flat(states_ref[f], CH).astype(BF16))
        same = lax.rem(iota2((12 * ROWS, TILE), 0), ROWS) == lax.rem(iota2((12 * ROWS, TILE), 1), ROWS)
        total = jnp.where(same, total, 0.0)
        pick_l = jnp.where(iota2((CH, 12 * ROWS), 0) == iota2((CH, 12 * ROWS), 1) // ROWS, 1.0, 0.0)
        pick_r = jnp.where(iota2((TILE, W), 0) // ROWS == iota2((TILE, W), 1), 1.0, 0.0)
        headacc[...] = dot_exact(dot_exact(pick_l, total), pick_r)

    @pl.when(is_last)
    def _():
        lax.fori_loop(0, chunks, send_chunk, 0)

    @pl.when(jnp.logical_not(is_last))
    def _():
        lax.fori_loop(0, chunks, send_previous, 0)

    build_weights()

    @pl.when(jnp.logical_not(is_last))
    def _():
        head_gradient()
        lax.fori_loop(0, chunks, send_chunk, 0)

    lane = iota2((1, W), 1)

    def shifted(now, before, steps):
        moved = pltpu.roll(now, steps, 1)
        return moved, jnp.where(lane >= steps, moved, before)

    def get_slopes(j):
        for k in range(STEPS):
            h = HALO[k]
            n = 16 - 2 * k

            def whole(slot):
                if k < STEPS - 1:
                    up_a = h_up[slot, A_AT[k] * CH : (A_AT[k] + h) * CH]
                    dn_a = h_dn[slot, A_AT[k] * CH : (A_AT[k] + h) * CH]
                else:
                    up_a, dn_a = p_up[slot], p_dn[slot]
                up_b = h_up[slot, B_AT[k] * CH : (B_AT[k] + h) * CH]
                dn_b = h_dn[slot, B_AT[k] * CH : (B_AT[k] + h) * CH]
                return (
                    jnp.concatenate([up_a, za[slot, k], dn_a], axis=0),
                    jnp.concatenate([up_b, zb[slot, k], dn_b], axis=0),
                )

            a_now, b_now = whole(j + 1)
            a_old, b_old = whole(j)
            both = jnp.concatenate([a_now, b_now], axis=0)
            both_old = jnp.concatenate([a_old, b_old], axis=0)
            size = CH * (n + 2)
            taps = []
            low = (h - 1) * CH
            for m in range(3):
                if m == 0:
                    x = both
                else:
                    x = jnp.where(lane >= m, pltpu.roll(both, m, 1), pltpu.roll(both_old, m, 1))
                taps.append(x)
                x_a, x_b = x[:size], x[size:]
                if m == 1:
                    pushed[j, k, 0 : CH * n] = dot(wp[0 : CH * n, 0 : CH * n], x_b[CH : CH + CH * n])
                xs[j, k, m, 0 : 10 * CH] = x_a[low : low + 10 * CH]
                xs[j, k, m, 10 * CH : 20 * CH] = x_b[low : low + 10 * CH]
            preact = biasb[0 : CH * n] + dot(wf[k][...], jnp.concatenate(taps, axis=0))
            col = W * j + lane - (skew0 + k + 1)
            row = ROWS * sp + iota2((CH * n, 1), 0) // CH + (k - STEPS)
            inside = (col >= 0) & (col < cols) & (row >= 0) & (row < ROWS * space_count)
            t = jnp.tanh(preact)
            slopes[j, k, 0 : CH * n] = jnp.where(inside, 1.0 - t * t, 0.0)

    def await_inputs(j):
        @pl.when(has_up)
        def _():
            h_copy(j, False).wait_recv()

        @pl.when(has_dn)
        def _():
            h_copy(j, True).wait_recv()

        @pl.when(jnp.logical_not(is_first))
        def _():
            p_copy(j, 0).wait_recv()

        @pl.when(has_dn)
        def _():
            p_copy(j, 1).wait_recv()

        @pl.when(has_up)
        def _():
            p_copy(j, 2).wait_recv()

    def prepare(j, carry):
        await_inputs(j)
        get_slopes(j)
        return carry

    def post(j, carry):
        for k in range(STEPS):
            zero = jnp.zeros((CH, W), BF16)
            d = tiles(dkeep[j, k], ROWS)
            g = tiles(gkeep[j, k], ROWS)
            right = jnp.concatenate(
                [
                    jnp.concatenate(d + [zero, zero], axis=1),
                    jnp.concatenate([zero] + d + [zero], axis=1),
                    jnp.concatenate([zero, zero] + d, axis=1),
                    jnp.concatenate([zero] + g + [zero], axis=1),
                ],
                axis=0,
            )
            rows_of = []
            for half in range(2):
                for m in range(3):
                    x = xs[j, k, m, half * 10 * CH : (half + 1) * 10 * CH]
                    rows_of.append(jnp.concatenate(tiles(x, 10), axis=1))
            left = jnp.concatenate(rows_of, axis=0)
            gram[...] += dot_nt(left, right)
        return carry

    def chain(j):
        carried = jnp.concatenate([c_up[j], c_own[j], c_dn[j]], axis=0).astype(F32)
        for k in range(STEPS):
            n = 16 - 2 * k
            size = CH * n
            g = carried + pushed[j, k, 0:size]
            d = (g * slopes[j, k, 0:size]).astype(BF16)
            r1_, d1 = shifted(d, d1prev[k, 0:size], 1)
            r2_, d2 = shifted(d, d2prev[k, 0:size], 2)
            d1prev[k, 0:size] = r1_
            d2prev[k, 0:size] = r2_
            inner = g[CH : size - CH]
            rg, gs = shifted(inner, gprev[k, 0 : size - 2 * CH], 1)
            gprev[k, 0 : size - 2 * CH] = rg
            conv = dot(wt[k][...], jnp.concatenate([d, d1, d2], axis=0))
            carried = retb[0 : size - 2 * CH] * gs + conv[0 : size - 2 * CH]
            gfs[j, k] = conv[size - 2 * CH : size]
            at = (STEPS - k) * CH
            dkeep[j, k] = d[at : at + TILE]
            gkeep[j, k] = g[at : at + TILE].astype(BF16)
        bnd[j] = carried
        c_send[j] = carried.astype(BF16)

    def step(j, carry):
        @pl.when(is_last)
        def _():
            prepare(j, 0)

        @pl.when(jnp.logical_not(is_last))
        def _():
            c_copy(j, 0).wait_recv()

            @pl.when(has_dn)
            def _():
                c_copy(j, 1).wait_recv()

            @pl.when(has_up)
            def _():
                c_copy(j, 2).wait_recv()

        chain(j)

        @pl.when(jnp.logical_not(is_first))
        def _():
            c_copy(j, 0).start()

            @pl.when(has_up)
            def _():
                c_copy(j, 1).start()

            @pl.when(has_dn)
            def _():
                c_copy(j, 2).start()

        @pl.when(jnp.logical_not(is_last))
        def _():
            post(j, 0)

        return carry

    @pl.when(jnp.logical_not(is_last))
    def _():
        lax.fori_loop(0, chunks, prepare, 0)

    lax.fori_loop(0, chunks, step, 0)

    @pl.when(is_last)
    def _():
        lax.fori_loop(0, chunks, post, 0)
        head_gradient()

    rpart[0:16, 0:64] = gram[0:16]
    rpart[0:16, 64:128] = gram[16:32]
    rpart[16:32, 0:64] = gram[32:48]
    rpart[16:32, 64:80] = headacc[:, 0:CH]
    rpart[16:24, 80:128] = gram[80:88, 0:48]
    rpart[24:32, 80:128] = jnp.zeros((8, 48), F32)
    rpart[32:40, 0:64] = gram[48:56]
    rpart[32:40, 64:128] = gram[64:72]

    def first_copy(p):
        return pltpu.make_async_remote_copy(
            src_ref=rpart, dst_ref=rs.at[p], send_sem=s1.at[0], recv_sem=r1.at[p],
            device_id=(0, sp), device_id_type=MESH,
        )

    @pl.when(jnp.logical_not(is_first))
    def _():
        first_copy(tm).start()

    out_shift = skew0 + STEPS + 1

    def put_outputs():
        for c in range(blocks):
            def unskew(now, after, shift):
                return jnp.where(lane < W - shift, pltpu.roll(now, W - shift, 1), pltpu.roll(after, W - shift, 1))

            value = unskew(bnd[c], bnd[c + 1], out_shift)
            for r in range(ROWS):
                bound_ref[0, :, r, W * c : W * (c + 1)] = value[CH * r : CH * (r + 1)]
            for k in range(STEPS):
                value = unskew(gfs[c, k, 0:24], gfs[c + 1, k, 0:24], skew0 + k + 2)
                gf_ref[STEPS - 1 - k, :, :, W * c : W * (c + 1)] = value.reshape(3, ROWS, W).astype(BF16)

    def second_copy(q):
        s = lax.rem(sp + q, space_count)
        return pltpu.make_async_remote_copy(
            src_ref=ag.at[sp], dst_ref=ag.at[sp], send_sem=s2.at[q], recv_sem=r2.at[q],
            device_id=(0, s), device_id_type=MESH,
        )

    def third_copy(t):
        return pltpu.make_async_remote_copy(
            src_ref=red, dst_ref=red, send_sem=s3.at[t], recv_sem=r3.at[0],
            device_id=(t, sp), device_id_type=MESH,
        )

    @pl.when(is_first)
    def _():
        part = rpart[...]
        for t in range(1, tm_count):
            first_copy(t).wait_recv()
            part = part + rs[t]
        ag[sp] = part
        for q in range(1, space_count):
            second_copy(q).start()
        put_outputs()
        for q in range(1, space_count):
            second_copy(q).wait_recv()
        part = ag[0]
        for q in range(1, space_count):
            part = part + ag[q]
        red[...] = part
        for t in range(1, tm_count):
            third_copy(t).start()

    @pl.when(jnp.logical_not(is_first))
    def _():
        put_outputs()
        third_copy(1).wait_recv()

    sums_ref[...] = red[...]

    @pl.when(is_first)
    def _():
        for q in range(1, space_count):
            second_copy(q).wait_send()
        for t in range(1, tm_count):
            third_copy(t).wait_send()

    @pl.when(jnp.logical_not(is_first))
    def _():
        first_copy(tm).wait_send()

    def drain(j, carry):
        @pl.when(has_up)
        def _():
            h_copy(j, True).wait_send()

        @pl.when(has_dn)
        def _():
            h_copy(j, False).wait_send()

        @pl.when(jnp.logical_not(is_last))
        def _():
            p_copy(j, 0).wait_send()

            @pl.when(has_up)
            def _():
                p_copy(j, 1).wait_send()

            @pl.when(has_dn)
            def _():
                p_copy(j, 2).wait_send()

        @pl.when(is_first)
        def _():
            @pl.when(has_up)
            def _():
                s_copy(j, 1).wait_send()

            @pl.when(has_dn)
            def _():
                s_copy(j, 2).wait_send()

        @pl.when(jnp.logical_not(is_first))
        def _():
            c_copy(j, 0).wait_send()

            @pl.when(has_up)
            def _():
                c_copy(j, 1).wait_send()

            @pl.when(has_dn)
            def _():
                c_copy(j, 2).wait_send()

        return carry

    lax.fori_loop(0, chunks, drain, 0)


def finish(sums_ref, gf_in, bound_in, rec_ref, in_ref, bias_ref, keep_ref, head_ref, gf_ref, bound_ref, sem):
    moves = [pltpu.make_async_copy(gf_in, gf_ref, sem.at[0]), pltpu.make_async_copy(bound_in, bound_ref, sem.at[1])]
    for move in moves:
        move.start()
    sums = sums_ref[...]
    turned = jnp.concatenate([sums, jnp.zeros((W - 40, W), F32)], axis=0).T
    for m in range(3):
        b = 2 - m
        lane_rec, row_rec = [(0, 0), (64, 0), (0, 16)][m]
        lane_in, row_in = [(0, 32), (64, 32), (80, 16)][m]
        for a in range(3):
            rec_ref[3 * a + b] = turned[lane_rec + CH * a : lane_rec + CH * (a + 1), row_rec : row_rec + CH]
            in_ref[3 * a + b] = sums[row_in : row_in + 3, lane_in + CH * a : lane_in + CH * (a + 1)]
    bias_ref[...] = sums[35:36, 80:96].reshape(CH)
    eye = iota2((CH, CH), 0) == iota2((CH, CH), 1)
    keep_ref[...] = jnp.sum(jnp.where(eye, sums[0:16, 112:128], 0.0), axis=0, keepdims=True).reshape(CH)
    head_ref[...] = sums[16:28, 64:80]
    for move in moves:
        move.wait()


def on_device(tm_count, space_count, frames, states, start_state, cotangent, w_rec, w_in, bias_vec, retain, w_head):
    cols = states.shape[3]
    chunks = -(-(cols + STEPS * tm_count + 1) // W)
    vmem = pl.BlockSpec(memory_space=pltpu.VMEM)
    anywhere = pl.BlockSpec(memory_space=pl.ANY)
    dma = pltpu.SemaphoreType.DMA
    scratch = [
        pltpu.VMEM(frames.shape, BF16),
        pltpu.VMEM(states.shape, BF16),
        pltpu.VMEM(start_state.shape, BF16),
        pltpu.VMEM(cotangent.shape, BF16),
        pltpu.VMEM((STEPS + 1, chunks + 1, TILE, W), BF16),
        pltpu.VMEM((STEPS, chunks + 1, TILE, W), BF16),
        pltpu.VMEM((chunks + 1, STEPS, TILE, W), BF16),
        pltpu.VMEM((chunks + 1, STEPS, TILE, W), BF16),
        pltpu.VMEM((chunks, TILE, W), BF16),
        pltpu.VMEM((chunks, MSG, W), BF16),
        pltpu.VMEM((chunks, MSG, W), BF16),
        pltpu.VMEM((chunks + 1, MSG, W), BF16),
        pltpu.VMEM((chunks + 1, MSG, W), BF16),
        pltpu.VMEM((chunks + 1, 2 * CH, W), BF16),
        pltpu.VMEM((chunks + 1, 2 * CH, W), BF16),
        pltpu.VMEM((chunks, 2 * CH, W), BF16),
        pltpu.VMEM((chunks, 2 * CH, W), BF16),
        pltpu.VMEM((chunks, STEPS, 256, W), F32),
        pltpu.VMEM((chunks, STEPS, 256, W), F32),
        pltpu.VMEM((chunks, STEPS, 3, 20 * CH, W), BF16),
        pltpu.VMEM((chunks, STEPS, TILE, W), BF16),
        pltpu.VMEM((chunks, STEPS, TILE, W), BF16),
        pltpu.VMEM((chunks, STEPS, 32, W), F32),
        pltpu.VMEM((chunks, TILE, W), F32),
        pltpu.VMEM((chunks, TILE, W), BF16),
        pltpu.VMEM((chunks, STEPS * CH, W), BF16),
        pltpu.VMEM((chunks, STEPS * CH, W), BF16),
        pltpu.VMEM((chunks, TILE, W), BF16),
        *[pltpu.VMEM((CH * n, 6 * CH * (n + 2)), BF16) for n in (16, 14, 12, 10)],
        pltpu.VMEM((256, 256), BF16),
        *[pltpu.VMEM((CH * n, 3 * CH * n), BF16) for n in (16, 14, 12, 10)],
        pltpu.VMEM((STEPS, 256, W), BF16),
        pltpu.VMEM((STEPS, 256, W), BF16),
        pltpu.VMEM((STEPS, 256, W), F32),
        pltpu.VMEM((256, W), F32),
        pltpu.VMEM((256, W), F32),
        pltpu.VMEM((96, 64), F32),
        pltpu.VMEM((CH, W), F32),
        pltpu.VMEM((40, W), F32),
        pltpu.VMEM((tm_count, 40, W), F32),
        pltpu.VMEM((space_count, 40, W), F32),
        pltpu.VMEM((40, W), F32),
        dma((2, chunks)), dma((2, chunks)),
        dma((3, chunks)), dma((3, chunks)), dma((3, chunks)),
        dma((3, chunks)), dma((3, chunks)),
        dma((tm_count,)), dma((tm_count,)),
        dma((space_count,)), dma((space_count,)),
        dma((tm_count,)), dma((tm_count,)), dma((4,)),
    ]
    grad_frames, bound, sums = pl.pallas_call(
        functools.partial(kernel, tm_count, space_count, cols, chunks),
        out_shape=[
            jax.ShapeDtypeStruct((STEPS, 3, ROWS, cols), BF16),
            jax.ShapeDtypeStruct((1, CH, ROWS, cols), F32),
            jax.ShapeDtypeStruct((40, W), F32),
        ],
        in_specs=[anywhere] * 4 + [vmem] * 5,
        out_specs=[vmem] * 3,
        scratch_shapes=scratch,
        compiler_params=pltpu.CompilerParams(
            collective_id=0, has_side_effects=True, vmem_limit_bytes=56 * 1024 * 1024
        ),
    )(
        frames, states, start_state, cotangent, w_rec.transpose(1, 0, 2), w_in.transpose(1, 2, 0), bias_vec, retain, w_head
    )
    out_shape = [
        jax.ShapeDtypeStruct((9, CH, CH), F32),
        jax.ShapeDtypeStruct((9, 3, CH), F32),
        jax.ShapeDtypeStruct((CH,), F32),
        jax.ShapeDtypeStruct((CH,), F32),
        jax.ShapeDtypeStruct((12, CH), F32),
        jax.ShapeDtypeStruct(grad_frames.shape, BF16),
        jax.ShapeDtypeStruct(bound.shape, F32),
    ]
    rec, inp, *rest = pl.pallas_call(
        finish,
        out_shape=out_shape,
        in_specs=[vmem, vmem, vmem],
        out_specs=[vmem] * 5 + [anywhere] * 2,
        scratch_shapes=[dma((2,))],
    )(sums, grad_frames, bound)
    return (rec.transpose(1, 0, 2), inp.transpose(2, 0, 1), *rest)


def solution(mesh):
    banded = P("tm", None, "space", None)
    in_specs = (banded, banded, P(None, "space", None), banded, P(), P(), P(), P(), P())
    out_specs = (P(), P(), P(), P(), P(), banded, banded)
    return jax.shard_map(
        functools.partial(on_device, mesh.shape["tm"], mesh.shape["space"]),
        mesh=mesh, in_specs=in_specs, out_specs=out_specs, check_vma=False,
    )
```

```python
import functools

import jax
import jax.numpy as jnp
from jax import lax
from jax.experimental import pallas as pl
from jax.experimental.pallas import tpu as pltpu
from jax.sharding import PartitionSpec as P

MESH = pl.DeviceIdType.MESH
F32 = jnp.float32
BF16 = jnp.bfloat16
W = 128
CH = 16
ROWS = 8
STEPS = 4
HALO = [STEPS + 1 - k for k in range(STEPS)]
A_AT = [0, 5, 9]
B_AT = [12, 17, 21, 24]
MSG = 26 * CH
TILE = ROWS * CH


def dot(a, b):
    return lax.dot_general(a, b, (((1,), (0,)), ((), ())), preferred_element_type=F32)


def dot_exact(a, b):
    return lax.dot_general(a, b, (((1,), (0,)), ((), ())), preferred_element_type=F32, precision=lax.Precision.HIGHEST)


def dot_tn(a, b):
    return lax.dot_general(a, b, (((0,), (0,)), ((), ())), preferred_element_type=F32)


def dot_nt(a, b):
    return lax.dot_general(a, b, (((1,), (1,)), ((), ())), preferred_element_type=F32)


def iota2(shape, dim):
    return lax.broadcasted_iota(jnp.int32, shape, dim)


def onehot(cond):
    return jnp.where(cond, 1.0, 0.0).astype(BF16)


def tiles(value, count):
    return [value[CH * i : CH * (i + 1)] for i in range(count)]


def kernel(
    tm_count, space_count, cols, chunks,
    frames_in, states_in, start_in, cot_in, wrec_ref, win_ref, bias_ref, retain_ref, whead_ref,
    gf_ref, bound_ref, sums_ref,
    frames_ref, states_ref, start_ref, cot_ref,
    zpa, zpb, zpq, stage_up, stage_dn, h_up, h_dn, p_up, p_dn, oldx,
    slopes, pushed, xs, dkeep, gkeep, gfs, bnd, c_own, c_up, c_dn, c_send, l_own, l_up, l_dn, l_send,
    wf0, wf1, wf2, wf3, wp, wt0, wt1, wt2, wt3, d1prev, d2prev, gprev, biasb, retb, gram, headacc, rpart, rs, ag, red,
    h_ssem, h_rsem, p_ssem, p_rsem, e_ssem, c_ssem, c_rsem, s1, r1, s2, r2, s3, r3, in_sem,
):
    tm = lax.axis_index("tm")
    sp = lax.axis_index("space")
    has_up = sp > 0
    has_dn = sp < space_count - 1
    is_last = tm == tm_count - 1
    is_first = tm == 0
    is_early = tm >= tm_count - 1
    blocks = cols // W
    wf = [wf0, wf1, wf2, wf3]
    wt = [wt0, wt1, wt2, wt3]
    skew0 = STEPS * (tm_count - 1 - tm)

    loads = [
        pltpu.make_async_copy(src, dst, in_sem.at[i])
        for i, (src, dst) in enumerate(
            [(states_in, states_ref), (frames_in, frames_ref), (cot_in, cot_ref), (start_in, start_ref)]
        )
    ]
    for load in loads:
        load.start()

    zh = jnp.zeros((MSG, W), BF16)
    z2 = jnp.zeros((2 * CH, W), BF16)
    zt = jnp.zeros((TILE, W), BF16)
    for slot in [0] + list(range(blocks + 1, chunks + 1)):
        h_up[slot] = zh
        h_dn[slot] = zh
        p_up[slot] = z2
        p_dn[slot] = z2
        zpq[slot] = zt
        for f in range(STEPS):
            zpa[f, slot] = zt
            zpb[f, slot] = zt
    for k in range(STEPS):
        for m in range(3):
            oldx[k, m] = jnp.zeros((36 * CH, W), BF16)
        gprev[k] = jnp.zeros((16 * CH, W), F32)
        d1prev[k] = jnp.zeros((16 * CH, W), BF16)
        d2prev[k] = jnp.zeros((16 * CH, W), BF16)
    gram[...] = jnp.zeros_like(gram)

    @pl.when(jnp.logical_not(has_up))
    def _():
        for j in range(blocks):
            h_up[j + 1] = zh
            p_up[j + 1] = z2
        l_up[...] = z2
        for j in range(blocks):
            c_up[j] = jnp.zeros((STEPS * CH, W), BF16)

    @pl.when(jnp.logical_not(has_dn))
    def _():
        for j in range(blocks):
            h_dn[j + 1] = zh
            p_dn[j + 1] = z2
        l_dn[...] = z2
        for j in range(blocks):
            c_dn[j] = jnp.zeros((STEPS * CH, W), BF16)

    @pl.when(is_last)
    def _():
        l_own[...] = z2
        l_up[...] = z2
        l_dn[...] = z2
        for j in range(blocks):
            c_own[j] = jnp.zeros((TILE, W), BF16)
            c_up[j] = jnp.zeros((STEPS * CH, W), BF16)
            c_dn[j] = jnp.zeros((STEPS * CH, W), BF16)

    barrier = pltpu.get_barrier_semaphore()

    def greet(t, s):
        pl.semaphore_signal(barrier, inc=1, device_id=(t, s), device_id_type=MESH)

    for p in range(1, tm_count):
        greet(lax.rem(tm + p, tm_count), sp)
    for q in range(1, space_count):
        greet(tm, lax.rem(sp + q, space_count))
    for dt in (1, tm_count - 1):
        for ds in (1, space_count - 1):
            greet(lax.rem(tm + dt, tm_count), lax.rem(sp + ds, space_count))

    pr = iota2((TILE, TILE), 0)
    pc = iota2((TILE, TILE), 1)
    perm_a = onehot((pr // CH == lax.rem(pc, ROWS)) & (lax.rem(pr, CH) == pc // ROWS))
    bc = iota2((TILE, 15 * ROWS), 1)
    br = iota2((TILE, 15 * ROWS), 0)
    b_chan = bc // ROWS
    b_chan = b_chan + jnp.where(b_chan >= 3, 1, 0)
    perm_b = onehot((br // CH == lax.rem(bc, ROWS)) & (lax.rem(br, CH) == b_chan))
    ones_b = jnp.where(lax.rem(iota2((TILE, cols), 0), CH) == 3, 1.0, 0.0)

    def flat(value, channels):
        return value.astype(F32).reshape(channels * ROWS, cols)

    def put(ref, value):
        value = value.astype(BF16)
        for c in range(blocks):
            ref[c + 1] = value[:, W * c : W * (c + 1)]

    for load in loads:
        load.wait()
    for f in range(STEPS):
        put(zpa.at[f], dot(perm_a, flat(states_ref[f], CH).astype(BF16)))
        both = jnp.concatenate([flat(frames_ref[f], 3), flat(cot_ref[f], 12)], axis=0).astype(BF16)
        put(zpb.at[f], dot(perm_b, both) + ones_b)

    @pl.when(is_first)
    def _():
        put(zpq, dot(perm_a, flat(start_ref[...], CH).astype(BF16)))

    pl.semaphore_wait(barrier, tm_count - 1 + space_count - 1 + 4)

    def h_copy(j, up):
        src, dst, target = (stage_up, h_dn, sp - 1) if up else (stage_dn, h_up, sp + 1)
        way = 0 if up else 1
        return pltpu.make_async_remote_copy(
            src_ref=src.at[j], dst_ref=dst.at[j + 1], send_sem=h_ssem.at[way, j], recv_sem=h_rsem.at[way, j],
            device_id=(tm, target), device_id_type=MESH,
        )

    def p_copy(j, way):
        rows = [pl.ds(0, TILE), pl.ds(0, 2 * CH), pl.ds(6 * CH, 2 * CH)][way]
        dst = [zpq.at[j + 1], p_dn.at[j + 1], p_up.at[j + 1]][way]
        target = (tm + 1, [sp, sp - 1, sp + 1][way])
        return pltpu.make_async_remote_copy(
            src_ref=zpa.at[STEPS - 1, j + 1, rows], dst_ref=dst, send_sem=p_ssem.at[way, j], recv_sem=p_rsem.at[way, j],
            device_id=target, device_id_type=MESH,
        )

    def s_copy(j, way):
        rows = [None, pl.ds(0, 2 * CH), pl.ds(6 * CH, 2 * CH)][way]
        dst = [None, p_dn.at[j + 1], p_up.at[j + 1]][way]
        target = (tm, [sp, sp - 1, sp + 1][way])
        return pltpu.make_async_remote_copy(
            src_ref=zpq.at[j + 1, rows], dst_ref=dst, send_sem=e_ssem.at[way, j], recv_sem=p_rsem.at[way, j],
            device_id=target, device_id_type=MESH,
        )

    def c_copy(j, way):
        src = [c_send.at[j], c_send.at[j, pl.ds(0, STEPS * CH)], c_send.at[j, pl.ds(STEPS * CH, STEPS * CH)]][way]
        dst = [c_own.at[j], c_dn.at[j], c_up.at[j]][way]
        target = (tm - 1, [sp, sp - 1, sp + 1][way])
        return pltpu.make_async_remote_copy(
            src_ref=src, dst_ref=dst, send_sem=c_ssem.at[way, j], recv_sem=c_rsem.at[way, j],
            device_id=target, device_id_type=MESH,
        )

    def send_chunk(j, carry):
        @pl.when(jnp.logical_not(is_last))
        def _():
            @pl.when(has_up)
            def _():
                p_copy(j, 1).start()

            @pl.when(has_dn)
            def _():
                p_copy(j, 2).start()

            p_copy(j, 0).start()

        for k in range(STEPS):
            h = HALO[k]
            b_val = zpb[STEPS - 1 - k, j + 1]
            stage_up[j, B_AT[k] * CH : (B_AT[k] + h) * CH] = b_val[: h * CH]
            stage_dn[j, B_AT[k] * CH : (B_AT[k] + h) * CH] = b_val[TILE - h * CH :]
            if k < STEPS - 1:
                a_val = zpa[STEPS - 2 - k, j + 1]
                stage_up[j, A_AT[k] * CH : (A_AT[k] + h) * CH] = a_val[: h * CH]
                stage_dn[j, A_AT[k] * CH : (A_AT[k] + h) * CH] = a_val[TILE - h * CH :]

        @pl.when(has_up)
        def _():
            h_copy(j, True).start()

        @pl.when(has_dn)
        def _():
            h_copy(j, False).start()

        @pl.when(is_first)
        def _():
            @pl.when(has_up)
            def _():
                s_copy(j, 1).start()

            @pl.when(has_dn)
            def _():
                s_copy(j, 2).start()

        return carry

    def l_copy(way):
        dst = [l_own, l_dn, l_up][way]
        target = (tm - 1, [sp, sp - 1, sp + 1][way])
        return pltpu.make_async_remote_copy(
            src_ref=l_send, dst_ref=dst, send_sem=c_ssem.at[way, blocks], recv_sem=c_rsem.at[way, blocks],
            device_id=target, device_id_type=MESH,
        )

    def column(ref):
        row = ref[...].reshape(1, CH)
        eye = iota2((CH, CH), 0) == iota2((CH, CH), 1)
        value = jnp.sum(jnp.where(eye, row, 0.0), axis=1, keepdims=True)
        return jnp.concatenate([jnp.broadcast_to(value, (CH, W))] * 16, axis=0)

    def build_weights():
        biasb[...] = column(bias_ref)
        retb[...] = column(retain_ref)
        rec = [wrec_ref[t] for t in range(9)]
        inp = [win_ref[t] for t in range(9)]
        chan_of = iota2((32, CH), 0) // ROWS == iota2((32, CH), 1)
        inp_rows = [dot(onehot(chan_of[:, :3]), inp[t]).astype(BF16) for t in range(9)]
        for k in range(STEPS):
            n = 16 - 2 * k
            size = CH * (n + 2)
            at = iota2((1, 6 * size), 1)
            part = at // size
            row_in = lax.rem(at, size) // CH
            chan = lax.rem(at, CH)
            picks = []
            for m in range(3):
                picks.append(
                    (
                        onehot((iota2((CH, 6 * size), 0) == chan) & (part == 2 * m)),
                        onehot((iota2((3, 6 * size), 0) == chan) & (part == 2 * m + 1)),
                    )
                )
            base = []
            for a in range(3):
                total = jnp.zeros((CH, 6 * size), F32)
                for m in range(3):
                    t = 3 * a + 2 - m
                    total = total + dot(rec[t], picks[m][0]) + dot_tn(inp[t], picks[m][1])
                base.append(total)
            for r in range(n):
                ahead = row_in - r
                value = jnp.where(ahead == 0, base[0], jnp.where(ahead == 1, base[1], jnp.where(ahead == 2, base[2], 0.0)))
                wf[k][CH * r : CH * (r + 1)] = value.astype(BF16)
            size = CH * n
            at = iota2((1, 3 * size), 1)
            part = at // size
            row_in = lax.rem(at, size) // CH
            chan = lax.rem(at, CH)
            picks = [onehot((iota2((CH, 3 * size), 0) == chan) & (part == b)) for b in range(3)]
            base = []
            base_in = []
            for a in range(3):
                total = jnp.zeros((CH, 3 * size), F32)
                total_in = jnp.zeros((32, 3 * size), F32)
                for b in range(3):
                    t = 3 * a + b
                    total = total + dot_tn(rec[t], picks[b])
                    total_in = total_in + dot(inp_rows[t], picks[b])
                base.append(total)
                base_in.append(total_in)
            for r in range(n - 2):
                behind = r + 2 - row_in
                value = jnp.where(
                    behind == 0, base[0], jnp.where(behind == 1, base[1], jnp.where(behind == 2, base[2], 0.0))
                )
                wt[k][CH * r : CH * (r + 1)] = value.astype(BF16)
            behind = lax.rem(iota2((32, 1), 0), ROWS) + 2 - (row_in - (STEPS - 1 - k))
            value = jnp.where(
                behind == 0, base_in[0], jnp.where(behind == 1, base_in[1], jnp.where(behind == 2, base_in[2], 0.0))
            )
            wt[k][CH * (n - 2) : CH * n] = value.astype(BF16)
        pick = onehot(iota2((12, 256), 0) == lax.rem(iota2((12, 256), 1), CH) - 4)
        base_h = dot_tn(whead_ref[...], pick)
        for r in range(16):
            wp[CH * r : CH * (r + 1)] = jnp.where(iota2((1, 256), 1) // CH == r, base_h, 0.0).astype(BF16)

    def head_gradient():
        total = jnp.zeros((12 * ROWS, TILE), F32)
        for f in range(STEPS):
            total = total + dot_nt(flat(cot_ref[f], 12).astype(BF16), flat(states_ref[f], CH).astype(BF16))
        same = lax.rem(iota2((12 * ROWS, TILE), 0), ROWS) == lax.rem(iota2((12 * ROWS, TILE), 1), ROWS)
        total = jnp.where(same, total, 0.0)
        pick_l = jnp.where(iota2((CH, 12 * ROWS), 0) == iota2((CH, 12 * ROWS), 1) // ROWS, 1.0, 0.0)
        pick_r = jnp.where(iota2((TILE, W), 0) // ROWS == iota2((TILE, W), 1), 1.0, 0.0)
        headacc[...] = dot_exact(dot_exact(pick_l, total), pick_r)

    lax.fori_loop(0, blocks, send_chunk, 0)
    build_weights()

    lane = iota2((1, W), 1)

    def shifted(now, before, steps):
        moved = pltpu.roll(now, steps, 1)
        return moved, jnp.where(lane >= steps, moved, before)

    def get_slopes(j):
        for k in range(STEPS):
            h = HALO[k]
            n = 16 - 2 * k

            def whole(slot):
                if k < STEPS - 1:
                    up_a = h_up[slot, A_AT[k] * CH : (A_AT[k] + h) * CH]
                    dn_a = h_dn[slot, A_AT[k] * CH : (A_AT[k] + h) * CH]
                else:
                    up_a, dn_a = p_up[slot], p_dn[slot]
                up_b = h_up[slot, B_AT[k] * CH : (B_AT[k] + h) * CH]
                dn_b = h_dn[slot, B_AT[k] * CH : (B_AT[k] + h) * CH]
                own_a = zpa[STEPS - 2 - k, slot] if k < STEPS - 1 else zpq[slot]
                return jnp.concatenate([up_a, own_a, dn_a, up_b, zpb[STEPS - 1 - k, slot], dn_b], axis=0)

            raw = whole(j + 1)
            size = CH * (n + 2)
            taps = []
            low = (h - 1) * CH
            for m in range(3):
                turn = skew0 + k + m
                moved = pltpu.roll(raw, turn, 1)
                x = jnp.where(lane >= turn, moved, oldx[k, m, 0 : 2 * size])
                oldx[k, m, 0 : 2 * size] = moved
                taps.append(x)
                x_a, x_b = x[:size], x[size:]
                if m == 1:
                    pushed[j, k, 0 : CH * n] = dot(wp[0 : CH * n, 0 : CH * n], x_b[CH : CH + CH * n])
                xs[j, k, m, 0 : 10 * CH] = x_a[low : low + 10 * CH]
                xs[j, k, m, 10 * CH : 20 * CH] = x_b[low : low + 10 * CH]
            preact = biasb[0 : CH * n] + dot(wf[k][...], jnp.concatenate(taps, axis=0))
            col = W * j + lane - (skew0 + k + 1)
            row = ROWS * sp + iota2((CH * n, 1), 0) // CH + (k - STEPS)
            inside = (col >= 0) & (col < cols) & (row >= 0) & (row < ROWS * space_count)
            t = jnp.tanh(preact)
            slopes[j, k, 0 : CH * n] = jnp.where(inside, 1.0 - t * t, 0.0)

    def await_inputs(j):
        @pl.when(has_up)
        def _():
            h_copy(j, False).wait_recv()

        @pl.when(has_dn)
        def _():
            h_copy(j, True).wait_recv()

        @pl.when(jnp.logical_not(is_first))
        def _():
            p_copy(j, 0).wait_recv()

        @pl.when(has_dn)
        def _():
            p_copy(j, 1).wait_recv()

        @pl.when(has_up)
        def _():
            p_copy(j, 2).wait_recv()

    def prepare(j, carry):
        @pl.when(j < blocks)
        def _():
            await_inputs(j)

        get_slopes(j)
        return carry

    def post(j, carry):
        for k in range(STEPS):
            zero = jnp.zeros((CH, W), BF16)
            d = tiles(dkeep[j, k], ROWS)
            g = tiles(gkeep[j, k], ROWS)
            right = jnp.concatenate(
                [
                    jnp.concatenate(d + [zero, zero], axis=1),
                    jnp.concatenate([zero] + d + [zero], axis=1),
                    jnp.concatenate([zero, zero] + d, axis=1),
                    jnp.concatenate([zero] + g + [zero], axis=1),
                ],
                axis=0,
            )
            rows_of = []
            for half in range(2):
                for m in range(3):
                    x = xs[j, k, m, half * 10 * CH : (half + 1) * 10 * CH]
                    rows_of.append(jnp.concatenate(tiles(x, 10), axis=1))
            left = jnp.concatenate(rows_of, axis=0)
            gram[...] += dot_nt(left, right)
        return carry

    group = 2 * CH
    spread_w = W // 4

    def unpack(ref, which):
        value = ref[...]
        return [value if q == 0 else pltpu.roll(value, W - spread_w * q, 1) for q in which]

    def chain(j, last):
        if last:
            parts = unpack(l_up, (2, 3)) + unpack(l_own, (0, 1, 2, 3)) + unpack(l_dn, (0, 1))
        else:
            parts = [c_up[j], c_own[j], c_dn[j]]
        carried = jnp.concatenate(parts, axis=0).astype(F32)
        for k in range(STEPS):
            n = 16 - 2 * k
            size = CH * n
            g = carried + pushed[j, k, 0:size]
            d = (g * slopes[j, k, 0:size]).astype(BF16)
            r1_, d1 = shifted(d, d1prev[k, 0:size], 1)
            r2_, d2 = shifted(d, d2prev[k, 0:size], 2)
            d1prev[k, 0:size] = r1_
            d2prev[k, 0:size] = r2_
            inner = g[CH : size - CH]
            rg, gs = shifted(inner, gprev[k, 0 : size - 2 * CH], 1)
            gprev[k, 0 : size - 2 * CH] = rg
            conv = dot(wt[k][...], jnp.concatenate([d, d1, d2], axis=0))
            carried = retb[0 : size - 2 * CH] * gs + conv[0 : size - 2 * CH]
            gfs[j, k] = conv[size - 2 * CH : size]
            at = (STEPS - k) * CH
            dkeep[j, k] = d[at : at + TILE]
            gkeep[j, k] = g[at : at + TILE].astype(BF16)
        out = carried.astype(BF16)
        if last:
            packed = out[0:group]
            for q in range(1, 4):
                packed = jnp.where(
                    lane >= spread_w * q, pltpu.roll(out[group * q : group * (q + 1)], spread_w * q, 1), packed
                )
            l_send[...] = packed
        else:
            c_send[j] = out
        bnd[j] = carried

    def step(j, carry, last=False):
        hop = l_copy if last else functools.partial(c_copy, j)

        @pl.when(is_early)
        def _():
            prepare(j, 0)

        @pl.when(jnp.logical_not(is_last))
        def _():
            hop(0).wait_recv()

            @pl.when(has_dn)
            def _():
                hop(1).wait_recv()

            @pl.when(has_up)
            def _():
                hop(2).wait_recv()

        chain(j, last)

        @pl.when(jnp.logical_not(is_first))
        def _():
            @pl.when(has_up)
            def _():
                hop(1).start()

            @pl.when(has_dn)
            def _():
                hop(2).start()

            hop(0).start()

        @pl.when(jnp.logical_not(is_early))
        def _():
            post(j, 0)

        return carry

    @pl.when(jnp.logical_not(is_early))
    def _():
        head_gradient()
        lax.fori_loop(0, chunks, prepare, 0)

    lax.fori_loop(0, blocks, step, 0)
    step(blocks, 0, True)

    @pl.when(is_early)
    def _():
        lax.fori_loop(0, chunks, post, 0)
        head_gradient()

    rpart[0:16, 0:64] = gram[0:16]
    rpart[0:16, 64:128] = gram[16:32]
    rpart[16:32, 0:64] = gram[32:48]
    rpart[16:32, 64:80] = headacc[:, 0:CH]
    rpart[16:24, 80:128] = gram[80:88, 0:48]
    rpart[24:32, 80:128] = jnp.zeros((8, 48), F32)
    rpart[32:40, 0:64] = gram[48:56]
    rpart[32:40, 64:128] = gram[64:72]

    def first_copy(p):
        return pltpu.make_async_remote_copy(
            src_ref=rpart, dst_ref=rs.at[p], send_sem=s1.at[0], recv_sem=r1.at[p],
            device_id=(0, sp), device_id_type=MESH,
        )

    @pl.when(jnp.logical_not(is_first))
    def _():
        first_copy(tm).start()

    out_shift = skew0 + STEPS + 1

    def put_outputs():
        for c in range(blocks):
            def unskew(now, after, shift):
                return jnp.where(lane < W - shift, pltpu.roll(now, W - shift, 1), pltpu.roll(after, W - shift, 1))

            value = unskew(bnd[c], bnd[c + 1], out_shift)
            for r in range(ROWS):
                bound_ref[0, :, r, W * c : W * (c + 1)] = value[CH * r : CH * (r + 1)]
            for k in range(STEPS):
                value = unskew(gfs[c, k, 0:24], gfs[c + 1, k, 0:24], skew0 + k + 2)
                gf_ref[STEPS - 1 - k, :, :, W * c : W * (c + 1)] = value.reshape(3, ROWS, W).astype(BF16)

    def second_copy(q):
        s = lax.rem(sp + q, space_count)
        return pltpu.make_async_remote_copy(
            src_ref=ag.at[sp], dst_ref=ag.at[sp], send_sem=s2.at[q], recv_sem=r2.at[q],
            device_id=(0, s), device_id_type=MESH,
        )

    def third_copy(t):
        return pltpu.make_async_remote_copy(
            src_ref=red, dst_ref=red, send_sem=s3.at[t], recv_sem=r3.at[0],
            device_id=(t, sp), device_id_type=MESH,
        )

    @pl.when(is_first)
    def _():
        part = rpart[...]
        for t in range(1, tm_count):
            first_copy(t).wait_recv()
            part = part + rs[t]
        ag[sp] = part
        for q in range(1, space_count):
            second_copy(q).start()
        put_outputs()
        for q in range(1, space_count):
            second_copy(q).wait_recv()
        part = ag[0]
        for q in range(1, space_count):
            part = part + ag[q]
        red[...] = part
        for t in range(1, tm_count):
            third_copy(t).start()

    @pl.when(jnp.logical_not(is_first))
    def _():
        put_outputs()
        third_copy(1).wait_recv()

    sums_ref[...] = red[...]

    @pl.when(is_first)
    def _():
        for q in range(1, space_count):
            second_copy(q).wait_send()
        for t in range(1, tm_count):
            third_copy(t).wait_send()

    @pl.when(jnp.logical_not(is_first))
    def _():
        first_copy(tm).wait_send()

    def drain(j, carry):
        @pl.when(has_up)
        def _():
            h_copy(j, True).wait_send()

        @pl.when(has_dn)
        def _():
            h_copy(j, False).wait_send()

        @pl.when(jnp.logical_not(is_last))
        def _():
            p_copy(j, 0).wait_send()

            @pl.when(has_up)
            def _():
                p_copy(j, 1).wait_send()

            @pl.when(has_dn)
            def _():
                p_copy(j, 2).wait_send()

        @pl.when(is_first)
        def _():
            @pl.when(has_up)
            def _():
                s_copy(j, 1).wait_send()

            @pl.when(has_dn)
            def _():
                s_copy(j, 2).wait_send()

        return carry

    lax.fori_loop(0, blocks, drain, 0)

    @pl.when(jnp.logical_not(is_first))
    def _():
        def drain_carried(way):
            def body(j, carry):
                c_copy(j, way).wait_send()
                return carry

            lax.fori_loop(0, blocks, body, 0)
            l_copy(way).wait_send()

        drain_carried(0)

        @pl.when(has_up)
        def _():
            drain_carried(1)

        @pl.when(has_dn)
        def _():
            drain_carried(2)


def finish(sums_ref, gf_in, bound_in, rec_ref, in_ref, bias_ref, keep_ref, head_ref, gf_ref, bound_ref, sem):
    moves = [pltpu.make_async_copy(gf_in, gf_ref, sem.at[0]), pltpu.make_async_copy(bound_in, bound_ref, sem.at[1])]
    for move in moves:
        move.start()
    sums = sums_ref[...]
    turned = jnp.concatenate([sums, jnp.zeros((W - 40, W), F32)], axis=0).T
    for m in range(3):
        b = 2 - m
        lane_rec, row_rec = [(0, 0), (64, 0), (0, 16)][m]
        lane_in, row_in = [(0, 32), (64, 32), (80, 16)][m]
        for a in range(3):
            rec_ref[3 * a + b] = turned[lane_rec + CH * a : lane_rec + CH * (a + 1), row_rec : row_rec + CH]
            in_ref[3 * a + b] = sums[row_in : row_in + 3, lane_in + CH * a : lane_in + CH * (a + 1)]
    bias_ref[...] = sums[35:36, 80:96].reshape(CH)
    eye = iota2((CH, CH), 0) == iota2((CH, CH), 1)
    keep_ref[...] = jnp.sum(jnp.where(eye, sums[0:16, 112:128], 0.0), axis=0, keepdims=True).reshape(CH)
    head_ref[...] = sums[16:28, 64:80]
    for move in moves:
        move.wait()


def on_device(tm_count, space_count, frames, states, start_state, cotangent, w_rec, w_in, bias_vec, retain, w_head):
    cols = states.shape[3]
    chunks = -(-(cols + STEPS * tm_count + 1) // W)
    blocks = cols // W
    vmem = pl.BlockSpec(memory_space=pltpu.VMEM)
    anywhere = pl.BlockSpec(memory_space=pl.ANY)
    dma = pltpu.SemaphoreType.DMA
    scratch = [
        pltpu.VMEM(frames.shape, BF16),
        pltpu.VMEM(states.shape, BF16),
        pltpu.VMEM(start_state.shape, BF16),
        pltpu.VMEM(cotangent.shape, BF16),
        pltpu.VMEM((STEPS, chunks + 1, TILE, W), BF16),
        pltpu.VMEM((STEPS, chunks + 1, TILE, W), BF16),
        pltpu.VMEM((chunks + 1, TILE, W), BF16),
        pltpu.VMEM((blocks, MSG, W), BF16),
        pltpu.VMEM((blocks, MSG, W), BF16),
        pltpu.VMEM((chunks + 1, MSG, W), BF16),
        pltpu.VMEM((chunks + 1, MSG, W), BF16),
        pltpu.VMEM((chunks + 1, 2 * CH, W), BF16),
        pltpu.VMEM((chunks + 1, 2 * CH, W), BF16),
        pltpu.VMEM((STEPS, 3, 36 * CH, W), BF16),
        pltpu.VMEM((chunks, STEPS, 256, W), F32),
        pltpu.VMEM((chunks, STEPS, 256, W), F32),
        pltpu.VMEM((chunks, STEPS, 3, 20 * CH, W), BF16),
        pltpu.VMEM((chunks, STEPS, TILE, W), BF16),
        pltpu.VMEM((chunks, STEPS, TILE, W), BF16),
        pltpu.VMEM((chunks, STEPS, 32, W), F32),
        pltpu.VMEM((chunks, TILE, W), F32),
        pltpu.VMEM((blocks, TILE, W), BF16),
        pltpu.VMEM((blocks, STEPS * CH, W), BF16),
        pltpu.VMEM((blocks, STEPS * CH, W), BF16),
        pltpu.VMEM((blocks, TILE, W), BF16),
        *[pltpu.VMEM((2 * CH, W), BF16)] * 4,
        *[pltpu.VMEM((CH * n, 6 * CH * (n + 2)), BF16) for n in (16, 14, 12, 10)],
        pltpu.VMEM((256, 256), BF16),
        *[pltpu.VMEM((CH * n, 3 * CH * n), BF16) for n in (16, 14, 12, 10)],
        pltpu.VMEM((STEPS, 256, W), BF16),
        pltpu.VMEM((STEPS, 256, W), BF16),
        pltpu.VMEM((STEPS, 256, W), F32),
        pltpu.VMEM((256, W), F32),
        pltpu.VMEM((256, W), F32),
        pltpu.VMEM((96, 64), F32),
        pltpu.VMEM((CH, W), F32),
        pltpu.VMEM((40, W), F32),
        pltpu.VMEM((tm_count, 40, W), F32),
        pltpu.VMEM((space_count, 40, W), F32),
        pltpu.VMEM((40, W), F32),
        dma((2, chunks)), dma((2, chunks)),
        dma((3, chunks)), dma((3, chunks)), dma((3, chunks)),
        dma((3, chunks)), dma((3, chunks)),
        dma((tm_count,)), dma((tm_count,)),
        dma((space_count,)), dma((space_count,)),
        dma((tm_count,)), dma((tm_count,)), dma((4,)),
    ]
    grad_frames, bound, sums = pl.pallas_call(
        functools.partial(kernel, tm_count, space_count, cols, chunks),
        out_shape=[
            jax.ShapeDtypeStruct((STEPS, 3, ROWS, cols), BF16),
            jax.ShapeDtypeStruct((1, CH, ROWS, cols), F32),
            jax.ShapeDtypeStruct((40, W), F32),
        ],
        in_specs=[anywhere] * 4 + [vmem] * 5,
        out_specs=[vmem] * 3,
        scratch_shapes=scratch,
        compiler_params=pltpu.CompilerParams(
            collective_id=0, has_side_effects=True, vmem_limit_bytes=56 * 1024 * 1024
        ),
    )(
        frames, states, start_state, cotangent, w_rec.transpose(1, 0, 2), w_in.transpose(1, 2, 0), bias_vec, retain, w_head
    )
    out_shape = [
        jax.ShapeDtypeStruct((9, CH, CH), F32),
        jax.ShapeDtypeStruct((9, 3, CH), F32),
        jax.ShapeDtypeStruct((CH,), F32),
        jax.ShapeDtypeStruct((CH,), F32),
        jax.ShapeDtypeStruct((12, CH), F32),
        jax.ShapeDtypeStruct(grad_frames.shape, BF16),
        jax.ShapeDtypeStruct(bound.shape, F32),
    ]
    rec, inp, *rest = pl.pallas_call(
        finish,
        out_shape=out_shape,
        in_specs=[vmem, vmem, vmem],
        out_specs=[vmem] * 5 + [anywhere] * 2,
        scratch_shapes=[dma((2,))],
    )(sums, grad_frames, bound)
    return (rec.transpose(1, 0, 2), inp.transpose(2, 0, 1), *rest)


def solution(mesh):
    banded = P("tm", None, "space", None)
    in_specs = (banded, banded, P(None, "space", None), banded, P(), P(), P(), P(), P())
    out_specs = (P(), P(), P(), P(), P(), banded, banded)
    return jax.shard_map(
        functools.partial(on_device, mesh.shape["tm"], mesh.shape["space"]),
        mesh=mesh, in_specs=in_specs, out_specs=out_specs, check_vma=False,
    )
```

```python
import functools

import jax
import jax.numpy as jnp
from jax import lax
from jax.experimental import pallas as pl
from jax.experimental.pallas import tpu as pltpu
from jax.sharding import PartitionSpec as P

MESH = pl.DeviceIdType.MESH
F32 = jnp.float32
BF16 = jnp.bfloat16
W = 128
CH = 16
ROWS = 8
STEPS = 4
HALO = [STEPS + 1 - k for k in range(STEPS)]
A_AT = [0, 5, 9]
B_AT = [12, 16, 19, 21]
RIM_AT = 22
MSG = 23 * CH
TILE = ROWS * CH


def dot(a, b):
    return lax.dot_general(a, b, (((1,), (0,)), ((), ())), preferred_element_type=F32)


def dot_exact(a, b):
    return lax.dot_general(a, b, (((1,), (0,)), ((), ())), preferred_element_type=F32, precision=lax.Precision.HIGHEST)


def dot_tn(a, b):
    return lax.dot_general(a, b, (((0,), (0,)), ((), ())), preferred_element_type=F32)


def dot_nt(a, b):
    return lax.dot_general(a, b, (((1,), (1,)), ((), ())), preferred_element_type=F32)


def iota2(shape, dim):
    return lax.broadcasted_iota(jnp.int32, shape, dim)


def onehot(cond):
    return jnp.where(cond, 1.0, 0.0).astype(BF16)


def tiles(value, count):
    return [value[CH * i : CH * (i + 1)] for i in range(count)]


def kernel(
    tm_count, space_count, cols, chunks,
    frames_in, states_in, start_in, cot_in, wrec_ref, win_ref, bias_ref, retain_ref, whead_ref,
    gf_out, bound_out, sums_ref,
    gf_ref, bound_ref, frames_ref, states_ref, start_ref, cot_ref,
    zpa, zpb, zpq, stage_up, stage_dn, h_up, h_dn, p_up, p_dn, oldx,
    slopes, pushed, xs, dkeep, gkeep, gfs, bnd, c_own, c_up, c_dn, c_send, l_own, l_up, l_dn, l_send,
    wf0, wf1, wf2, wf3, wp, wt0, wt1, wt2, wt3, wc, d1prev, d2prev, gprev, biasb, retb, gram, headacc, rpart, rs, ag, red,
    h_ssem, h_rsem, p_ssem, p_rsem, e_ssem, c_ssem, c_rsem, s1, r1, s2, r2, s3, r3, in_sem, out_sem,
):
    tm = lax.axis_index("tm")
    sp = lax.axis_index("space")
    has_up = sp > 0
    has_dn = sp < space_count - 1
    is_last = tm == tm_count - 1
    is_first = tm == 0
    is_early = tm >= tm_count - 1
    blocks = cols // W
    wf = [wf0, wf1, wf2, wf3]
    wt = [wt0, wt1, wt2, wt3]
    skew0 = STEPS * (tm_count - 1 - tm)

    loads = [
        pltpu.make_async_copy(src, dst, in_sem.at[i])
        for i, (src, dst) in enumerate(
            [(states_in, states_ref), (frames_in, frames_ref), (cot_in, cot_ref), (start_in, start_ref)]
        )
    ]
    for load in loads:
        load.start()

    zh = jnp.zeros((MSG, W), BF16)
    z2 = jnp.zeros((2 * CH, W), BF16)
    zt = jnp.zeros((TILE, W), BF16)
    for slot in [0] + list(range(blocks + 1, chunks + 1)):
        h_up[slot] = zh
        h_dn[slot] = zh
        p_up[slot] = z2
        p_dn[slot] = z2
        zpq[slot] = zt
        for f in range(STEPS):
            zpa[f, slot] = zt
            zpb[f, slot] = zt
    for k in range(STEPS):
        for m in range(3):
            oldx[k, m] = jnp.zeros((36 * CH, W), BF16)
        gprev[k] = jnp.zeros((16 * CH, W), F32)
        d1prev[k] = jnp.zeros((16 * CH, W), BF16)
        d2prev[k] = jnp.zeros((16 * CH, W), BF16)
    gram[...] = jnp.zeros_like(gram)

    @pl.when(jnp.logical_not(has_up))
    def _():
        for j in range(blocks):
            h_up[j + 1] = zh
            p_up[j + 1] = z2
        l_up[...] = z2
        for j in range(blocks):
            c_up[j] = jnp.zeros((STEPS * CH, W), BF16)

    @pl.when(jnp.logical_not(has_dn))
    def _():
        for j in range(blocks):
            h_dn[j + 1] = zh
            p_dn[j + 1] = z2
        l_dn[...] = z2
        for j in range(blocks):
            c_dn[j] = jnp.zeros((STEPS * CH, W), BF16)

    @pl.when(is_last)
    def _():
        l_own[...] = z2
        l_up[...] = z2
        l_dn[...] = z2
        for j in range(blocks):
            c_own[j] = jnp.zeros((TILE, W), BF16)
            c_up[j] = jnp.zeros((STEPS * CH, W), BF16)
            c_dn[j] = jnp.zeros((STEPS * CH, W), BF16)

    barrier = pltpu.get_barrier_semaphore()

    def greet(t, s):
        pl.semaphore_signal(barrier, inc=1, device_id=(t, s), device_id_type=MESH)

    for p in range(1, tm_count):
        greet(lax.rem(tm + p, tm_count), sp)
    for q in range(1, space_count):
        greet(tm, lax.rem(sp + q, space_count))
    for dt in (1, tm_count - 1):
        for ds in (1, space_count - 1):
            greet(lax.rem(tm + dt, tm_count), lax.rem(sp + ds, space_count))

    pr = iota2((TILE, TILE), 0)
    pc = iota2((TILE, TILE), 1)
    perm_a = onehot((pr // CH == lax.rem(pc, ROWS)) & (lax.rem(pr, CH) == pc // ROWS))
    bc = iota2((TILE, 15 * ROWS), 1)
    br = iota2((TILE, 15 * ROWS), 0)
    b_chan = bc // ROWS
    b_chan = b_chan + jnp.where(b_chan >= 3, 1, 0)
    perm_b = onehot((br // CH == lax.rem(bc, ROWS)) & (lax.rem(br, CH) == b_chan))
    ones_b = jnp.where(lax.rem(iota2((TILE, cols), 0), CH) == 3, 1.0, 0.0)

    def flat(value, channels):
        return value.astype(F32).reshape(channels * ROWS, cols)

    def put(ref, value):
        value = value.astype(BF16)
        for c in range(blocks):
            ref[c + 1] = value[:, W * c : W * (c + 1)]

    for load in loads:
        load.wait()
    for f in range(STEPS):
        put(zpa.at[f], dot(perm_a, flat(states_ref[f], CH).astype(BF16)))
        both = jnp.concatenate([flat(frames_ref[f], 3), flat(cot_ref[f], 12)], axis=0).astype(BF16)
        put(zpb.at[f], dot(perm_b, both) + ones_b)

    @pl.when(is_first)
    def _():
        put(zpq, dot(perm_a, flat(start_ref[...], CH).astype(BF16)))

    pl.semaphore_wait(barrier, tm_count - 1 + space_count - 1 + 4)

    def h_copy(j, up):
        src, dst, target = (stage_up, h_dn, sp - 1) if up else (stage_dn, h_up, sp + 1)
        way = 0 if up else 1
        return pltpu.make_async_remote_copy(
            src_ref=src.at[j], dst_ref=dst.at[j + 1], send_sem=h_ssem.at[way, j], recv_sem=h_rsem.at[way, j],
            device_id=(tm, target), device_id_type=MESH,
        )

    def p_copy(j, way):
        rows = [pl.ds(0, TILE), pl.ds(0, 2 * CH), pl.ds(6 * CH, 2 * CH)][way]
        dst = [zpq.at[j + 1], p_dn.at[j + 1], p_up.at[j + 1]][way]
        target = (tm + 1, [sp, sp - 1, sp + 1][way])
        return pltpu.make_async_remote_copy(
            src_ref=zpa.at[STEPS - 1, j + 1, rows], dst_ref=dst, send_sem=p_ssem.at[way, j], recv_sem=p_rsem.at[way, j],
            device_id=target, device_id_type=MESH,
        )

    def s_copy(j, way):
        rows = [None, pl.ds(0, 2 * CH), pl.ds(6 * CH, 2 * CH)][way]
        dst = [None, p_dn.at[j + 1], p_up.at[j + 1]][way]
        target = (tm, [sp, sp - 1, sp + 1][way])
        return pltpu.make_async_remote_copy(
            src_ref=zpq.at[j + 1, rows], dst_ref=dst, send_sem=e_ssem.at[way, j], recv_sem=p_rsem.at[way, j],
            device_id=target, device_id_type=MESH,
        )

    def c_copy(j, way):
        src = [c_send.at[j], c_send.at[j, pl.ds(0, STEPS * CH)], c_send.at[j, pl.ds(STEPS * CH, STEPS * CH)]][way]
        dst = [c_own.at[j], c_dn.at[j], c_up.at[j]][way]
        target = (tm - 1, [sp, sp - 1, sp + 1][way])
        return pltpu.make_async_remote_copy(
            src_ref=src, dst_ref=dst, send_sem=c_ssem.at[way, j], recv_sem=c_rsem.at[way, j],
            device_id=target, device_id_type=MESH,
        )

    def send_chunk(j, carry):
        @pl.when(jnp.logical_not(is_last))
        def _():
            @pl.when(has_up)
            def _():
                p_copy(j, 1).start()

            @pl.when(has_dn)
            def _():
                p_copy(j, 2).start()

            p_copy(j, 0).start()

        rims = [[], []]
        for k in range(STEPS):
            h = HALO[k]
            b_val = zpb[STEPS - 1 - k, j + 1]
            stage_up[j, B_AT[k] * CH : (B_AT[k] + h - 1) * CH] = b_val[: (h - 1) * CH]
            stage_dn[j, B_AT[k] * CH : (B_AT[k] + h - 1) * CH] = b_val[TILE - (h - 1) * CH :]
            rims[0].append(b_val[(h - 1) * CH : h * CH].astype(F32))
            rims[1].append(b_val[TILE - h * CH : TILE - (h - 1) * CH].astype(F32))
            if k < STEPS - 1:
                a_val = zpa[STEPS - 2 - k, j + 1]
                stage_up[j, A_AT[k] * CH : (A_AT[k] + h) * CH] = a_val[: h * CH]
                stage_dn[j, A_AT[k] * CH : (A_AT[k] + h) * CH] = a_val[TILE - h * CH :]

        for stage, rim in ((stage_up, rims[0]), (stage_dn, rims[1])):
            value = rim[0]
            for k in range(1, STEPS):
                value = jnp.where(iota2((CH, 1), 0) >= 4 * k, pltpu.roll(rim[k], 4 * k, 0), value)
            stage[j, RIM_AT * CH : (RIM_AT + 1) * CH] = value.astype(BF16)

        @pl.when(has_up)
        def _():
            h_copy(j, True).start()

        @pl.when(has_dn)
        def _():
            h_copy(j, False).start()

        @pl.when(is_first)
        def _():
            @pl.when(has_up)
            def _():
                s_copy(j, 1).start()

            @pl.when(has_dn)
            def _():
                s_copy(j, 2).start()

        return carry

    def l_copy(way):
        dst = [l_own, l_dn, l_up][way]
        target = (tm - 1, [sp, sp - 1, sp + 1][way])
        return pltpu.make_async_remote_copy(
            src_ref=l_send, dst_ref=dst, send_sem=c_ssem.at[way, blocks], recv_sem=c_rsem.at[way, blocks],
            device_id=target, device_id_type=MESH,
        )

    def column(ref):
        row = ref[...].reshape(1, CH)
        eye = iota2((CH, CH), 0) == iota2((CH, CH), 1)
        value = jnp.sum(jnp.where(eye, row, 0.0), axis=1, keepdims=True)
        return jnp.concatenate([jnp.broadcast_to(value, (CH, W))] * 16, axis=0)

    def build_weights():
        biasb[...] = column(bias_ref)
        retb[...] = column(retain_ref)
        rec = [wrec_ref[t] for t in range(9)]
        inp = [win_ref[t] for t in range(9)]
        chan_of = iota2((32, CH), 0) // ROWS == iota2((32, CH), 1)
        inp_rows = [dot(onehot(chan_of[:, :3]), inp[t]).astype(BF16) for t in range(9)]
        for k in range(STEPS):
            n = 16 - 2 * k
            size = CH * (n + 2)
            at = iota2((1, 6 * size), 1)
            part = at // size
            row_in = lax.rem(at, size) // CH
            chan = lax.rem(at, CH)
            picks = []
            for m in range(3):
                picks.append(
                    (
                        onehot((iota2((CH, 6 * size), 0) == chan) & (part == 2 * m)),
                        onehot((iota2((3, 6 * size), 0) == chan) & (part == 2 * m + 1)),
                    )
                )
            base = []
            for a in range(3):
                total = jnp.zeros((CH, 6 * size), F32)
                for m in range(3):
                    t = 3 * a + 2 - m
                    total = total + dot(rec[t], picks[m][0]) + dot_tn(inp[t], picks[m][1])
                base.append(total)
            for r in range(n):
                ahead = row_in - r
                value = jnp.where(ahead == 0, base[0], jnp.where(ahead == 1, base[1], jnp.where(ahead == 2, base[2], 0.0)))
                wf[k][CH * r : CH * (r + 1)] = value.astype(BF16)
            half = n // 2 - 1
            size = CH * (half + 2)
            at = iota2((1, 3 * size), 1)
            part = at // size
            row_in = lax.rem(at, size) // CH
            chan = lax.rem(at, CH)
            picks = [onehot((iota2((CH, 3 * size), 0) == chan) & (part == b)) for b in range(3)]
            base = []
            for a in range(3):
                total = jnp.zeros((CH, 3 * size), F32)
                for b in range(3):
                    total = total + dot_tn(rec[3 * a + b], picks[b])
                base.append(total)
            for r in range(half):
                behind = r + 2 - row_in
                value = jnp.where(
                    behind == 0, base[0], jnp.where(behind == 1, base[1], jnp.where(behind == 2, base[2], 0.0))
                )
                wt[k][CH * r : CH * (r + 1)] = value.astype(BF16)
        size = 10 * CH
        at = iota2((1, 3 * size), 1)
        part = at // size
        row_in = lax.rem(at, size) // CH
        chan = lax.rem(at, CH)
        picks = [onehot((iota2((CH, 3 * size), 0) == chan) & (part == b)) for b in range(3)]
        behind = lax.rem(iota2((32, 1), 0), ROWS) + 2 - row_in
        value = jnp.zeros((32, 3 * size), F32)
        for a in range(3):
            total = jnp.zeros((32, 3 * size), F32)
            for b in range(3):
                total = total + dot(inp_rows[3 * a + b], picks[b])
            value = jnp.where(behind == a, total, value)
        wc[...] = value.astype(BF16)
        pick = onehot(iota2((12, 256), 0) == lax.rem(iota2((12, 256), 1), CH) - 4)
        base_h = dot_tn(whead_ref[...], pick)
        for r in range(16):
            wp[CH * r : CH * (r + 1)] = jnp.where(iota2((1, 256), 1) // CH == r, base_h, 0.0).astype(BF16)

    def head_gradient():
        total = jnp.zeros((12 * ROWS, TILE), F32)
        for f in range(STEPS):
            total = total + dot_nt(flat(cot_ref[f], 12).astype(BF16), flat(states_ref[f], CH).astype(BF16))
        same = lax.rem(iota2((12 * ROWS, TILE), 0), ROWS) == lax.rem(iota2((12 * ROWS, TILE), 1), ROWS)
        total = jnp.where(same, total, 0.0)
        pick_l = jnp.where(iota2((CH, 12 * ROWS), 0) == iota2((CH, 12 * ROWS), 1) // ROWS, 1.0, 0.0)
        pick_r = jnp.where(iota2((TILE, W), 0) // ROWS == iota2((TILE, W), 1), 1.0, 0.0)
        headacc[...] = dot_exact(dot_exact(pick_l, total), pick_r)

    lax.fori_loop(0, blocks, send_chunk, 0)
    build_weights()

    lane = iota2((1, W), 1)

    def shifted(now, before, steps):
        moved = pltpu.roll(now, steps, 1)
        return moved, jnp.where(lane >= steps, moved, before)

    def get_slopes(j):
        for k in range(STEPS):
            h = HALO[k]
            n = 16 - 2 * k

            def whole(slot):
                if k < STEPS - 1:
                    up_a = h_up[slot, A_AT[k] * CH : (A_AT[k] + h) * CH]
                    dn_a = h_dn[slot, A_AT[k] * CH : (A_AT[k] + h) * CH]
                else:
                    up_a, dn_a = p_up[slot], p_dn[slot]
                up_b = h_up[slot, B_AT[k] * CH : (B_AT[k] + h - 1) * CH]
                dn_b = h_dn[slot, B_AT[k] * CH : (B_AT[k] + h - 1) * CH]
                rims = []
                for ref in (h_up, h_dn):
                    rim = ref[slot, RIM_AT * CH : (RIM_AT + 1) * CH]
                    if k > 0:
                        rim = pltpu.roll(rim.astype(F32), CH - 4 * k, 0).astype(BF16)
                    rims.append(rim)
                own_a = zpa[STEPS - 2 - k, slot] if k < STEPS - 1 else zpq[slot]
                return jnp.concatenate(
                    [up_a, own_a, dn_a, rims[0], up_b, zpb[STEPS - 1 - k, slot], dn_b, rims[1]], axis=0
                )

            raw = whole(j + 1)
            size = CH * (n + 2)
            taps = []
            low = (h - 1) * CH
            for m in range(3):
                turn = skew0 + k + m
                moved = pltpu.roll(raw, turn, 1)
                x = jnp.where(lane >= turn, moved, oldx[k, m, 0 : 2 * size])
                oldx[k, m, 0 : 2 * size] = moved
                taps.append(x)
                x_a, x_b = x[:size], x[size:]
                if m == 1:
                    pushed[j, k, 0 : CH * n] = dot(wp[0 : CH * n, 0 : CH * n], x_b[CH : CH + CH * n])
                xs[j, k, m, 0 : 10 * CH] = x_a[low : low + 10 * CH]
                xs[j, k, m, 10 * CH : 20 * CH] = x_b[low : low + 10 * CH]
            preact = biasb[0 : CH * n] + dot(wf[k][...], jnp.concatenate(taps, axis=0))
            col = W * j + lane - (skew0 + k + 1)
            row = ROWS * sp + iota2((CH * n, 1), 0) // CH + (k - STEPS)
            inside = (col >= 0) & (col < cols) & (row >= 0) & (row < ROWS * space_count)
            t = jnp.tanh(preact)
            slopes[j, k, 0 : CH * n] = jnp.where(inside, 1.0 - t * t, 0.0)

    def await_inputs(j):
        @pl.when(has_up)
        def _():
            h_copy(j, False).wait_recv()

        @pl.when(has_dn)
        def _():
            h_copy(j, True).wait_recv()

        @pl.when(jnp.logical_not(is_first))
        def _():
            p_copy(j, 0).wait_recv()

        @pl.when(has_dn)
        def _():
            p_copy(j, 1).wait_recv()

        @pl.when(has_up)
        def _():
            p_copy(j, 2).wait_recv()

    def prepare(j, carry):
        @pl.when(j < blocks)
        def _():
            await_inputs(j)

        get_slopes(j)
        return carry

    def post(j, carry):
        for k in range(STEPS):
            zero = jnp.zeros((CH, W), BF16)
            d = tiles(dkeep[j, k], ROWS)
            g = tiles(gkeep[j, k], ROWS)
            right = jnp.concatenate(
                [
                    jnp.concatenate(d + [zero, zero], axis=1),
                    jnp.concatenate([zero] + d + [zero], axis=1),
                    jnp.concatenate([zero, zero] + d, axis=1),
                    jnp.concatenate([zero] + g + [zero], axis=1),
                ],
                axis=0,
            )
            rows_of = []
            for half in range(2):
                for m in range(3):
                    x = xs[j, k, m, half * 10 * CH : (half + 1) * 10 * CH]
                    rows_of.append(jnp.concatenate(tiles(x, 10), axis=1))
            left = jnp.concatenate(rows_of, axis=0)
            gram[...] += dot_nt(left, right)
        return carry

    group = 2 * CH
    spread_w = W // 4

    def unpack(ref, which):
        value = ref[...]
        return [value if q == 0 else pltpu.roll(value, W - spread_w * q, 1) for q in which]

    def chain(j, last):
        if last:
            parts = unpack(l_up, (2, 3)) + unpack(l_own, (0, 1, 2, 3)) + unpack(l_dn, (0, 1))
        else:
            parts = [c_up[j], c_own[j], c_dn[j]]
        carried = jnp.concatenate(parts, axis=0).astype(F32)
        for k in range(STEPS):
            n = 16 - 2 * k
            size = CH * n
            g = carried + pushed[j, k, 0:size]
            d = (g * slopes[j, k, 0:size]).astype(BF16)
            r1_, d1 = shifted(d, d1prev[k, 0:size], 1)
            r2_, d2 = shifted(d, d2prev[k, 0:size], 2)
            d1prev[k, 0:size] = r1_
            d2prev[k, 0:size] = r2_
            inner = g[CH : size - CH]
            rg, gs = shifted(inner, gprev[k, 0 : size - 2 * CH], 1)
            gprev[k, 0 : size - 2 * CH] = rg
            taps = [d, d1, d2]
            half = CH * (n // 2 - 1)
            conv = jnp.concatenate(
                [
                    dot(wt[k][...], jnp.concatenate([t[at : at + half + 2 * CH] for t in taps], axis=0))
                    for at in (0, half)
                ],
                axis=0,
            )
            carried = retb[0 : size - 2 * CH] * gs + conv
            at = (STEPS - k) * CH
            gfs[j, k] = dot(wc[...], jnp.concatenate([t[at - CH : at + 9 * CH] for t in taps], axis=0))
            dkeep[j, k] = d[at : at + TILE]
            gkeep[j, k] = g[at : at + TILE].astype(BF16)
        out = carried.astype(BF16)
        if last:
            packed = out[0:group]
            for q in range(1, 4):
                packed = jnp.where(
                    lane >= spread_w * q, pltpu.roll(out[group * q : group * (q + 1)], spread_w * q, 1), packed
                )
            l_send[...] = packed
        else:
            c_send[j] = out
        bnd[j] = carried

    def step(j, carry, last=False):
        hop = l_copy if last else functools.partial(c_copy, j)

        @pl.when(is_early)
        def _():
            prepare(j, 0)

        @pl.when(jnp.logical_not(is_last))
        def _():
            hop(0).wait_recv()

            @pl.when(has_dn)
            def _():
                hop(1).wait_recv()

            @pl.when(has_up)
            def _():
                hop(2).wait_recv()

        chain(j, last)

        @pl.when(jnp.logical_not(is_first))
        def _():
            @pl.when(has_up)
            def _():
                hop(1).start()

            @pl.when(has_dn)
            def _():
                hop(2).start()

            hop(0).start()

        @pl.when(jnp.logical_not(is_early))
        def _():
            post(j, 0)

        return carry

    @pl.when(jnp.logical_not(is_early))
    def _():
        head_gradient()
        lax.fori_loop(0, chunks, prepare, 0)

    lax.fori_loop(0, blocks, step, 0)
    step(blocks, 0, True)

    @pl.when(is_early)
    def _():
        lax.fori_loop(0, chunks, post, 0)
        head_gradient()

    rpart[0:16, 0:64] = gram[0:16]
    rpart[0:16, 64:128] = gram[16:32]
    rpart[16:32, 0:64] = gram[32:48]
    rpart[16:32, 64:80] = headacc[:, 0:CH]
    rpart[16:24, 80:128] = gram[80:88, 0:48]
    rpart[24:32, 80:128] = jnp.zeros((8, 48), F32)
    rpart[32:40, 0:64] = gram[48:56]
    rpart[32:40, 64:128] = gram[64:72]

    def first_copy(p):
        return pltpu.make_async_remote_copy(
            src_ref=rpart, dst_ref=rs.at[p], send_sem=s1.at[0], recv_sem=r1.at[p],
            device_id=(0, sp), device_id_type=MESH,
        )

    @pl.when(jnp.logical_not(is_first))
    def _():
        first_copy(tm).start()

    out_shift = skew0 + STEPS + 1

    moves = [
        pltpu.make_async_copy(gf_ref, gf_out, out_sem.at[0]),
        pltpu.make_async_copy(bound_ref, bound_out, out_sem.at[1]),
    ]

    def put_outputs():
        for c in range(blocks):
            def unskew(now, after, shift):
                return jnp.where(lane < W - shift, pltpu.roll(now, W - shift, 1), pltpu.roll(after, W - shift, 1))

            value = unskew(bnd[c], bnd[c + 1], out_shift)
            for r in range(ROWS):
                bound_ref[0, :, r, W * c : W * (c + 1)] = value[CH * r : CH * (r + 1)]
            for k in range(STEPS):
                value = unskew(gfs[c, k, 0:24], gfs[c + 1, k, 0:24], skew0 + k + 2)
                gf_ref[STEPS - 1 - k, :, :, W * c : W * (c + 1)] = value.reshape(3, ROWS, W).astype(BF16)
        for move in moves:
            move.start()

    def second_copy(q):
        s = lax.rem(sp + q, space_count)
        return pltpu.make_async_remote_copy(
            src_ref=ag.at[sp], dst_ref=ag.at[sp], send_sem=s2.at[q], recv_sem=r2.at[q],
            device_id=(0, s), device_id_type=MESH,
        )

    def third_copy(t):
        return pltpu.make_async_remote_copy(
            src_ref=red, dst_ref=red, send_sem=s3.at[t], recv_sem=r3.at[0],
            device_id=(t, sp), device_id_type=MESH,
        )

    @pl.when(is_first)
    def _():
        part = rpart[...]
        for t in range(1, tm_count):
            first_copy(t).wait_recv()
            part = part + rs[t]
        ag[sp] = part
        for q in range(1, space_count):
            second_copy(q).start()
        put_outputs()
        for q in range(1, space_count):
            second_copy(q).wait_recv()
        part = ag[0]
        for q in range(1, space_count):
            part = part + ag[q]
        red[...] = part
        for t in range(1, tm_count):
            third_copy(t).start()

    @pl.when(jnp.logical_not(is_first))
    def _():
        put_outputs()
        third_copy(1).wait_recv()

    sums_ref[...] = red[...]
    for move in moves:
        move.wait()

    @pl.when(is_first)
    def _():
        for q in range(1, space_count):
            second_copy(q).wait_send()
        for t in range(1, tm_count):
            third_copy(t).wait_send()

    @pl.when(jnp.logical_not(is_first))
    def _():
        first_copy(tm).wait_send()

    def drain(j, carry):
        @pl.when(has_up)
        def _():
            h_copy(j, True).wait_send()

        @pl.when(has_dn)
        def _():
            h_copy(j, False).wait_send()

        @pl.when(jnp.logical_not(is_last))
        def _():
            p_copy(j, 0).wait_send()

            @pl.when(has_up)
            def _():
                p_copy(j, 1).wait_send()

            @pl.when(has_dn)
            def _():
                p_copy(j, 2).wait_send()

        @pl.when(is_first)
        def _():
            @pl.when(has_up)
            def _():
                s_copy(j, 1).wait_send()

            @pl.when(has_dn)
            def _():
                s_copy(j, 2).wait_send()

        return carry

    lax.fori_loop(0, blocks, drain, 0)

    @pl.when(jnp.logical_not(is_first))
    def _():
        def drain_carried(way):
            def body(j, carry):
                c_copy(j, way).wait_send()
                return carry

            lax.fori_loop(0, blocks, body, 0)
            l_copy(way).wait_send()

        drain_carried(0)

        @pl.when(has_up)
        def _():
            drain_carried(1)

        @pl.when(has_dn)
        def _():
            drain_carried(2)


def finish(sums_ref, gf_in, bound_in, rec_ref, in_ref, bias_ref, keep_ref, head_ref, gf_ref, bound_ref, sem):
    moves = [pltpu.make_async_copy(gf_in, gf_ref, sem.at[0]), pltpu.make_async_copy(bound_in, bound_ref, sem.at[1])]
    for move in moves:
        move.start()
    sums = sums_ref[...]
    turned = jnp.concatenate([sums, jnp.zeros((W - 40, W), F32)], axis=0).T
    for m in range(3):
        b = 2 - m
        lane_rec, row_rec = [(0, 0), (64, 0), (0, 16)][m]
        lane_in, row_in = [(0, 32), (64, 32), (80, 16)][m]
        for a in range(3):
            rec_ref[3 * a + b] = turned[lane_rec + CH * a : lane_rec + CH * (a + 1), row_rec : row_rec + CH]
            in_ref[3 * a + b] = sums[row_in : row_in + 3, lane_in + CH * a : lane_in + CH * (a + 1)]
    bias_ref[...] = sums[35:36, 80:96].reshape(CH)
    eye = iota2((CH, CH), 0) == iota2((CH, CH), 1)
    keep_ref[...] = jnp.sum(jnp.where(eye, sums[0:16, 112:128], 0.0), axis=0, keepdims=True).reshape(CH)
    head_ref[...] = sums[16:28, 64:80]
    for move in moves:
        move.wait()


def on_device(tm_count, space_count, frames, states, start_state, cotangent, w_rec, w_in, bias_vec, retain, w_head):
    cols = states.shape[3]
    chunks = -(-(cols + STEPS * tm_count + 1) // W)
    blocks = cols // W
    vmem = pl.BlockSpec(memory_space=pltpu.VMEM)
    anywhere = pl.BlockSpec(memory_space=pl.ANY)
    dma = pltpu.SemaphoreType.DMA
    scratch = [
        pltpu.VMEM(frames.shape, BF16),
        pltpu.VMEM((1, CH, ROWS, cols), F32),
        pltpu.VMEM(frames.shape, BF16),
        pltpu.VMEM(states.shape, BF16),
        pltpu.VMEM(start_state.shape, BF16),
        pltpu.VMEM(cotangent.shape, BF16),
        pltpu.VMEM((STEPS, chunks + 1, TILE, W), BF16),
        pltpu.VMEM((STEPS, chunks + 1, TILE, W), BF16),
        pltpu.VMEM((chunks + 1, TILE, W), BF16),
        pltpu.VMEM((blocks, MSG, W), BF16),
        pltpu.VMEM((blocks, MSG, W), BF16),
        pltpu.VMEM((chunks + 1, MSG, W), BF16),
        pltpu.VMEM((chunks + 1, MSG, W), BF16),
        pltpu.VMEM((chunks + 1, 2 * CH, W), BF16),
        pltpu.VMEM((chunks + 1, 2 * CH, W), BF16),
        pltpu.VMEM((STEPS, 3, 36 * CH, W), BF16),
        pltpu.VMEM((chunks, STEPS, 256, W), F32),
        pltpu.VMEM((chunks, STEPS, 256, W), F32),
        pltpu.VMEM((chunks, STEPS, 3, 20 * CH, W), BF16),
        pltpu.VMEM((chunks, STEPS, TILE, W), BF16),
        pltpu.VMEM((chunks, STEPS, TILE, W), BF16),
        pltpu.VMEM((chunks, STEPS, 32, W), F32),
        pltpu.VMEM((chunks, TILE, W), F32),
        pltpu.VMEM((blocks, TILE, W), BF16),
        pltpu.VMEM((blocks, STEPS * CH, W), BF16),
        pltpu.VMEM((blocks, STEPS * CH, W), BF16),
        pltpu.VMEM((blocks, TILE, W), BF16),
        *[pltpu.VMEM((2 * CH, W), BF16)] * 4,
        *[pltpu.VMEM((CH * n, 6 * CH * (n + 2)), BF16) for n in (16, 14, 12, 10)],
        pltpu.VMEM((256, 256), BF16),
        *[pltpu.VMEM((CH * h, 3 * CH * (h + 2)), BF16) for h in (7, 6, 5, 4)],
        pltpu.VMEM((32, 30 * CH), BF16),
        pltpu.VMEM((STEPS, 256, W), BF16),
        pltpu.VMEM((STEPS, 256, W), BF16),
        pltpu.VMEM((STEPS, 256, W), F32),
        pltpu.VMEM((256, W), F32),
        pltpu.VMEM((256, W), F32),
        pltpu.VMEM((96, 64), F32),
        pltpu.VMEM((CH, W), F32),
        pltpu.VMEM((40, W), F32),
        pltpu.VMEM((tm_count, 40, W), F32),
        pltpu.VMEM((space_count, 40, W), F32),
        pltpu.VMEM((40, W), F32),
        dma((2, chunks)), dma((2, chunks)),
        dma((3, chunks)), dma((3, chunks)), dma((3, chunks)),
        dma((3, chunks)), dma((3, chunks)),
        dma((tm_count,)), dma((tm_count,)),
        dma((space_count,)), dma((space_count,)),
        dma((tm_count,)), dma((tm_count,)), dma((4,)), dma((2,)),
    ]
    grad_frames, bound, sums = pl.pallas_call(
        functools.partial(kernel, tm_count, space_count, cols, chunks),
        out_shape=[
            jax.ShapeDtypeStruct((STEPS, 3, ROWS, cols), BF16),
            jax.ShapeDtypeStruct((1, CH, ROWS, cols), F32),
            jax.ShapeDtypeStruct((40, W), F32),
        ],
        in_specs=[anywhere] * 4 + [vmem] * 5,
        out_specs=[anywhere, anywhere, vmem],
        scratch_shapes=scratch,
        compiler_params=pltpu.CompilerParams(
            collective_id=0, has_side_effects=True, vmem_limit_bytes=56 * 1024 * 1024
        ),
    )(
        frames, states, start_state, cotangent, w_rec.transpose(1, 0, 2), w_in.transpose(1, 2, 0), bias_vec, retain, w_head
    )
    out_shape = [
        jax.ShapeDtypeStruct((9, CH, CH), F32),
        jax.ShapeDtypeStruct((9, 3, CH), F32),
        jax.ShapeDtypeStruct((CH,), F32),
        jax.ShapeDtypeStruct((CH,), F32),
        jax.ShapeDtypeStruct((12, CH), F32),
        jax.ShapeDtypeStruct(grad_frames.shape, BF16),
        jax.ShapeDtypeStruct(bound.shape, F32),
    ]
    rec, inp, *rest = pl.pallas_call(
        finish,
        out_shape=out_shape,
        in_specs=[vmem, vmem, vmem],
        out_specs=[vmem] * 5 + [anywhere] * 2,
        scratch_shapes=[dma((2,))],
    )(sums, grad_frames, bound)
    return (rec.transpose(1, 0, 2), inp.transpose(2, 0, 1), *rest)


def solution(mesh):
    banded = P("tm", None, "space", None)
    in_specs = (banded, banded, P(None, "space", None), banded, P(), P(), P(), P(), P())
    out_specs = (P(), P(), P(), P(), P(), banded, banded)
    return jax.shard_map(
        functools.partial(on_device, mesh.shape["tm"], mesh.shape["space"]),
        mesh=mesh, in_specs=in_specs, out_specs=out_specs, check_vma=False,
    )
```

```python
import functools

import jax
import jax.numpy as jnp
from jax import lax
from jax.experimental import pallas as pl
from jax.experimental.pallas import tpu as pltpu
from jax.sharding import PartitionSpec as P

MESH = pl.DeviceIdType.MESH
F32 = jnp.float32
BF16 = jnp.bfloat16
W = 128
CH = 16
ROWS = 8
STEPS = 4
HALO = [STEPS + 1 - k for k in range(STEPS)]
A_AT = [0, 5, 9]
B_AT = [12, 16, 19, 21]
RIM_AT = 22
MSG = 23 * CH
TILE = ROWS * CH


def dot(a, b):
    return lax.dot_general(a, b, (((1,), (0,)), ((), ())), preferred_element_type=F32)


def dot_exact(a, b):
    return lax.dot_general(a, b, (((1,), (0,)), ((), ())), preferred_element_type=F32, precision=lax.Precision.HIGHEST)


def dot_tn(a, b):
    return lax.dot_general(a, b, (((0,), (0,)), ((), ())), preferred_element_type=F32)


def dot_nt(a, b):
    return lax.dot_general(a, b, (((1,), (1,)), ((), ())), preferred_element_type=F32)


def iota2(shape, dim):
    return lax.broadcasted_iota(jnp.int32, shape, dim)


def onehot(cond):
    return jnp.where(cond, 1.0, 0.0).astype(BF16)


def tiles(value, count):
    return [value[CH * i : CH * (i + 1)] for i in range(count)]


def kernel(
    tm_count, space_count, cols, chunks,
    frames_in, states_in, start_in, cot_in, wrec_ref, win_ref, bias_ref, retain_ref, whead_ref,
    gf_out, bound_out, sums_ref,
    gf_ref, bound_ref, frames_ref, states_ref, start_ref, cot_ref,
    zpa, zpb, zpq, stage_up, stage_dn, h_up, h_dn, p_up, p_dn, oldx,
    slopes, pushed, xs, dkeep, gkeep, gfs, bnd, c_own, c_up, c_dn, c_send, l_own, l_up, l_dn, l_send,
    wf0, wf1, wf2, wf3, wp, wt0, wt1, wt2, wt3, wc, d1prev, d2prev, gprev, biasb, retb, gram, headacc, rpart, rs, ag, red,
    h_ssem, h_rsem, p_ssem, p_rsem, e_ssem, c_ssem, c_rsem, s1, r1, s2, r2, s3, r3, in_sem, out_sem,
):
    tm = lax.axis_index("tm")
    sp = lax.axis_index("space")
    has_up = sp > 0
    has_dn = sp < space_count - 1
    is_last = tm == tm_count - 1
    is_first = tm == 0
    is_early = tm >= tm_count - 1
    blocks = cols // W
    wf = [wf0, wf1, wf2, wf3]
    wt = [wt0, wt1, wt2, wt3]
    skew0 = STEPS * (tm_count - 1 - tm)

    loads = [
        pltpu.make_async_copy(src, dst, in_sem.at[i])
        for i, (src, dst) in enumerate(
            [(states_in, states_ref), (frames_in, frames_ref), (cot_in, cot_ref), (start_in, start_ref)]
        )
    ]
    for load in loads:
        load.start()

    zh = jnp.zeros((MSG, W), BF16)
    z2 = jnp.zeros((2 * CH, W), BF16)
    zt = jnp.zeros((TILE, W), BF16)
    @pl.when(jnp.logical_not(has_up))
    def _():
        for j in range(blocks):
            h_up[j + 1] = zh
            p_up[j + 1] = z2
        for j in range(chunks):
            c_up[j] = jnp.zeros((STEPS * CH, W), BF16)

    @pl.when(jnp.logical_not(has_dn))
    def _():
        for j in range(blocks):
            h_dn[j + 1] = zh
            p_dn[j + 1] = z2
        for j in range(chunks):
            c_dn[j] = jnp.zeros((STEPS * CH, W), BF16)

    @pl.when(is_last)
    def _():
        for j in range(chunks):
            c_own[j] = jnp.zeros((TILE, W), BF16)
            c_up[j] = jnp.zeros((STEPS * CH, W), BF16)
            c_dn[j] = jnp.zeros((STEPS * CH, W), BF16)

    barrier = pltpu.get_barrier_semaphore()

    def greet(t, s):
        pl.semaphore_signal(barrier, inc=1, device_id=(t, s), device_id_type=MESH)

    for dt in (0, 1, tm_count - 1):
        for ds in (0, 1, space_count - 1):
            if dt or ds:
                greet(lax.rem(tm + dt, tm_count), lax.rem(sp + ds, space_count))

    @pl.when(jnp.logical_not(is_first))
    def _():
        greet(0, sp)

    @pl.when(is_first)
    def _():
        for t in range(1, tm_count):
            greet(t, sp)
        for q in range(1, space_count):
            greet(0, lax.rem(sp + q, space_count))

    for slot in [0] + list(range(blocks + 1, chunks + 1)):
        h_up[slot] = zh
        h_dn[slot] = zh
        p_up[slot] = z2
        p_dn[slot] = z2
        zpq[slot] = zt
        for f in range(STEPS):
            zpa[f, slot] = zt
            zpb[f, slot] = zt
    for k in range(STEPS):
        for m in range(3):
            oldx[k, m] = jnp.zeros((36 * CH, W), BF16)
        gprev[k] = jnp.zeros((16 * CH, W), F32)
        d1prev[k] = jnp.zeros((16 * CH, W), BF16)
        d2prev[k] = jnp.zeros((16 * CH, W), BF16)
    gram[...] = jnp.zeros_like(gram)

    pr = iota2((TILE, TILE), 0)
    pc = iota2((TILE, TILE), 1)
    perm_a = onehot((pr // CH == lax.rem(pc, ROWS)) & (lax.rem(pr, CH) == pc // ROWS))
    bc = iota2((TILE, 15 * ROWS), 1)
    br = iota2((TILE, 15 * ROWS), 0)
    b_chan = bc // ROWS
    b_chan = b_chan + jnp.where(b_chan >= 3, 1, 0)
    perm_b = onehot((br // CH == lax.rem(bc, ROWS)) & (lax.rem(br, CH) == b_chan))
    ones_b = jnp.where(lax.rem(iota2((TILE, cols), 0), CH) == 3, 1.0, 0.0)

    def flat(value, channels):
        return value.astype(F32).reshape(channels * ROWS, cols)

    def put(ref, value):
        value = value.astype(BF16)
        for c in range(blocks):
            ref[c + 1] = value[:, W * c : W * (c + 1)]

    for load in loads:
        load.wait()
    for f in range(STEPS):
        put(zpa.at[f], dot(perm_a, flat(states_ref[f], CH).astype(BF16)))
        both = jnp.concatenate([flat(frames_ref[f], 3), flat(cot_ref[f], 12)], axis=0).astype(BF16)
        put(zpb.at[f], dot(perm_b, both) + ones_b)

    @pl.when(is_first)
    def _():
        put(zpq, dot(perm_a, flat(start_ref[...], CH).astype(BF16)))

    pl.semaphore_wait(barrier, 8 + jnp.where(is_first, tm_count - 1 + space_count - 1, 1))

    def h_copy(j, up):
        src, dst, target = (stage_up, h_dn, sp - 1) if up else (stage_dn, h_up, sp + 1)
        way = 0 if up else 1
        return pltpu.make_async_remote_copy(
            src_ref=src.at[j], dst_ref=dst.at[j + 1], send_sem=h_ssem.at[way, j], recv_sem=h_rsem.at[way, j],
            device_id=(tm, target), device_id_type=MESH,
        )

    def p_copy(j, way):
        rows = [pl.ds(0, TILE), pl.ds(0, 2 * CH), pl.ds(6 * CH, 2 * CH)][way]
        dst = [zpq.at[j + 1], p_dn.at[j + 1], p_up.at[j + 1]][way]
        target = (tm + 1, [sp, sp - 1, sp + 1][way])
        return pltpu.make_async_remote_copy(
            src_ref=zpa.at[STEPS - 1, j + 1, rows], dst_ref=dst, send_sem=p_ssem.at[way, j], recv_sem=p_rsem.at[way, j],
            device_id=target, device_id_type=MESH,
        )

    def s_copy(j, way):
        rows = [None, pl.ds(0, 2 * CH), pl.ds(6 * CH, 2 * CH)][way]
        dst = [None, p_dn.at[j + 1], p_up.at[j + 1]][way]
        target = (tm, [sp, sp - 1, sp + 1][way])
        return pltpu.make_async_remote_copy(
            src_ref=zpq.at[j + 1, rows], dst_ref=dst, send_sem=e_ssem.at[way, j], recv_sem=p_rsem.at[way, j],
            device_id=target, device_id_type=MESH,
        )

    def c_copy(j, way):
        src = [c_send.at[j], c_send.at[j, pl.ds(0, STEPS * CH)], c_send.at[j, pl.ds(STEPS * CH, STEPS * CH)]][way]
        dst = [c_own.at[j], c_dn.at[j], c_up.at[j]][way]
        target = (tm - 1, [sp, sp - 1, sp + 1][way])
        return pltpu.make_async_remote_copy(
            src_ref=src, dst_ref=dst, send_sem=c_ssem.at[way, j], recv_sem=c_rsem.at[way, j],
            device_id=target, device_id_type=MESH,
        )

    def send_chunk(j, carry):
        @pl.when(jnp.logical_not(is_last))
        def _():
            @pl.when(has_up)
            def _():
                p_copy(j, 1).start()

            @pl.when(has_dn)
            def _():
                p_copy(j, 2).start()

            p_copy(j, 0).start()

        rims = [[], []]
        for k in range(STEPS):
            h = HALO[k]
            b_val = zpb[STEPS - 1 - k, j + 1]
            stage_up[j, B_AT[k] * CH : (B_AT[k] + h - 1) * CH] = b_val[: (h - 1) * CH]
            stage_dn[j, B_AT[k] * CH : (B_AT[k] + h - 1) * CH] = b_val[TILE - (h - 1) * CH :]
            rims[0].append(b_val[(h - 1) * CH : h * CH].astype(F32))
            rims[1].append(b_val[TILE - h * CH : TILE - (h - 1) * CH].astype(F32))
            if k < STEPS - 1:
                a_val = zpa[STEPS - 2 - k, j + 1]
                stage_up[j, A_AT[k] * CH : (A_AT[k] + h) * CH] = a_val[: h * CH]
                stage_dn[j, A_AT[k] * CH : (A_AT[k] + h) * CH] = a_val[TILE - h * CH :]

        for stage, rim in ((stage_up, rims[0]), (stage_dn, rims[1])):
            value = rim[0]
            for k in range(1, STEPS):
                value = jnp.where(iota2((CH, 1), 0) >= 4 * k, pltpu.roll(rim[k], 4 * k, 0), value)
            stage[j, RIM_AT * CH : (RIM_AT + 1) * CH] = value.astype(BF16)

        @pl.when(has_up)
        def _():
            h_copy(j, True).start()

        @pl.when(has_dn)
        def _():
            h_copy(j, False).start()

        @pl.when(is_first)
        def _():
            @pl.when(has_up)
            def _():
                s_copy(j, 1).start()

            @pl.when(has_dn)
            def _():
                s_copy(j, 2).start()

        return carry

    def l_copy(way):
        dst = [l_own, l_dn, l_up][way]
        target = (tm - 1, [sp, sp - 1, sp + 1][way])
        return pltpu.make_async_remote_copy(
            src_ref=l_send, dst_ref=dst, send_sem=c_ssem.at[way, blocks], recv_sem=c_rsem.at[way, blocks],
            device_id=target, device_id_type=MESH,
        )

    def column(ref):
        row = ref[...].reshape(1, CH)
        eye = iota2((CH, CH), 0) == iota2((CH, CH), 1)
        value = jnp.sum(jnp.where(eye, row, 0.0), axis=1, keepdims=True)
        return jnp.concatenate([jnp.broadcast_to(value, (CH, W))] * 16, axis=0)

    def build_weights():
        biasb[...] = column(bias_ref)
        retb[...] = column(retain_ref)
        rec = [wrec_ref[t] for t in range(9)]
        inp = [win_ref[t] for t in range(9)]
        chan_of = iota2((32, CH), 0) // ROWS == iota2((32, CH), 1)
        inp_rows = [dot(onehot(chan_of[:, :3]), inp[t]).astype(BF16) for t in range(9)]
        for k in range(STEPS):
            n = 16 - 2 * k
            size = CH * (n + 2)
            at = iota2((1, 6 * size), 1)
            part = at // size
            row_in = lax.rem(at, size) // CH
            chan = lax.rem(at, CH)
            picks = []
            for m in range(3):
                picks.append(
                    (
                        onehot((iota2((CH, 6 * size), 0) == chan) & (part == 2 * m)),
                        onehot((iota2((3, 6 * size), 0) == chan) & (part == 2 * m + 1)),
                    )
                )
            base = []
            for a in range(3):
                total = jnp.zeros((CH, 6 * size), F32)
                for m in range(3):
                    t = 3 * a + 2 - m
                    total = total + dot(rec[t], picks[m][0]) + dot_tn(inp[t], picks[m][1])
                base.append(total)
            for r in range(n):
                ahead = row_in - r
                value = jnp.where(ahead == 0, base[0], jnp.where(ahead == 1, base[1], jnp.where(ahead == 2, base[2], 0.0)))
                wf[k][CH * r : CH * (r + 1)] = value.astype(BF16)
            half = n // 2 - 1
            size = CH * (half + 2)
            at = iota2((1, 3 * size), 1)
            part = at // size
            row_in = lax.rem(at, size) // CH
            chan = lax.rem(at, CH)
            picks = [onehot((iota2((CH, 3 * size), 0) == chan) & (part == b)) for b in range(3)]
            base = []
            for a in range(3):
                total = jnp.zeros((CH, 3 * size), F32)
                for b in range(3):
                    total = total + dot_tn(rec[3 * a + b], picks[b])
                base.append(total)
            for r in range(half):
                behind = r + 2 - row_in
                value = jnp.where(
                    behind == 0, base[0], jnp.where(behind == 1, base[1], jnp.where(behind == 2, base[2], 0.0))
                )
                wt[k][CH * r : CH * (r + 1)] = value.astype(BF16)
        size = 10 * CH
        at = iota2((1, 3 * size), 1)
        part = at // size
        row_in = lax.rem(at, size) // CH
        chan = lax.rem(at, CH)
        picks = [onehot((iota2((CH, 3 * size), 0) == chan) & (part == b)) for b in range(3)]
        behind = lax.rem(iota2((32, 1), 0), ROWS) + 2 - row_in
        value = jnp.zeros((32, 3 * size), F32)
        for a in range(3):
            total = jnp.zeros((32, 3 * size), F32)
            for b in range(3):
                total = total + dot(inp_rows[3 * a + b], picks[b])
            value = jnp.where(behind == a, total, value)
        wc[...] = value.astype(BF16)
        pick = onehot(iota2((12, 256), 0) == lax.rem(iota2((12, 256), 1), CH) - 4)
        base_h = dot_tn(whead_ref[...], pick)
        for r in range(16):
            wp[CH * r : CH * (r + 1)] = jnp.where(iota2((1, 256), 1) // CH == r, base_h, 0.0).astype(BF16)

    def head_gradient():
        total = jnp.zeros((12 * ROWS, TILE), F32)
        for f in range(STEPS):
            total = total + dot_nt(flat(cot_ref[f], 12).astype(BF16), flat(states_ref[f], CH).astype(BF16))
        same = lax.rem(iota2((12 * ROWS, TILE), 0), ROWS) == lax.rem(iota2((12 * ROWS, TILE), 1), ROWS)
        total = jnp.where(same, total, 0.0)
        pick_l = jnp.where(iota2((CH, 12 * ROWS), 0) == iota2((CH, 12 * ROWS), 1) // ROWS, 1.0, 0.0)
        pick_r = jnp.where(iota2((TILE, W), 0) // ROWS == iota2((TILE, W), 1), 1.0, 0.0)
        headacc[...] = dot_exact(dot_exact(pick_l, total), pick_r)

    lax.fori_loop(0, blocks, send_chunk, 0)
    build_weights()

    lane = iota2((1, W), 1)

    def shifted(now, before, steps):
        moved = pltpu.roll(now, steps, 1)
        return moved, jnp.where(lane >= steps, moved, before)

    def get_slopes(j):
        for k in range(STEPS):
            h = HALO[k]
            n = 16 - 2 * k

            def whole(slot):
                if k < STEPS - 1:
                    up_a = h_up[slot, A_AT[k] * CH : (A_AT[k] + h) * CH]
                    dn_a = h_dn[slot, A_AT[k] * CH : (A_AT[k] + h) * CH]
                else:
                    up_a, dn_a = p_up[slot], p_dn[slot]
                up_b = h_up[slot, B_AT[k] * CH : (B_AT[k] + h - 1) * CH]
                dn_b = h_dn[slot, B_AT[k] * CH : (B_AT[k] + h - 1) * CH]
                rims = []
                for ref in (h_up, h_dn):
                    rim = ref[slot, RIM_AT * CH : (RIM_AT + 1) * CH]
                    if k > 0:
                        rim = pltpu.roll(rim.astype(F32), CH - 4 * k, 0).astype(BF16)
                    rims.append(rim)
                own_a = zpa[STEPS - 2 - k, slot] if k < STEPS - 1 else zpq[slot]
                return jnp.concatenate(
                    [up_a, own_a, dn_a, rims[0], up_b, zpb[STEPS - 1 - k, slot], dn_b, rims[1]], axis=0
                )

            raw = whole(j + 1)
            size = CH * (n + 2)
            taps = []
            low = (h - 1) * CH
            for m in range(3):
                turn = skew0 + k + m
                moved = pltpu.roll(raw, turn, 1)
                x = jnp.where(lane >= turn, moved, oldx[k, m, 0 : 2 * size])
                oldx[k, m, 0 : 2 * size] = moved
                taps.append(x)
                x_a, x_b = x[:size], x[size:]
                if m == 1:
                    pushed[j, k, 0 : CH * n] = dot(wp[0 : CH * n, 0 : CH * n], x_b[CH : CH + CH * n])
                xs[j, k, m, 0 : 10 * CH] = x_a[low : low + 10 * CH]
                xs[j, k, m, 10 * CH : 20 * CH] = x_b[low : low + 10 * CH]
            preact = biasb[0 : CH * n] + dot(wf[k][...], jnp.concatenate(taps, axis=0))
            col = W * j + lane - (skew0 + k + 1)
            row = ROWS * sp + iota2((CH * n, 1), 0) // CH + (k - STEPS)
            inside = (col >= 0) & (col < cols) & (row >= 0) & (row < ROWS * space_count)
            t = jnp.tanh(preact)
            slopes[j, k, 0 : CH * n] = jnp.where(inside, 1.0 - t * t, 0.0)

    def await_inputs(j):
        @pl.when(has_up)
        def _():
            h_copy(j, False).wait_recv()

        @pl.when(has_dn)
        def _():
            h_copy(j, True).wait_recv()

        @pl.when(jnp.logical_not(is_first))
        def _():
            p_copy(j, 0).wait_recv()

        @pl.when(has_dn)
        def _():
            p_copy(j, 1).wait_recv()

        @pl.when(has_up)
        def _():
            p_copy(j, 2).wait_recv()

    def prepare(j, carry):
        @pl.when(j < blocks)
        def _():
            await_inputs(j)

        get_slopes(j)
        return carry

    def post(j, carry):
        for k in range(STEPS):
            zero = jnp.zeros((CH, W), BF16)
            d = tiles(dkeep[j, k], ROWS)
            g = tiles(gkeep[j, k], ROWS)
            right = jnp.concatenate(
                [
                    jnp.concatenate(d + [zero, zero], axis=1),
                    jnp.concatenate([zero] + d + [zero], axis=1),
                    jnp.concatenate([zero, zero] + d, axis=1),
                    jnp.concatenate([zero] + g + [zero], axis=1),
                ],
                axis=0,
            )
            rows_of = []
            for half in range(2):
                for m in range(3):
                    x = xs[j, k, m, half * 10 * CH : (half + 1) * 10 * CH]
                    rows_of.append(jnp.concatenate(tiles(x, 10), axis=1))
            left = jnp.concatenate(rows_of, axis=0)
            gram[...] += dot_nt(left, right)
        return carry

    group = 2 * CH
    spread_w = W // 4

    def unpack(ref, dst, which):
        value = ref[...]
        for at, q in enumerate(which):
            part = value if q == 0 else pltpu.roll(value, W - spread_w * q, 1)
            dst[blocks, group * at : group * (at + 1)] = part

    def chain(j):
        carried = jnp.concatenate([c_up[j], c_own[j], c_dn[j]], axis=0).astype(F32)
        for k in range(STEPS):
            n = 16 - 2 * k
            size = CH * n
            g = carried + pushed[j, k, 0:size]
            d = (g * slopes[j, k, 0:size]).astype(BF16)
            r1_, d1 = shifted(d, d1prev[k, 0:size], 1)
            r2_, d2 = shifted(d, d2prev[k, 0:size], 2)
            d1prev[k, 0:size] = r1_
            d2prev[k, 0:size] = r2_
            inner = g[CH : size - CH]
            rg, gs = shifted(inner, gprev[k, 0 : size - 2 * CH], 1)
            gprev[k, 0 : size - 2 * CH] = rg
            taps = [d, d1, d2]
            half = CH * (n // 2 - 1)
            conv = jnp.concatenate(
                [
                    dot(wt[k][...], jnp.concatenate([t[at : at + half + 2 * CH] for t in taps], axis=0))
                    for at in (0, half)
                ],
                axis=0,
            )
            carried = retb[0 : size - 2 * CH] * gs + conv
            at = (STEPS - k) * CH
            gfs[j, k] = dot(wc[...], jnp.concatenate([t[at - CH : at + 9 * CH] for t in taps], axis=0))
            dkeep[j, k] = d[at : at + TILE]
            gkeep[j, k] = g[at : at + TILE].astype(BF16)
        c_send[j] = carried.astype(BF16)
        bnd[j] = carried

    def await_carried(hop):
        hop(0).wait_recv()

        @pl.when(has_dn)
        def _():
            hop(1).wait_recv()

        @pl.when(has_up)
        def _():
            hop(2).wait_recv()

    def start_carried(hop):
        @pl.when(has_up)
        def _():
            hop(1).start()

        @pl.when(has_dn)
        def _():
            hop(2).start()

        hop(0).start()

    def step(j, carry):
        @pl.when(is_last)
        def _():
            prepare(j, 0)

        @pl.when(jnp.logical_not(is_last) & (j < blocks))
        def _():
            await_carried(functools.partial(c_copy, j))

        @pl.when(jnp.logical_not(is_last) & (j == blocks))
        def _():
            await_carried(l_copy)
            unpack(l_own, c_own, (0, 1, 2, 3))

            @pl.when(has_up)
            def _():
                unpack(l_up, c_up, (2, 3))

            @pl.when(has_dn)
            def _():
                unpack(l_dn, c_dn, (0, 1))

        chain(j)

        @pl.when(jnp.logical_not(is_first) & (j < blocks))
        def _():
            start_carried(functools.partial(c_copy, j))

        @pl.when(jnp.logical_not(is_first) & (j == blocks))
        def _():
            packed = c_send[blocks, 0:group]
            for q in range(1, 4):
                turned = pltpu.roll(c_send[blocks, group * q : group * (q + 1)], spread_w * q, 1)
                packed = jnp.where(lane >= spread_w * q, turned, packed)
            l_send[...] = packed
            start_carried(l_copy)

        @pl.when(jnp.logical_not(is_early))
        def _():
            post(j, 0)

        return carry

    @pl.when(jnp.logical_not(is_early))
    def _():
        head_gradient()
        lax.fori_loop(0, chunks, prepare, 0)

    lax.fori_loop(0, chunks, step, 0)

    @pl.when(is_early)
    def _():
        lax.fori_loop(0, chunks, post, 0)
        head_gradient()

    rpart[0:16, 0:64] = gram[0:16]
    rpart[0:16, 64:128] = gram[16:32]
    rpart[16:32, 0:64] = gram[32:48]
    rpart[16:32, 64:80] = headacc[:, 0:CH]
    rpart[16:24, 80:128] = gram[80:88, 0:48]
    rpart[24:32, 80:128] = jnp.zeros((8, 48), F32)
    rpart[32:40, 0:64] = gram[48:56]
    rpart[32:40, 64:128] = gram[64:72]

    def first_copy(p):
        return pltpu.make_async_remote_copy(
            src_ref=rpart, dst_ref=rs.at[p], send_sem=s1.at[0], recv_sem=r1.at[p],
            device_id=(0, sp), device_id_type=MESH,
        )

    @pl.when(jnp.logical_not(is_first))
    def _():
        first_copy(tm).start()

    out_shift = skew0 + STEPS + 1

    moves = [
        pltpu.make_async_copy(gf_ref, gf_out, out_sem.at[0]),
        pltpu.make_async_copy(bound_ref, bound_out, out_sem.at[1]),
    ]

    def put_outputs():
        for c in range(blocks):
            def unskew(now, after, shift):
                return jnp.where(lane < W - shift, pltpu.roll(now, W - shift, 1), pltpu.roll(after, W - shift, 1))

            value = unskew(bnd[c], bnd[c + 1], out_shift)
            for r in range(ROWS):
                bound_ref[0, :, r, W * c : W * (c + 1)] = value[CH * r : CH * (r + 1)]
            for k in range(STEPS):
                value = unskew(gfs[c, k, 0:24], gfs[c + 1, k, 0:24], skew0 + k + 2)
                gf_ref[STEPS - 1 - k, :, :, W * c : W * (c + 1)] = value.reshape(3, ROWS, W).astype(BF16)
        for move in moves:
            move.start()

    def second_copy(q):
        s = lax.rem(sp + q, space_count)
        return pltpu.make_async_remote_copy(
            src_ref=ag.at[sp], dst_ref=ag.at[sp], send_sem=s2.at[q], recv_sem=r2.at[q],
            device_id=(0, s), device_id_type=MESH,
        )

    def third_copy(t):
        return pltpu.make_async_remote_copy(
            src_ref=red, dst_ref=red, send_sem=s3.at[t], recv_sem=r3.at[0],
            device_id=(t, sp), device_id_type=MESH,
        )

    @pl.when(is_first)
    def _():
        part = rpart[...]
        for t in range(1, tm_count):
            first_copy(t).wait_recv()
            part = part + rs[t]
        ag[sp] = part
        for q in range(1, space_count):
            second_copy(q).start()
        put_outputs()
        for q in range(1, space_count):
            second_copy(q).wait_recv()
        part = ag[0]
        for q in range(1, space_count):
            part = part + ag[q]
        red[...] = part
        for t in range(1, tm_count):
            third_copy(t).start()

    @pl.when(jnp.logical_not(is_first))
    def _():
        put_outputs()
        third_copy(1).wait_recv()

    sums_ref[...] = red[...]
    for move in moves:
        move.wait()

    @pl.when(is_first)
    def _():
        for q in range(1, space_count):
            second_copy(q).wait_send()
        for t in range(1, tm_count):
            third_copy(t).wait_send()

    @pl.when(jnp.logical_not(is_first))
    def _():
        first_copy(tm).wait_send()

    def drain(j, carry):
        @pl.when(has_up)
        def _():
            h_copy(j, True).wait_send()

        @pl.when(has_dn)
        def _():
            h_copy(j, False).wait_send()

        @pl.when(jnp.logical_not(is_last))
        def _():
            p_copy(j, 0).wait_send()

            @pl.when(has_up)
            def _():
                p_copy(j, 1).wait_send()

            @pl.when(has_dn)
            def _():
                p_copy(j, 2).wait_send()

        @pl.when(is_first)
        def _():
            @pl.when(has_up)
            def _():
                s_copy(j, 1).wait_send()

            @pl.when(has_dn)
            def _():
                s_copy(j, 2).wait_send()

        return carry

    lax.fori_loop(0, blocks, drain, 0)

    @pl.when(jnp.logical_not(is_first))
    def _():
        def drain_carried(way):
            def body(j, carry):
                c_copy(j, way).wait_send()
                return carry

            lax.fori_loop(0, blocks, body, 0)
            l_copy(way).wait_send()

        drain_carried(0)

        @pl.when(has_up)
        def _():
            drain_carried(1)

        @pl.when(has_dn)
        def _():
            drain_carried(2)


def finish(sums_ref, gf_in, bound_in, rec_ref, in_ref, bias_ref, keep_ref, head_ref, gf_ref, bound_ref, sem):
    moves = [pltpu.make_async_copy(gf_in, gf_ref, sem.at[0]), pltpu.make_async_copy(bound_in, bound_ref, sem.at[1])]
    for move in moves:
        move.start()
    sums = sums_ref[...]
    turned = jnp.concatenate([sums, jnp.zeros((W - 40, W), F32)], axis=0).T
    for m in range(3):
        b = 2 - m
        lane_rec, row_rec = [(0, 0), (64, 0), (0, 16)][m]
        lane_in, row_in = [(0, 32), (64, 32), (80, 16)][m]
        for a in range(3):
            rec_ref[3 * a + b] = turned[lane_rec + CH * a : lane_rec + CH * (a + 1), row_rec : row_rec + CH]
            in_ref[3 * a + b] = sums[row_in : row_in + 3, lane_in + CH * a : lane_in + CH * (a + 1)]
    bias_ref[...] = sums[35:36, 80:96].reshape(CH)
    eye = iota2((CH, CH), 0) == iota2((CH, CH), 1)
    keep_ref[...] = jnp.sum(jnp.where(eye, sums[0:16, 112:128], 0.0), axis=0, keepdims=True).reshape(CH)
    head_ref[...] = sums[16:28, 64:80]
    for move in moves:
        move.wait()


def on_device(tm_count, space_count, frames, states, start_state, cotangent, w_rec, w_in, bias_vec, retain, w_head):
    cols = states.shape[3]
    chunks = -(-(cols + STEPS * tm_count + 1) // W)
    blocks = cols // W
    vmem = pl.BlockSpec(memory_space=pltpu.VMEM)
    anywhere = pl.BlockSpec(memory_space=pl.ANY)
    dma = pltpu.SemaphoreType.DMA
    scratch = [
        pltpu.VMEM(frames.shape, BF16),
        pltpu.VMEM((1, CH, ROWS, cols), F32),
        pltpu.VMEM(frames.shape, BF16),
        pltpu.VMEM(states.shape, BF16),
        pltpu.VMEM(start_state.shape, BF16),
        pltpu.VMEM(cotangent.shape, BF16),
        pltpu.VMEM((STEPS, chunks + 1, TILE, W), BF16),
        pltpu.VMEM((STEPS, chunks + 1, TILE, W), BF16),
        pltpu.VMEM((chunks + 1, TILE, W), BF16),
        pltpu.VMEM((blocks, MSG, W), BF16),
        pltpu.VMEM((blocks, MSG, W), BF16),
        pltpu.VMEM((chunks + 1, MSG, W), BF16),
        pltpu.VMEM((chunks + 1, MSG, W), BF16),
        pltpu.VMEM((chunks + 1, 2 * CH, W), BF16),
        pltpu.VMEM((chunks + 1, 2 * CH, W), BF16),
        pltpu.VMEM((STEPS, 3, 36 * CH, W), BF16),
        pltpu.VMEM((chunks, STEPS, 256, W), F32),
        pltpu.VMEM((chunks, STEPS, 256, W), F32),
        pltpu.VMEM((chunks, STEPS, 3, 20 * CH, W), BF16),
        pltpu.VMEM((chunks, STEPS, TILE, W), BF16),
        pltpu.VMEM((chunks, STEPS, TILE, W), BF16),
        pltpu.VMEM((chunks, STEPS, 32, W), F32),
        pltpu.VMEM((chunks, TILE, W), F32),
        pltpu.VMEM((chunks, TILE, W), BF16),
        pltpu.VMEM((chunks, STEPS * CH, W), BF16),
        pltpu.VMEM((chunks, STEPS * CH, W), BF16),
        pltpu.VMEM((chunks, TILE, W), BF16),
        *[pltpu.VMEM((2 * CH, W), BF16)] * 4,
        *[pltpu.VMEM((CH * n, 6 * CH * (n + 2)), BF16) for n in (16, 14, 12, 10)],
        pltpu.VMEM((256, 256), BF16),
        *[pltpu.VMEM((CH * h, 3 * CH * (h + 2)), BF16) for h in (7, 6, 5, 4)],
        pltpu.VMEM((32, 30 * CH), BF16),
        pltpu.VMEM((STEPS, 256, W), BF16),
        pltpu.VMEM((STEPS, 256, W), BF16),
        pltpu.VMEM((STEPS, 256, W), F32),
        pltpu.VMEM((256, W), F32),
        pltpu.VMEM((256, W), F32),
        pltpu.VMEM((96, 64), F32),
        pltpu.VMEM((CH, W), F32),
        pltpu.VMEM((40, W), F32),
        pltpu.VMEM((tm_count, 40, W), F32),
        pltpu.VMEM((space_count, 40, W), F32),
        pltpu.VMEM((40, W), F32),
        dma((2, chunks)), dma((2, chunks)),
        dma((3, chunks)), dma((3, chunks)), dma((3, chunks)),
        dma((3, chunks)), dma((3, chunks)),
        dma((tm_count,)), dma((tm_count,)),
        dma((space_count,)), dma((space_count,)),
        dma((tm_count,)), dma((tm_count,)), dma((4,)), dma((2,)),
    ]
    grad_frames, bound, sums = pl.pallas_call(
        functools.partial(kernel, tm_count, space_count, cols, chunks),
        out_shape=[
            jax.ShapeDtypeStruct((STEPS, 3, ROWS, cols), BF16),
            jax.ShapeDtypeStruct((1, CH, ROWS, cols), F32),
            jax.ShapeDtypeStruct((40, W), F32),
        ],
        in_specs=[anywhere] * 4 + [vmem] * 5,
        out_specs=[anywhere, anywhere, vmem],
        scratch_shapes=scratch,
        compiler_params=pltpu.CompilerParams(
            collective_id=0, has_side_effects=True, vmem_limit_bytes=56 * 1024 * 1024
        ),
    )(
        frames, states, start_state, cotangent, w_rec.transpose(1, 0, 2), w_in.transpose(1, 2, 0), bias_vec, retain, w_head
    )
    out_shape = [
        jax.ShapeDtypeStruct((9, CH, CH), F32),
        jax.ShapeDtypeStruct((9, 3, CH), F32),
        jax.ShapeDtypeStruct((CH,), F32),
        jax.ShapeDtypeStruct((CH,), F32),
        jax.ShapeDtypeStruct((12, CH), F32),
        jax.ShapeDtypeStruct(grad_frames.shape, BF16),
        jax.ShapeDtypeStruct(bound.shape, F32),
    ]
    rec, inp, *rest = pl.pallas_call(
        finish,
        out_shape=out_shape,
        in_specs=[vmem, vmem, vmem],
        out_specs=[vmem] * 5 + [anywhere] * 2,
        scratch_shapes=[dma((2,))],
    )(sums, grad_frames, bound)
    return (rec.transpose(1, 0, 2), inp.transpose(2, 0, 1), *rest)


def solution(mesh):
    banded = P("tm", None, "space", None)
    in_specs = (banded, banded, P(None, "space", None), banded, P(), P(), P(), P(), P())
    out_specs = (P(), P(), P(), P(), P(), banded, banded)
    return jax.shard_map(
        functools.partial(on_device, mesh.shape["tm"], mesh.shape["space"]),
        mesh=mesh, in_specs=in_specs, out_specs=out_specs, check_vma=False,
    )
```

```python
import functools

import jax
import jax.numpy as jnp
from jax import lax
from jax.experimental import pallas as pl
from jax.experimental.pallas import tpu as pltpu
from jax.sharding import PartitionSpec as P

MESH = pl.DeviceIdType.MESH
F32 = jnp.float32
BF16 = jnp.bfloat16
W = 128
CH = 16
ROWS = 8
STEPS = 4
HALO = [STEPS + 1 - k for k in range(STEPS)]
A_AT = [0, 5, 9]
B_AT = [12, 16, 19, 21]
RIM_AT = 22
MSG = 23 * CH
TILE = ROWS * CH


def dot(a, b):
    return lax.dot_general(a, b, (((1,), (0,)), ((), ())), preferred_element_type=F32)


def dot_exact(a, b):
    return lax.dot_general(a, b, (((1,), (0,)), ((), ())), preferred_element_type=F32, precision=lax.Precision.HIGHEST)


def dot_tn(a, b):
    return lax.dot_general(a, b, (((0,), (0,)), ((), ())), preferred_element_type=F32)


def dot_nt(a, b):
    return lax.dot_general(a, b, (((1,), (1,)), ((), ())), preferred_element_type=F32)


def iota2(shape, dim):
    return lax.broadcasted_iota(jnp.int32, shape, dim)


def onehot(cond):
    return jnp.where(cond, 1.0, 0.0).astype(BF16)


def tiles(value, count):
    return [value[CH * i : CH * (i + 1)] for i in range(count)]


def kernel(
    tm_count, space_count, cols, chunks,
    frames_in, states_in, start_in, cot_in, wrec_ref, win_ref, bias_ref, retain_ref, whead_ref,
    gf_out, bound_out, sums_ref,
    gf_ref, bound_ref, frames_ref, states_ref, start_ref, cot_ref,
    zpa, zpb, zpq, stage_up, stage_dn, h_up, h_dn, p_up, p_dn, oldx,
    slopes, pushed, xs, dkeep, gkeep, gfs, bnd, c_own, c_up, c_dn, c_send, l_own, l_up, l_dn, l_send,
    wf0, wf1, wf2, wf3, wp, wt0, wt1, wt2, wt3, wc, d1prev, d2prev, gprev, biasb, retb, gram, headacc, rpart, rs, ag, red,
    h_ssem, h_rsem, p_ssem, p_rsem, e_ssem, c_ssem, c_rsem, s1, r1, s2, r2, s3, r3, in_sem, out_sem,
):
    tm = lax.axis_index("tm")
    sp = lax.axis_index("space")
    has_up = sp > 0
    has_dn = sp < space_count - 1
    is_last = tm == tm_count - 1
    is_first = tm == 0
    is_early = tm >= tm_count - 2
    blocks = cols // W
    wf = [wf0, wf1, wf2, wf3]
    wt = [wt0, wt1, wt2, wt3]
    skew0 = STEPS * (tm_count - 1 - tm)

    loads = [
        pltpu.make_async_copy(src, dst, in_sem.at[i])
        for i, (src, dst) in enumerate(
            [(states_in, states_ref), (frames_in, frames_ref), (cot_in, cot_ref), (start_in, start_ref)]
        )
    ]
    for load in loads:
        load.start()

    zh = jnp.zeros((MSG, W), BF16)
    z2 = jnp.zeros((2 * CH, W), BF16)
    zt = jnp.zeros((TILE, W), BF16)
    @pl.when(jnp.logical_not(has_up))
    def _():
        for j in range(blocks):
            h_up[j + 1] = zh
            p_up[j + 1] = z2
        for j in range(chunks):
            c_up[j] = jnp.zeros((STEPS * CH, W), BF16)

    @pl.when(jnp.logical_not(has_dn))
    def _():
        for j in range(blocks):
            h_dn[j + 1] = zh
            p_dn[j + 1] = z2
        for j in range(chunks):
            c_dn[j] = jnp.zeros((STEPS * CH, W), BF16)

    @pl.when(is_last)
    def _():
        for j in range(chunks):
            c_own[j] = jnp.zeros((TILE, W), BF16)
            c_up[j] = jnp.zeros((STEPS * CH, W), BF16)
            c_dn[j] = jnp.zeros((STEPS * CH, W), BF16)

    barrier = pltpu.get_barrier_semaphore()

    def greet(t, s):
        pl.semaphore_signal(barrier, inc=1, device_id=(t, s), device_id_type=MESH)

    for dt in (0, 1, tm_count - 1):
        for ds in (0, 1, space_count - 1):
            if dt or ds:
                greet(lax.rem(tm + dt, tm_count), lax.rem(sp + ds, space_count))

    @pl.when(jnp.logical_not(is_first))
    def _():
        greet(0, sp)

    @pl.when(is_first)
    def _():
        for t in range(1, tm_count):
            greet(t, sp)
        for q in range(1, space_count):
            greet(0, lax.rem(sp + q, space_count))

    for slot in [0] + list(range(blocks + 1, chunks + 1)):
        h_up[slot] = zh
        h_dn[slot] = zh
        p_up[slot] = z2
        p_dn[slot] = z2
        zpq[slot] = zt
        for f in range(STEPS):
            zpa[f, slot] = zt
            zpb[f, slot] = zt
    for k in range(STEPS):
        for m in range(3):
            oldx[k, m] = jnp.zeros((36 * CH, W), BF16)
        gprev[k] = jnp.zeros((16 * CH, W), F32)
        d1prev[k] = jnp.zeros((16 * CH, W), BF16)
        d2prev[k] = jnp.zeros((16 * CH, W), BF16)
    gram[...] = jnp.zeros_like(gram)

    pr = iota2((TILE, TILE), 0)
    pc = iota2((TILE, TILE), 1)
    perm_a = onehot((pr // CH == lax.rem(pc, ROWS)) & (lax.rem(pr, CH) == pc // ROWS))
    bc = iota2((TILE, 15 * ROWS), 1)
    br = iota2((TILE, 15 * ROWS), 0)
    b_chan = bc // ROWS
    b_chan = b_chan + jnp.where(b_chan >= 3, 1, 0)
    perm_b = onehot((br // CH == lax.rem(bc, ROWS)) & (lax.rem(br, CH) == b_chan))
    ones_b = jnp.where(lax.rem(iota2((TILE, cols), 0), CH) == 3, 1.0, 0.0)

    def flat(value, channels):
        return value.astype(F32).reshape(channels * ROWS, cols)

    def put(ref, value):
        value = value.astype(BF16)
        for c in range(blocks):
            ref[c + 1] = value[:, W * c : W * (c + 1)]

    for load in loads:
        load.wait()
    for f in range(STEPS):
        put(zpa.at[f], dot(perm_a, flat(states_ref[f], CH).astype(BF16)))
        both = jnp.concatenate([flat(frames_ref[f], 3), flat(cot_ref[f], 12)], axis=0).astype(BF16)
        put(zpb.at[f], dot(perm_b, both) + ones_b)

    @pl.when(is_first)
    def _():
        put(zpq, dot(perm_a, flat(start_ref[...], CH).astype(BF16)))

    pl.semaphore_wait(barrier, 8 + jnp.where(is_first, tm_count - 1 + space_count - 1, 1))

    def h_copy(j, up):
        src, dst, target = (stage_up, h_dn, sp - 1) if up else (stage_dn, h_up, sp + 1)
        way = 0 if up else 1
        return pltpu.make_async_remote_copy(
            src_ref=src.at[j], dst_ref=dst.at[j + 1], send_sem=h_ssem.at[way, j], recv_sem=h_rsem.at[way, j],
            device_id=(tm, target), device_id_type=MESH,
        )

    def p_copy(j, way):
        rows = [pl.ds(0, TILE), pl.ds(0, 2 * CH), pl.ds(6 * CH, 2 * CH)][way]
        dst = [zpq.at[j + 1], p_dn.at[j + 1], p_up.at[j + 1]][way]
        target = (tm + 1, [sp, sp - 1, sp + 1][way])
        return pltpu.make_async_remote_copy(
            src_ref=zpa.at[STEPS - 1, j + 1, rows], dst_ref=dst, send_sem=p_ssem.at[way, j], recv_sem=p_rsem.at[way, j],
            device_id=target, device_id_type=MESH,
        )

    def s_copy(j, way):
        rows = [None, pl.ds(0, 2 * CH), pl.ds(6 * CH, 2 * CH)][way]
        dst = [None, p_dn.at[j + 1], p_up.at[j + 1]][way]
        target = (tm, [sp, sp - 1, sp + 1][way])
        return pltpu.make_async_remote_copy(
            src_ref=zpq.at[j + 1, rows], dst_ref=dst, send_sem=e_ssem.at[way, j], recv_sem=p_rsem.at[way, j],
            device_id=target, device_id_type=MESH,
        )

    def c_copy(j, way):
        src = [c_send.at[j], c_send.at[j, pl.ds(0, STEPS * CH)], c_send.at[j, pl.ds(STEPS * CH, STEPS * CH)]][way]
        dst = [c_own.at[j], c_dn.at[j], c_up.at[j]][way]
        target = (tm - 1, [sp, sp - 1, sp + 1][way])
        return pltpu.make_async_remote_copy(
            src_ref=src, dst_ref=dst, send_sem=c_ssem.at[way, j], recv_sem=c_rsem.at[way, j],
            device_id=target, device_id_type=MESH,
        )

    def send_chunk(j, carry):
        @pl.when(jnp.logical_not(is_last))
        def _():
            @pl.when(has_up)
            def _():
                p_copy(j, 1).start()

            @pl.when(has_dn)
            def _():
                p_copy(j, 2).start()

            p_copy(j, 0).start()

        rims = [[], []]
        for k in range(STEPS):
            h = HALO[k]
            b_val = zpb[STEPS - 1 - k, j + 1]
            stage_up[j, B_AT[k] * CH : (B_AT[k] + h - 1) * CH] = b_val[: (h - 1) * CH]
            stage_dn[j, B_AT[k] * CH : (B_AT[k] + h - 1) * CH] = b_val[TILE - (h - 1) * CH :]
            rims[0].append(b_val[(h - 1) * CH : h * CH].astype(F32))
            rims[1].append(b_val[TILE - h * CH : TILE - (h - 1) * CH].astype(F32))
            if k < STEPS - 1:
                a_val = zpa[STEPS - 2 - k, j + 1]
                stage_up[j, A_AT[k] * CH : (A_AT[k] + h) * CH] = a_val[: h * CH]
                stage_dn[j, A_AT[k] * CH : (A_AT[k] + h) * CH] = a_val[TILE - h * CH :]

        for stage, rim in ((stage_up, rims[0]), (stage_dn, rims[1])):
            value = rim[0]
            for k in range(1, STEPS):
                value = jnp.where(iota2((CH, 1), 0) >= 4 * k, pltpu.roll(rim[k], 4 * k, 0), value)
            stage[j, RIM_AT * CH : (RIM_AT + 1) * CH] = value.astype(BF16)

        @pl.when(has_up)
        def _():
            h_copy(j, True).start()

        @pl.when(has_dn)
        def _():
            h_copy(j, False).start()

        @pl.when(is_first)
        def _():
            @pl.when(has_up)
            def _():
                s_copy(j, 1).start()

            @pl.when(has_dn)
            def _():
                s_copy(j, 2).start()

        return carry

    def l_copy(way):
        dst = [l_own, l_dn, l_up][way]
        target = (tm - 1, [sp, sp - 1, sp + 1][way])
        return pltpu.make_async_remote_copy(
            src_ref=l_send, dst_ref=dst, send_sem=c_ssem.at[way, blocks], recv_sem=c_rsem.at[way, blocks],
            device_id=target, device_id_type=MESH,
        )

    def column(ref):
        row = ref[...].reshape(1, CH)
        eye = iota2((CH, CH), 0) == iota2((CH, CH), 1)
        value = jnp.sum(jnp.where(eye, row, 0.0), axis=1, keepdims=True)
        return jnp.concatenate([jnp.broadcast_to(value, (CH, W))] * 16, axis=0)

    def build_weights():
        biasb[...] = column(bias_ref)
        retb[...] = column(retain_ref)
        rec = [wrec_ref[t] for t in range(9)]
        inp = [win_ref[t] for t in range(9)]
        chan_of = iota2((32, CH), 0) // ROWS == iota2((32, CH), 1)
        inp_rows = [dot(onehot(chan_of[:, :3]), inp[t]).astype(BF16) for t in range(9)]
        for k in range(STEPS):
            n = 16 - 2 * k
            size = CH * (n + 2)
            at = iota2((1, 6 * size), 1)
            part = at // size
            row_in = lax.rem(at, size) // CH
            chan = lax.rem(at, CH)
            picks = []
            for m in range(3):
                picks.append(
                    (
                        onehot((iota2((CH, 6 * size), 0) == chan) & (part == 2 * m)),
                        onehot((iota2((3, 6 * size), 0) == chan) & (part == 2 * m + 1)),
                    )
                )
            base = []
            for a in range(3):
                total = jnp.zeros((CH, 6 * size), F32)
                for m in range(3):
                    t = 3 * a + 2 - m
                    total = total + dot(rec[t], picks[m][0]) + dot_tn(inp[t], picks[m][1])
                base.append(total)
            for r in range(n):
                ahead = row_in - r
                value = jnp.where(ahead == 0, base[0], jnp.where(ahead == 1, base[1], jnp.where(ahead == 2, base[2], 0.0)))
                wf[k][CH * r : CH * (r + 1)] = value.astype(BF16)
            half = n // 2 - 1
            size = CH * (half + 2)
            at = iota2((1, 3 * size), 1)
            part = at // size
            row_in = lax.rem(at, size) // CH
            chan = lax.rem(at, CH)
            picks = [onehot((iota2((CH, 3 * size), 0) == chan) & (part == b)) for b in range(3)]
            base = []
            for a in range(3):
                total = jnp.zeros((CH, 3 * size), F32)
                for b in range(3):
                    total = total + dot_tn(rec[3 * a + b], picks[b])
                base.append(total)
            for r in range(half):
                behind = r + 2 - row_in
                value = jnp.where(
                    behind == 0, base[0], jnp.where(behind == 1, base[1], jnp.where(behind == 2, base[2], 0.0))
                )
                wt[k][CH * r : CH * (r + 1)] = value.astype(BF16)
        size = 10 * CH
        at = iota2((1, 3 * size), 1)
        part = at // size
        row_in = lax.rem(at, size) // CH
        chan = lax.rem(at, CH)
        picks = [onehot((iota2((CH, 3 * size), 0) == chan) & (part == b)) for b in range(3)]
        behind = lax.rem(iota2((32, 1), 0), ROWS) + 2 - row_in
        value = jnp.zeros((32, 3 * size), F32)
        for a in range(3):
            total = jnp.zeros((32, 3 * size), F32)
            for b in range(3):
                total = total + dot(inp_rows[3 * a + b], picks[b])
            value = jnp.where(behind == a, total, value)
        wc[...] = value.astype(BF16)
        pick = onehot(iota2((12, 256), 0) == lax.rem(iota2((12, 256), 1), CH) - 4)
        base_h = dot_tn(whead_ref[...], pick)
        for r in range(16):
            wp[CH * r : CH * (r + 1)] = jnp.where(iota2((1, 256), 1) // CH == r, base_h, 0.0).astype(BF16)

    def head_gradient():
        total = jnp.zeros((12 * ROWS, TILE), F32)
        for f in range(STEPS):
            total = total + dot_nt(flat(cot_ref[f], 12).astype(BF16), flat(states_ref[f], CH).astype(BF16))
        same = lax.rem(iota2((12 * ROWS, TILE), 0), ROWS) == lax.rem(iota2((12 * ROWS, TILE), 1), ROWS)
        total = jnp.where(same, total, 0.0)
        pick_l = jnp.where(iota2((CH, 12 * ROWS), 0) == iota2((CH, 12 * ROWS), 1) // ROWS, 1.0, 0.0)
        pick_r = jnp.where(iota2((TILE, W), 0) // ROWS == iota2((TILE, W), 1), 1.0, 0.0)
        headacc[...] = dot_exact(dot_exact(pick_l, total), pick_r)

    lax.fori_loop(0, blocks, send_chunk, 0)
    build_weights()

    lane = iota2((1, W), 1)

    def shifted(now, before, steps):
        moved = pltpu.roll(now, steps, 1)
        return moved, jnp.where(lane >= steps, moved, before)

    def get_slopes(j):
        for k in range(STEPS):
            h = HALO[k]
            n = 16 - 2 * k

            def whole(slot):
                if k < STEPS - 1:
                    up_a = h_up[slot, A_AT[k] * CH : (A_AT[k] + h) * CH]
                    dn_a = h_dn[slot, A_AT[k] * CH : (A_AT[k] + h) * CH]
                else:
                    up_a, dn_a = p_up[slot], p_dn[slot]
                up_b = h_up[slot, B_AT[k] * CH : (B_AT[k] + h - 1) * CH]
                dn_b = h_dn[slot, B_AT[k] * CH : (B_AT[k] + h - 1) * CH]
                rims = []
                for ref in (h_up, h_dn):
                    rim = ref[slot, RIM_AT * CH : (RIM_AT + 1) * CH]
                    if k > 0:
                        rim = pltpu.roll(rim.astype(F32), CH - 4 * k, 0).astype(BF16)
                    rims.append(rim)
                own_a = zpa[STEPS - 2 - k, slot] if k < STEPS - 1 else zpq[slot]
                return jnp.concatenate(
                    [up_a, own_a, dn_a, rims[0], up_b, zpb[STEPS - 1 - k, slot], dn_b, rims[1]], axis=0
                )

            raw = whole(j + 1)
            size = CH * (n + 2)
            taps = []
            low = (h - 1) * CH
            for m in range(3):
                turn = skew0 + k + m
                moved = pltpu.roll(raw, turn, 1)
                x = jnp.where(lane >= turn, moved, oldx[k, m, 0 : 2 * size])
                oldx[k, m, 0 : 2 * size] = moved
                taps.append(x)
                x_a, x_b = x[:size], x[size:]
                if m == 1:
                    pushed[j, k, 0 : CH * n] = dot(wp[0 : CH * n, 0 : CH * n], x_b[CH : CH + CH * n])
                xs[j, k, m, 0 : 10 * CH] = x_a[low : low + 10 * CH]
                xs[j, k, m, 10 * CH : 20 * CH] = x_b[low : low + 10 * CH]
            preact = biasb[0 : CH * n] + dot(wf[k][...], jnp.concatenate(taps, axis=0))
            col = W * j + lane - (skew0 + k + 1)
            row = ROWS * sp + iota2((CH * n, 1), 0) // CH + (k - STEPS)
            inside = (col >= 0) & (col < cols) & (row >= 0) & (row < ROWS * space_count)
            t = jnp.tanh(preact)
            slopes[j, k, 0 : CH * n] = jnp.where(inside, 1.0 - t * t, 0.0)

    def await_inputs(j):
        @pl.when(has_up)
        def _():
            h_copy(j, False).wait_recv()

        @pl.when(has_dn)
        def _():
            h_copy(j, True).wait_recv()

        @pl.when(jnp.logical_not(is_first))
        def _():
            p_copy(j, 0).wait_recv()

        @pl.when(has_dn)
        def _():
            p_copy(j, 1).wait_recv()

        @pl.when(has_up)
        def _():
            p_copy(j, 2).wait_recv()

    def prepare(j, carry):
        @pl.when(j < blocks)
        def _():
            await_inputs(j)

        get_slopes(j)
        return carry

    def post(j, carry):
        for k in range(STEPS):
            zero = jnp.zeros((CH, W), BF16)
            d = tiles(dkeep[j, k], ROWS)
            g = tiles(gkeep[j, k], ROWS)
            right = jnp.concatenate(
                [
                    jnp.concatenate(d + [zero, zero], axis=1),
                    jnp.concatenate([zero] + d + [zero], axis=1),
                    jnp.concatenate([zero, zero] + d, axis=1),
                    jnp.concatenate([zero] + g + [zero], axis=1),
                ],
                axis=0,
            )
            rows_of = []
            for half in range(2):
                for m in range(3):
                    x = xs[j, k, m, half * 10 * CH : (half + 1) * 10 * CH]
                    rows_of.append(jnp.concatenate(tiles(x, 10), axis=1))
            left = jnp.concatenate(rows_of, axis=0)
            gram[...] += dot_nt(left, right)
        return carry

    group = 2 * CH
    spread_w = W // 4

    def unpack(ref, dst, which):
        value = ref[...]
        for at, q in enumerate(which):
            part = value if q == 0 else pltpu.roll(value, W - spread_w * q, 1)
            dst[blocks, group * at : group * (at + 1)] = part

    def chain(j):
        carried = jnp.concatenate([c_up[j], c_own[j], c_dn[j]], axis=0).astype(F32)
        for k in range(STEPS):
            n = 16 - 2 * k
            size = CH * n
            g = carried + pushed[j, k, 0:size]
            d = (g * slopes[j, k, 0:size]).astype(BF16)
            r1_, d1 = shifted(d, d1prev[k, 0:size], 1)
            r2_, d2 = shifted(d, d2prev[k, 0:size], 2)
            d1prev[k, 0:size] = r1_
            d2prev[k, 0:size] = r2_
            inner = g[CH : size - CH]
            rg, gs = shifted(inner, gprev[k, 0 : size - 2 * CH], 1)
            gprev[k, 0 : size - 2 * CH] = rg
            taps = [d, d1, d2]
            half = CH * (n // 2 - 1)
            conv = jnp.concatenate(
                [
                    dot(wt[k][...], jnp.concatenate([t[at : at + half + 2 * CH] for t in taps], axis=0))
                    for at in (0, half)
                ],
                axis=0,
            )
            carried = retb[0 : size - 2 * CH] * gs + conv
            at = (STEPS - k) * CH
            gfs[j, k] = dot(wc[...], jnp.concatenate([t[at - CH : at + 9 * CH] for t in taps], axis=0))
            dkeep[j, k] = d[at : at + TILE]
            gkeep[j, k] = g[at : at + TILE].astype(BF16)
        c_send[j] = carried.astype(BF16)
        bnd[j] = carried

    def await_carried(hop):
        hop(0).wait_recv()

        @pl.when(has_dn)
        def _():
            hop(1).wait_recv()

        @pl.when(has_up)
        def _():
            hop(2).wait_recv()

    def start_carried(hop):
        @pl.when(has_up)
        def _():
            hop(1).start()

        @pl.when(has_dn)
        def _():
            hop(2).start()

        hop(0).start()

    def step(j, carry):
        @pl.when(is_last)
        def _():
            prepare(j, 0)

        @pl.when(jnp.logical_not(is_last) & (j < blocks))
        def _():
            await_carried(functools.partial(c_copy, j))

        @pl.when(jnp.logical_not(is_last) & (j == blocks))
        def _():
            await_carried(l_copy)
            unpack(l_own, c_own, (0, 1, 2, 3))

            @pl.when(has_up)
            def _():
                unpack(l_up, c_up, (2, 3))

            @pl.when(has_dn)
            def _():
                unpack(l_dn, c_dn, (0, 1))

        chain(j)

        @pl.when(jnp.logical_not(is_first) & (j < blocks))
        def _():
            start_carried(functools.partial(c_copy, j))

        @pl.when(jnp.logical_not(is_first) & (j == blocks))
        def _():
            packed = c_send[blocks, 0:group]
            for q in range(1, 4):
                turned = pltpu.roll(c_send[blocks, group * q : group * (q + 1)], spread_w * q, 1)
                packed = jnp.where(lane >= spread_w * q, turned, packed)
            l_send[...] = packed
            start_carried(l_copy)

        @pl.when(jnp.logical_not(is_early))
        def _():
            post(j, 0)

        return carry

    @pl.when(jnp.logical_not(is_early))
    def _():
        head_gradient()

    @pl.when(jnp.logical_not(is_last))
    def _():
        lax.fori_loop(0, chunks, prepare, 0)

    lax.fori_loop(0, chunks, step, 0)

    @pl.when(is_early)
    def _():
        lax.fori_loop(0, chunks, post, 0)
        head_gradient()

    rpart[0:16, 0:64] = gram[0:16]
    rpart[0:16, 64:128] = gram[16:32]
    rpart[16:32, 0:64] = gram[32:48]
    rpart[16:32, 64:80] = headacc[:, 0:CH]
    rpart[16:24, 80:128] = gram[80:88, 0:48]
    rpart[24:32, 80:128] = jnp.zeros((8, 48), F32)
    rpart[32:40, 0:64] = gram[48:56]
    rpart[32:40, 64:128] = gram[64:72]

    def first_copy(p):
        return pltpu.make_async_remote_copy(
            src_ref=rpart, dst_ref=rs.at[p], send_sem=s1.at[0], recv_sem=r1.at[p],
            device_id=(0, sp), device_id_type=MESH,
        )

    @pl.when(jnp.logical_not(is_first))
    def _():
        first_copy(tm).start()

    out_shift = skew0 + STEPS + 1

    moves = [
        pltpu.make_async_copy(gf_ref, gf_out, out_sem.at[0]),
        pltpu.make_async_copy(bound_ref, bound_out, out_sem.at[1]),
    ]

    def put_outputs():
        for c in range(blocks):
            def unskew(now, after, shift):
                return jnp.where(lane < W - shift, pltpu.roll(now, W - shift, 1), pltpu.roll(after, W - shift, 1))

            value = unskew(bnd[c], bnd[c + 1], out_shift)
            for r in range(ROWS):
                bound_ref[0, :, r, W * c : W * (c + 1)] = value[CH * r : CH * (r + 1)]
            for k in range(STEPS):
                value = unskew(gfs[c, k, 0:24], gfs[c + 1, k, 0:24], skew0 + k + 2)
                gf_ref[STEPS - 1 - k, :, :, W * c : W * (c + 1)] = value.reshape(3, ROWS, W).astype(BF16)
        for move in moves:
            move.start()

    def second_copy(q):
        s = lax.rem(sp + q, space_count)
        return pltpu.make_async_remote_copy(
            src_ref=ag.at[sp], dst_ref=ag.at[sp], send_sem=s2.at[q], recv_sem=r2.at[q],
            device_id=(0, s), device_id_type=MESH,
        )

    def third_copy(t):
        return pltpu.make_async_remote_copy(
            src_ref=red, dst_ref=red, send_sem=s3.at[t], recv_sem=r3.at[0],
            device_id=(t, sp), device_id_type=MESH,
        )

    @pl.when(is_first)
    def _():
        part = rpart[...]
        for t in range(1, tm_count):
            first_copy(t).wait_recv()
            part = part + rs[t]
        ag[sp] = part
        for q in range(1, space_count):
            second_copy(q).start()
        put_outputs()
        for q in range(1, space_count):
            second_copy(q).wait_recv()
        part = ag[0]
        for q in range(1, space_count):
            part = part + ag[q]
        red[...] = part
        for t in range(1, tm_count):
            third_copy(t).start()

    @pl.when(jnp.logical_not(is_first))
    def _():
        put_outputs()
        third_copy(1).wait_recv()

    sums_ref[...] = red[...]
    for move in moves:
        move.wait()

    @pl.when(is_first)
    def _():
        for q in range(1, space_count):
            second_copy(q).wait_send()
        for t in range(1, tm_count):
            third_copy(t).wait_send()

    @pl.when(jnp.logical_not(is_first))
    def _():
        first_copy(tm).wait_send()

    def drain(j, carry):
        @pl.when(has_up)
        def _():
            h_copy(j, True).wait_send()

        @pl.when(has_dn)
        def _():
            h_copy(j, False).wait_send()

        @pl.when(jnp.logical_not(is_last))
        def _():
            p_copy(j, 0).wait_send()

            @pl.when(has_up)
            def _():
                p_copy(j, 1).wait_send()

            @pl.when(has_dn)
            def _():
                p_copy(j, 2).wait_send()

        @pl.when(is_first)
        def _():
            @pl.when(has_up)
            def _():
                s_copy(j, 1).wait_send()

            @pl.when(has_dn)
            def _():
                s_copy(j, 2).wait_send()

        return carry

    lax.fori_loop(0, blocks, drain, 0)

    @pl.when(jnp.logical_not(is_first))
    def _():
        def drain_carried(way):
            def body(j, carry):
                c_copy(j, way).wait_send()
                return carry

            lax.fori_loop(0, blocks, body, 0)
            l_copy(way).wait_send()

        drain_carried(0)

        @pl.when(has_up)
        def _():
            drain_carried(1)

        @pl.when(has_dn)
        def _():
            drain_carried(2)


def finish(sums_ref, gf_in, bound_in, rec_ref, in_ref, bias_ref, keep_ref, head_ref, gf_ref, bound_ref, sem):
    moves = [pltpu.make_async_copy(gf_in, gf_ref, sem.at[0]), pltpu.make_async_copy(bound_in, bound_ref, sem.at[1])]
    for move in moves:
        move.start()
    sums = sums_ref[...]
    turned = jnp.concatenate([sums, jnp.zeros((W - 40, W), F32)], axis=0).T
    for m in range(3):
        b = 2 - m
        lane_rec, row_rec = [(0, 0), (64, 0), (0, 16)][m]
        lane_in, row_in = [(0, 32), (64, 32), (80, 16)][m]
        for a in range(3):
            rec_ref[3 * a + b] = turned[lane_rec + CH * a : lane_rec + CH * (a + 1), row_rec : row_rec + CH]
            in_ref[3 * a + b] = sums[row_in : row_in + 3, lane_in + CH * a : lane_in + CH * (a + 1)]
    bias_ref[...] = sums[35:36, 80:96].reshape(CH)
    eye = iota2((CH, CH), 0) == iota2((CH, CH), 1)
    keep_ref[...] = jnp.sum(jnp.where(eye, sums[0:16, 112:128], 0.0), axis=0, keepdims=True).reshape(CH)
    head_ref[...] = sums[16:28, 64:80]
    for move in moves:
        move.wait()


def on_device(tm_count, space_count, frames, states, start_state, cotangent, w_rec, w_in, bias_vec, retain, w_head):
    cols = states.shape[3]
    chunks = -(-(cols + STEPS * tm_count + 1) // W)
    blocks = cols // W
    vmem = pl.BlockSpec(memory_space=pltpu.VMEM)
    anywhere = pl.BlockSpec(memory_space=pl.ANY)
    dma = pltpu.SemaphoreType.DMA
    scratch = [
        pltpu.VMEM(frames.shape, BF16),
        pltpu.VMEM((1, CH, ROWS, cols), F32),
        pltpu.VMEM(frames.shape, BF16),
        pltpu.VMEM(states.shape, BF16),
        pltpu.VMEM(start_state.shape, BF16),
        pltpu.VMEM(cotangent.shape, BF16),
        pltpu.VMEM((STEPS, chunks + 1, TILE, W), BF16),
        pltpu.VMEM((STEPS, chunks + 1, TILE, W), BF16),
        pltpu.VMEM((chunks + 1, TILE, W), BF16),
        pltpu.VMEM((blocks, MSG, W), BF16),
        pltpu.VMEM((blocks, MSG, W), BF16),
        pltpu.VMEM((chunks + 1, MSG, W), BF16),
        pltpu.VMEM((chunks + 1, MSG, W), BF16),
        pltpu.VMEM((chunks + 1, 2 * CH, W), BF16),
        pltpu.VMEM((chunks + 1, 2 * CH, W), BF16),
        pltpu.VMEM((STEPS, 3, 36 * CH, W), BF16),
        pltpu.VMEM((chunks, STEPS, 256, W), F32),
        pltpu.VMEM((chunks, STEPS, 256, W), F32),
        pltpu.VMEM((chunks, STEPS, 3, 20 * CH, W), BF16),
        pltpu.VMEM((chunks, STEPS, TILE, W), BF16),
        pltpu.VMEM((chunks, STEPS, TILE, W), BF16),
        pltpu.VMEM((chunks, STEPS, 32, W), F32),
        pltpu.VMEM((chunks, TILE, W), F32),
        pltpu.VMEM((chunks, TILE, W), BF16),
        pltpu.VMEM((chunks, STEPS * CH, W), BF16),
        pltpu.VMEM((chunks, STEPS * CH, W), BF16),
        pltpu.VMEM((chunks, TILE, W), BF16),
        *[pltpu.VMEM((2 * CH, W), BF16)] * 4,
        *[pltpu.VMEM((CH * n, 6 * CH * (n + 2)), BF16) for n in (16, 14, 12, 10)],
        pltpu.VMEM((256, 256), BF16),
        *[pltpu.VMEM((CH * h, 3 * CH * (h + 2)), BF16) for h in (7, 6, 5, 4)],
        pltpu.VMEM((32, 30 * CH), BF16),
        pltpu.VMEM((STEPS, 256, W), BF16),
        pltpu.VMEM((STEPS, 256, W), BF16),
        pltpu.VMEM((STEPS, 256, W), F32),
        pltpu.VMEM((256, W), F32),
        pltpu.VMEM((256, W), F32),
        pltpu.VMEM((96, 64), F32),
        pltpu.VMEM((CH, W), F32),
        pltpu.VMEM((40, W), F32),
        pltpu.VMEM((tm_count, 40, W), F32),
        pltpu.VMEM((space_count, 40, W), F32),
        pltpu.VMEM((40, W), F32),
        dma((2, chunks)), dma((2, chunks)),
        dma((3, chunks)), dma((3, chunks)), dma((3, chunks)),
        dma((3, chunks)), dma((3, chunks)),
        dma((tm_count,)), dma((tm_count,)),
        dma((space_count,)), dma((space_count,)),
        dma((tm_count,)), dma((tm_count,)), dma((4,)), dma((2,)),
    ]
    grad_frames, bound, sums = pl.pallas_call(
        functools.partial(kernel, tm_count, space_count, cols, chunks),
        out_shape=[
            jax.ShapeDtypeStruct((STEPS, 3, ROWS, cols), BF16),
            jax.ShapeDtypeStruct((1, CH, ROWS, cols), F32),
            jax.ShapeDtypeStruct((40, W), F32),
        ],
        in_specs=[anywhere] * 4 + [vmem] * 5,
        out_specs=[anywhere, anywhere, vmem],
        scratch_shapes=scratch,
        compiler_params=pltpu.CompilerParams(
            collective_id=0, has_side_effects=True, vmem_limit_bytes=56 * 1024 * 1024
        ),
    )(
        frames, states, start_state, cotangent, w_rec.transpose(1, 0, 2), w_in.transpose(1, 2, 0), bias_vec, retain, w_head
    )
    out_shape = [
        jax.ShapeDtypeStruct((9, CH, CH), F32),
        jax.ShapeDtypeStruct((9, 3, CH), F32),
        jax.ShapeDtypeStruct((CH,), F32),
        jax.ShapeDtypeStruct((CH,), F32),
        jax.ShapeDtypeStruct((12, CH), F32),
        jax.ShapeDtypeStruct(grad_frames.shape, BF16),
        jax.ShapeDtypeStruct(bound.shape, F32),
    ]
    rec, inp, *rest = pl.pallas_call(
        finish,
        out_shape=out_shape,
        in_specs=[vmem, vmem, vmem],
        out_specs=[vmem] * 5 + [anywhere] * 2,
        scratch_shapes=[dma((2,))],
    )(sums, grad_frames, bound)
    return (rec.transpose(1, 0, 2), inp.transpose(2, 0, 1), *rest)


def solution(mesh):
    banded = P("tm", None, "space", None)
    in_specs = (banded, banded, P(None, "space", None), banded, P(), P(), P(), P(), P())
    out_specs = (P(), P(), P(), P(), P(), banded, banded)
    return jax.shard_map(
        functools.partial(on_device, mesh.shape["tm"], mesh.shape["space"]),
        mesh=mesh, in_specs=in_specs, out_specs=out_specs, check_vma=False,
    )
```
